32 devices in a mesh: groups: 2 (over x), sub: 16 (over z, y, core).
Axes of the slice: x: 2, y: 2, z: 4, core: 2. Of those that a mesh axis runs over, the one named last changes fastest.
Arguments:
- loads: float32 [8192, 1024], P(('groups', 'sub')), parts along dimension 0, may hold values from -250 to 250
- row_ids: int32 [8192], P(('groups', 'sub')), parts along dimension 0, may hold values from 0 to 4095, as said below
- densities: float32 [8192, 12], P(('groups', 'sub')), parts along dimension 0, may hold values from 0 to 1
- block_cols: int32 [8192, 12], P(('groups', 'sub')), parts along dimension 0, may hold values from 0 to 4095, as said below
- block_types: int32 [8192, 12], P(('groups', 'sub')), parts along dimension 0, may hold values from 0 to 2
- ref_blocks: float32 [3, 64, 64], replicated, may hold values from -1 to 1.5, as said below
Outputs:
- solution: float32 [8192, 1024], P(('groups', 'sub')), parts along dimension 0
- residual: float32 [8192, 1024], P(('groups', 'sub')), parts along dimension 0
The draws below stay inside these ranges and needn't reach their ends.
There are 2 independent parts, one for each index of `groups`. The reference program is written for one: setup_inputs(seed, part) draws one part's arguments, and reference() takes and returns one part's arrays. A program takes and returns all parts, laid end to end along the dimension named above; an argument that names none is the same for every part. Nothing has to cross between parts.
Inputs may be any that keep to these rules, and one draw needn't show every extreme that they name: `row_ids`: A permutation of the mesh's block rows. Device d's rows are 256 * d to 256 * d + 255; its partner is device (d + 8) mod 16. The slots of device d hold rows of devices d - 1, d, d + 1 and of its partner; at most 64 rows of one device belong to each other device; across some boundary exactly 64 go each way, and some pair of partners swaps exactly 64. `block_cols`: every column lies within 32 rows of its block row, and some lies exactly 32 away. Couplings are symmetric: if a slot of row g points to row h with a density and a type, a slot of row h points to g with the same. A slot of density zero may point to its own row. `ref_blocks`: each block is symmetric and positive definite.
All inputs are finite; a program needn't handle non-finite values.
Results may differ from the reference program's by a relative error of at most 0.0003.
Values sent between devices are 32-bit elements; how exact they have to be, the bound alone decides.
No kernel may reach another device: no remote copies, remote signals or barrier semaphores. Data moves between devices by JAX's collectives and lax.ppermute only.
A program may use at most 128 MiB of HBM per device.

```python
import jax
import jax.numpy as jnp
from jax import lax

DOF = 64
CASES = 16
BLK_DEV = 256
HALO = 32
PAIRS = 6
TYPES = 3
ITERS = 3
NNZ = 12
CAP = 64
ROWS = 4096
N_SUB = 16


def mesh_layout(key):
    key_offsets, key_types, key_counts, key_chosen, key_shuffle, key_pairs, key_pick = jax.random.split(key, 7)
    ordering = jax.random.permutation(key_offsets, HALO - 1) + 1
    offsets = jnp.concatenate([ordering[:PAIRS - 1], jnp.array([HALO])]).astype(jnp.int32)
    types_upper = jax.random.randint(key_types, (ROWS, PAIRS), 0, TYPES).astype(jnp.int32)
    counts = jax.random.randint(key_counts, (N_SUB - 1,), 1, CAP + 1)
    chosen = jax.random.randint(key_chosen, (), 0, N_SUB - 1)
    counts = jnp.where(jnp.arange(N_SUB - 1) == chosen, CAP, counts).astype(jnp.int32)
    half_count = N_SUB // 2
    swaps = jax.random.randint(key_pairs, (half_count,), 1, CAP + 1)
    picked = jax.random.randint(key_pick, (), 0, half_count)
    swaps = jnp.where(jnp.arange(half_count) == picked, CAP, swaps).astype(jnp.int32)
    single_zero = jnp.zeros((1,), jnp.int32)
    before = jnp.concatenate([single_zero, counts])
    after = jnp.concatenate([counts, single_zero])
    rows_all = jnp.arange(ROWS, dtype=jnp.int32)
    device_of = rows_all // BLK_DEV
    position = rows_all % BLK_DEV
    below = before[device_of]
    above = after[device_of]
    partner = (device_of + half_count) % N_SUB
    swapped = swaps[device_of % half_count]
    mirror_live = (position >= CAP) & (position < CAP + swapped)
    slot_rows = jnp.where(position < below, (device_of - 1) * BLK_DEV + BLK_DEV - below + position, jnp.where(position >= BLK_DEV - above, (device_of + 1) * BLK_DEV + position - (BLK_DEV - above), jnp.where(mirror_live, partner * BLK_DEV + position, rows_all)))
    device_keys = jax.random.split(key_shuffle, N_SUB)
    shuffles = jax.vmap(lambda single: jax.random.permutation(single, BLK_DEV))(device_keys).astype(jnp.int32)
    slot_rows = jnp.take_along_axis(slot_rows.reshape(N_SUB, BLK_DEV), shuffles, axis=1).reshape(ROWS)
    upper_rows = rows_all[:, None] + offsets[None, :]
    lower_rows = rows_all[:, None] - offsets[None, :]
    upper_live = upper_rows < ROWS
    lower_live = lower_rows >= 0
    lower_clip = jnp.maximum(lower_rows, 0)
    return (slot_rows, rows_all, upper_rows, lower_rows, upper_live, lower_live, lower_clip, types_upper)


def draw_row_ids(key, part):
    layout = mesh_layout(key)
    return layout[0]


def draw_block_cols(key, part):
    slot_rows, rows_all, upper_rows, lower_rows, upper_live, lower_live, lower_clip, types_upper = mesh_layout(key)
    itself = rows_all[:, None]
    columns = jnp.concatenate([jnp.where(upper_live, upper_rows, itself), jnp.where(lower_live, lower_rows, itself)], axis=1)
    return columns[slot_rows].astype(jnp.int32)


def draw_block_types(key, part):
    slot_rows, rows_all, upper_rows, lower_rows, upper_live, lower_live, lower_clip, types_upper = mesh_layout(key)
    types_lower = jnp.take_along_axis(types_upper, lower_clip, axis=0)
    kinds = jnp.concatenate([types_upper, types_lower], axis=1)
    return kinds[slot_rows].astype(jnp.int32)


def draw_densities(key, part):
    slot_rows, rows_all, upper_rows, lower_rows, upper_live, lower_live, lower_clip, types_upper = mesh_layout(key)
    key = jax.random.fold_in(key, 11)
    key_design, key_void = jax.random.split(key)
    design = jax.random.uniform(key_design, (ROWS, PAIRS), jnp.float32)
    void_flags = jax.random.randint(key_void, (ROWS // 8,), 0, 2)
    void_rows = void_flags[rows_all // 8]
    design = design * jnp.where(void_rows == 1, 0.3, 1.0)[:, None]
    stiffness = 0.001 + 0.999 * design * design * design
    upper_part = stiffness * upper_live.astype(jnp.float32)
    lower_part = jnp.take_along_axis(stiffness, lower_clip, axis=0) * lower_live.astype(jnp.float32)
    values = jnp.concatenate([upper_part, lower_part], axis=1)
    return values[slot_rows]


def draw_loads(key, part):
    layout = mesh_layout(key)
    slot_rows = layout[0]
    key = jax.random.fold_in(key, 12)
    key_values, key_rows, key_cases = jax.random.split(key, 3)
    rows_all = jnp.arange(ROWS, dtype=jnp.float32)
    row_scale = 0.3 * jnp.exp(jnp.log(10.0) * jax.random.uniform(key_rows, (ROWS,), jnp.float32))
    row_scale = row_scale * jnp.exp(jnp.log(3.0) * rows_all / ROWS)
    case_scale = 0.5 * jnp.exp(jnp.log(10.0) * jax.random.uniform(key_cases, (CASES,), jnp.float32))
    column_scale = jnp.tile(case_scale, DOF)
    values = jnp.clip(jax.random.normal(key_values, (ROWS, DOF * CASES), jnp.float32), -5.0, 5.0)
    field_geo = values * row_scale[:, None] * column_scale[None, :]
    return field_geo[slot_rows]


def draw_ref_blocks(key, part):
    key = jax.random.fold_in(key, 13)
    key_off, key_diag = jax.random.split(key)
    raw = jax.random.uniform(key_off, (TYPES, DOF, DOF), jnp.float32, -1.0, 1.0)
    symmetric = (raw + jnp.swapaxes(raw, 1, 2)) * (0.5 / DOF)
    diagonal = 1.0 + jax.random.uniform(key_diag, (TYPES, DOF), jnp.float32, 0.0, 0.25)
    identity = jnp.eye(DOF, dtype=jnp.float32)
    return symmetric * (1.0 - identity)[None] + diagonal[:, :, None] * identity[None]


def setup_inputs(seed: int = 0, part: int = 0) -> dict:
    splits = jax.random.split(jax.random.key(seed), 7)
    part_keys = jax.random.split(jax.random.fold_in(splits[6], part), 7)
    loads = draw_loads(jax.random.fold_in(jax.random.fold_in(splits[6], part), 71), part)
    row_ids = draw_row_ids(jax.random.fold_in(jax.random.fold_in(splits[6], part), 71), part)
    densities = draw_densities(jax.random.fold_in(jax.random.fold_in(splits[6], part), 71), part)
    block_cols = draw_block_cols(jax.random.fold_in(jax.random.fold_in(splits[6], part), 71), part)
    block_types = draw_block_types(jax.random.fold_in(jax.random.fold_in(splits[6], part), 71), part)
    ref_blocks = draw_ref_blocks(jax.random.fold_in(splits[6], 71), part)
    return {"loads": loads, "row_ids": row_ids, "densities": densities, "block_cols": block_cols, "block_types": block_types, "ref_blocks": ref_blocks}


mass_shift = 0.5

def gram_solve(matrix, target):
    factor = jnp.linalg.cholesky(matrix)
    return jax.scipy.linalg.cho_solve((factor, True), target)

def cross_gram(left, right):
    left_flat = left.reshape(-1, CASES)
    right_flat = right.reshape(-1, CASES)
    return jnp.dot(left_flat.T.astype(jnp.float32), right_flat.astype(jnp.float32), precision=lax.Precision.HIGHEST, preferred_element_type=jnp.float32)

def times_small(vector_in, matrix):
    flat = vector_in.reshape(-1, CASES)
    return jnp.dot(flat.astype(jnp.float32), matrix.astype(jnp.float32), precision=lax.Precision.HIGHEST, preferred_element_type=jnp.float32).reshape(vector_in.shape)

def reference(loads, row_ids, densities, block_cols, block_types, ref_blocks):

    def place(source):
        return jnp.zeros_like(source).at[row_ids].set(source)
    loads_geo = place(loads)
    density_geo = place(densities)
    column_geo = place(block_cols)
    type_geo = place(block_types)
    kinds = jnp.arange(TYPES, dtype=jnp.int32)
    weights = density_geo[:, :, None] * (type_geo[:, :, None] == kinds[None, None, :]).astype(jnp.float32)

    def operate(vector_in):
        bucket = jnp.zeros((TYPES, ROWS, DOF * CASES), jnp.float32)
        for column in range(NNZ):
            difference = vector_in - vector_in[column_geo[:, column]]
            bucket = bucket + weights[:, column, :].T[:, :, None] * difference[None]
        blocks = bucket.reshape(TYPES, ROWS, DOF, CASES)
        applied = jnp.einsum('tij,tgjc->gic', ref_blocks, blocks, precision=lax.Precision.HIGHEST)
        return mass_shift * vector_in + applied.reshape(ROWS, DOF * CASES)
    solution = jnp.zeros_like(loads_geo)
    residual = loads_geo
    direction = loads_geo
    residual_gram = cross_gram(residual, residual)
    for step in range(ITERS):
        applied = operate(direction)
        curvature_gram = cross_gram(direction, applied)
        step_size = gram_solve(curvature_gram, residual_gram)
        solution = solution + times_small(direction, step_size)
        residual = residual - times_small(applied, step_size)
        if step + 1 < ITERS:
            next_gram = cross_gram(residual, residual)
            update_mix = gram_solve(residual_gram, next_gram)
            direction = residual + times_small(direction, update_mix)
            residual_gram = next_gram
    return (solution, residual)
```

```python
import functools

import jax
import jax.numpy as jnp
from jax import lax
from jax.experimental import pallas as pl
from jax.experimental.pallas import tpu as pltpu
from jax.sharding import PartitionSpec as P

HALO = 32
TYPES = 3
ITERS = 3
MASS_SHIFT = 0.5
META = 128
TILE = 256

F32 = jnp.float32
BF16 = jnp.bfloat16
VMEM = pl.BlockSpec(memory_space=pltpu.VMEM)
SMEM = pl.BlockSpec(memory_space=pltpu.SMEM)
PARAMS = pltpu.CompilerParams(vmem_limit_bytes=40 * 1024 * 1024)


def dot(left, right):
    return jnp.dot(left, right, preferred_element_type=F32)


def dot_nt(left, right):
    return lax.dot_general(left, right, (((1,), (1,)), ((), ())), preferred_element_type=F32)


def dot_tn(left, right):
    return lax.dot_general(left, right, (((0,), (0,)), ((), ())), preferred_element_type=F32)


def halves(value):
    high = value.astype(BF16)
    return high, (value - high.astype(F32)).astype(BF16)


def iota(shape, axis):
    return lax.broadcasted_iota(jnp.int32, shape, axis)


def one_hot(condition):
    return jnp.where(condition, 1.0, 0.0).astype(BF16)


def basis_shift(blocks, slots):
    dof = blocks.shape[1]
    same = iota((dof, dof), 0) == iota((dof, dof), 1)
    total = sum(jnp.where(same, blocks[t], 0.0) for t in range(TYPES))
    mean = jnp.sum(jnp.sum(total, axis=1, keepdims=True), axis=0, keepdims=True) / (TYPES * dof)
    return MASS_SHIFT + 0.2 * slots * mean


def pack_kernel(devices, pos_ref, loads_ref, rows_ref, dens_ref, cols_ref, types_ref,
                left_ref, right_ref, partner_ref, meta_ref):
    rows, width = loads_ref.shape
    slots = dens_ref.shape[0]
    cap = rows // 4
    pos = pos_ref[0, 0]
    ids = rows_ref[...]
    owner = lax.div(ids, jnp.int32(rows))
    local = (ids - owner * rows + 1).astype(F32)
    kept = owner == pos
    opposite = lax.rem(pos + devices // 2, jnp.int32(devices))
    goes = [owner == pos - 1, owner == pos + 1]
    goes.append((owner == opposite) & ~goes[0] & ~goes[1])
    flags = jnp.concatenate(
        [jnp.where(g, 1.0, 0.0) for g in goes] + [jnp.zeros((5, rows), F32)], axis=0
    )
    before = one_hot(iota((rows, rows), 0) < iota((rows, rows), 1))
    rank = dot(flags.astype(BF16), before).astype(jnp.int32)
    target = jnp.full((1, rows), -1, jnp.int32)
    for side in range(3):
        target = jnp.where(goes[side], rank[side:side + 1] + side * cap, target)
    pick = one_hot(iota((3 * cap, rows), 0) == target)

    density = dens_ref[...]
    kinds = types_ref[...]
    for kind in range(TYPES):
        meta_ref[kind * slots:(kind + 1) * slots, :] = jnp.where(kinds == kind, density, 0.0)
    meta_ref[3 * slots:4 * slots, :] = (cols_ref[...] - ids).astype(F32)
    meta_ref[4 * slots:, :] = jnp.zeros((META - 4 * slots, rows), F32)
    meta_ref[4 * slots:4 * slots + 1, :] = local
    meta_ref[4 * slots + 1:4 * slots + 2, :] = jnp.where(kept, local, 0.0)

    twice = jnp.concatenate([pick, pick], axis=1)
    body = dot(twice, jnp.concatenate(halves(loads_ref[...]), axis=0))
    meta = dot_nt(twice, jnp.concatenate(halves(meta_ref[...]), axis=1))
    for side, out_ref in enumerate((left_ref, right_ref, partner_ref)):
        out_ref[:, :width] = body[side * cap:(side + 1) * cap]
        out_ref[:, width:] = meta[side * cap:(side + 1) * cap]


def lane_order(width, dof, transpose):
    cases = width // dof
    source = iota((width, width), 1 if transpose else 0)
    target = iota((width, width), 0 if transpose else 1)
    return one_hot(target == (source % cases) * dof + source // cases)


def arrange_kernel(dof, slots, loads_ref, meta_ref, left_ref, right_ref, partner_ref,
                   geo_ref, field_ref, geo_meta_ref, head_ref, tail_ref):
    rows, width = loads_ref.shape
    edge = head_ref.shape[0]
    arrived = jnp.concatenate([left_ref[...], right_ref[...], partner_ref[...]], axis=0)
    count = arrived.shape[0]
    arrived_meta = arrived[:, width:]
    unit = one_hot(iota((8, META), 1) == 4 * slots)
    tags = dot_nt(unit, arrived_meta.astype(BF16))[0:1]
    place = iota((rows, rows), 0) + 1
    own = one_hot(place == meta_ref[4 * slots + 1:4 * slots + 2, :].astype(jnp.int32))
    other = one_hot(iota((rows, count), 0) + 1 == tags.astype(jnp.int32))

    parts = []
    for part_own, part_other in zip(halves(loads_ref[...]), halves(arrived[:, :width])):
        parts.append((dot(own, part_own) + dot(other, part_other)).astype(BF16))
    both = jnp.concatenate(parts, axis=0)
    geo_ref[...] = both
    meta = dot_nt(
        jnp.concatenate([own, own], axis=1), jnp.concatenate(halves(meta_ref[...]), axis=1)
    )
    for part in halves(arrived_meta):
        meta += dot(other, part)
    geo_meta_ref[...] = meta

    moved = dot(both, lane_order(width, dof, False))
    field = moved[:rows] + moved[rows:]
    field_ref[...] = field
    head_ref[:, :width] = field[:edge]
    head_ref[:, width:] = meta[:edge]
    tail_ref[:, :width] = field[rows - edge:]
    tail_ref[:, width:] = meta[rows - edge:]


def krylov_kernel(slots, before_ref, field_ref, meta_ref, after_ref, blocks_ref, geo_ref,
                  basis_ref, moments_ref, v_refs, ext_meta, stencil, mixer):
    rows, width = field_ref.shape
    dof = blocks_ref.shape[1]
    cases = width // dof
    tiles = width // TILE
    edge = before_ref.shape[0]
    span = rows + 2 * edge
    half = (span - 2 * HALO) // 2
    window = half + 2 * HALO
    chunks = half // HALO

    shift = basis_shift(blocks_ref[...], slots)

    fold = one_hot(iota((TILE, dof), 0) % dof == iota((TILE, dof), 1))
    unfold = one_hot(iota((dof, TILE), 1) % dof == iota((dof, TILE), 0))
    same_case = iota((TILE, TILE), 0) // dof == iota((TILE, TILE), 1) // dof
    for kind in range(TYPES):
        for copies, part in zip(((0, 2), (1,)), halves(blocks_ref[kind])):
            spread = dot(dot_nt(fold, part).astype(BF16), unfold)
            spread = jnp.where(same_case, spread, 0.0).astype(BF16)
            for copy in copies:
                start = (copy * TYPES + kind) * TILE
                mixer[start:start + TILE, :] = spread

    ext_meta[:edge, :] = before_ref[:, width:]
    ext_meta[edge:edge + rows, :] = meta_ref[...]
    ext_meta[edge + rows:, :] = after_ref[:, width:]

    def build(chunk, carry):
        part = lax.div(chunk, jnp.int32(chunks))
        first = pl.multiple_of(lax.rem(chunk, jnp.int32(chunks)) * HALO, HALO)
        meta = ext_meta[pl.ds(pl.multiple_of(HALO + chunk * HALO, HALO), HALO), :]
        lane = iota((HALO, META), 1)
        spot = iota((HALO, window), 1)
        centre = iota((HALO, 1), 0) + (first + HALO)
        sums = [jnp.zeros((HALO, window), F32) for _ in range(TYPES)]
        for slot in range(slots):
            column = centre + meta[:, 3 * slots + slot:3 * slots + slot + 1].astype(jnp.int32)
            hit = spot == column
            for kind in range(TYPES):
                weight = meta[:, kind * slots + slot:kind * slots + slot + 1]
                sums[kind] += jnp.where(hit, weight, 0.0)
        for kind in range(TYPES):
            inside = (lane >= kind * slots) & (lane < (kind + 1) * slots)
            total = jnp.sum(jnp.where(inside, meta, 0.0), axis=1, keepdims=True)
            high, low = halves(jnp.where(spot == centre, total, 0.0) - sums[kind])
            stencil[part, kind, pl.ds(first, HALO), 0:window] = high
            stencil[part, kind, pl.ds(first, HALO), window:2 * window] = high
            stencil[part, kind, pl.ds(first, HALO), 2 * window:3 * window] = low
        return carry

    lax.fori_loop(0, 2 * chunks, build, 0)

    for tile in range(tiles):
        lanes = slice(tile * TILE, (tile + 1) * TILE)
        for start, source in ((0, before_ref), (edge, field_ref), (edge + rows, after_ref)):
            high, low = halves(source[:, lanes])
            v_refs[0, 0, tile, start:start + high.shape[0], :] = high
            v_refs[0, 1, tile, start:start + high.shape[0], :] = low
        for step in range(1, ITERS):
            for part in range(2):
                blank = jnp.zeros((HALO * step, TILE), BF16)
                v_refs[step, part, tile, :HALO * step, :] = blank
                v_refs[step, part, tile, span - HALO * step:, :] = blank

    def advance(tile, carry):
        for step in range(ITERS):
            for part in range(2):
                low_row = HALO * step if part == 0 else 0
                high_row = half if part == 0 else half - HALO * step
                count = high_row - low_row
                start = part * half
                first = start + HALO + low_row
                near = v_refs[step, 0, tile, start:start + window, :]
                fine = v_refs[step, 1, tile, start:start + window, :]
                gather = jnp.concatenate(
                    [stencil[part, kind, low_row:high_row, :] for kind in range(TYPES)], axis=0
                )
                bucket = dot(gather, jnp.concatenate([near, fine, near], axis=0))
                high, low = halves(bucket)
                highs = [high[kind * count:(kind + 1) * count] for kind in range(TYPES)]
                lows = [low[kind * count:(kind + 1) * count] for kind in range(TYPES)]
                applied = dot(jnp.concatenate(highs + highs + lows, axis=1), mixer[...])
                here = (
                    v_refs[step, 0, tile, first:first + count, :].astype(F32)
                    + v_refs[step, 1, tile, first:first + count, :].astype(F32)
                )
                high, low = halves(applied + (MASS_SHIFT - shift) * here)
                v_refs[step + 1, 0, tile, first:first + count, :] = high
                v_refs[step + 1, 1, tile, first:first + count, :] = low
        return carry

    lax.fori_loop(0, tiles, advance, 0)

    back = lane_order(width, dof, True)
    for step in range(1, ITERS + 1):
        both = jnp.concatenate(
            [
                jnp.concatenate(
                    [v_refs[step, part, tile, edge:edge + rows, :] for tile in range(tiles)],
                    axis=1,
                )
                for part in range(2)
            ],
            axis=0,
        )
        basis_ref[step - 1] = dot(both, back).astype(BF16)

    def stacked(step, order):
        pieces = []
        for tile in range(tiles):
            lanes = slice(tile * TILE, (tile + 1) * TILE)
            for part in order:
                block = slice(part * rows, (part + 1) * rows)
                if step == 0:
                    pieces.append(geo_ref[block, lanes])
                else:
                    pieces.append(basis_ref[step - 1, block, lanes])
        return jnp.concatenate(pieces, axis=0)

    same_dof = iota((TILE, TILE), 0) // cases == iota((TILE, TILE), 1) // cases
    group = iota((cases, META), 1) // cases
    moments = jnp.zeros((cases, META), F32)
    for number in range(2 * ITERS):
        left, right = number // 2, (number + 1) // 2
        gram = dot_tn(stacked(left, (0, 0, 1)), stacked(right, (0, 1, 0)))
        gram = jnp.where(same_dof, gram, 0.0)
        rows_sum = gram[0:cases]
        for part in range(1, TILE // cases):
            rows_sum = rows_sum + gram[part * cases:(part + 1) * cases]
        lanes_sum = rows_sum[:, :META] + rows_sum[:, META:]
        step = META // 2
        while step >= cases:
            lanes_sum = lanes_sum + pltpu.roll(lanes_sum, step, 1)
            step //= 2
        moments = jnp.where(group == number, lanes_sum, moments)
    for device in range(moments_ref.shape[0]):
        moments_ref[device] = moments


def finish_kernel(slots, moments_ref, blocks_ref, geo_ref, basis_ref, solution_ref, residual_ref):
    rows, width = solution_ref.shape
    dof = blocks_ref.shape[1]
    cases = width // dof
    tiles = width // TILE
    shift = basis_shift(blocks_ref[...], slots)
    moments = moments_ref[0]
    for device in range(1, moments_ref.shape[0]):
        moments = moments + moments_ref[device]
    group = iota((cases, META), 1) // cases
    system = []
    for row in range(ITERS):
        plain = moments if row == 0 else pltpu.roll(moments, META - cases * row, 1)
        ahead = pltpu.roll(moments, META - cases * (row + 1), 1)
        target = pltpu.roll(moments, cases * (ITERS - row), 1)
        system.append(jnp.where(group < ITERS, ahead + shift * plain, target))
    system = jnp.concatenate(system, axis=0)
    size = ITERS * cases
    index = iota((size, 1), 0)
    for pivot in range(size):
        column = system[:, pivot:pivot + 1]
        line = system[pivot:pivot + 1, :]
        line = line / line[:, pivot:pivot + 1]
        system = jnp.where(index == pivot, line, system - column * line)

    same_dof = iota((TILE, TILE), 0) // cases == iota((TILE, TILE), 1) // cases
    unit = jnp.where(iota((cases, META), 1) % cases == iota((cases, META), 0), 1.0, 0.0)

    answers = []
    for row in range(ITERS):
        part = jnp.where(group == ITERS, system[row * cases:(row + 1) * cases], 0.0)
        step = cases
        while step < META:
            part = part + pltpu.roll(part, step, 1)
            step *= 2
        answers.append(part)
    left_over = [unit - shift * answers[0]]
    for row in range(1, ITERS):
        left_over.append(-(answers[row - 1] + shift * answers[row]))
    left_over.append(-answers[ITERS - 1])

    def spread(parts):
        highs, lows = [], []
        for part in parts:
            tall = jnp.concatenate([part] * (TILE // cases), axis=0)
            wide = jnp.concatenate([tall] * (TILE // META), axis=1)
            high, low = halves(jnp.where(same_dof, wide, 0.0))
            highs.append(high)
            lows.append(low)
        return jnp.concatenate(highs + highs + lows, axis=0)

    for out_ref, matrix in ((solution_ref, spread(answers)), (residual_ref, spread(left_over))):
        terms = matrix.shape[0] // (3 * TILE)
        for tile in range(tiles):
            lanes = slice(tile * TILE, (tile + 1) * TILE)
            highs, lows = [], []
            for term in range(terms):
                for part, pile in ((0, highs), (1, lows)):
                    block = slice(part * rows, (part + 1) * rows)
                    if term == 0:
                        pile.append(geo_ref[block, lanes])
                    else:
                        pile.append(basis_ref[term - 1, block, lanes])
            out_ref[:, lanes] = dot(jnp.concatenate(highs + lows + highs, axis=1), matrix)


def on_device(loads, row_ids, densities, block_cols, block_types, ref_blocks):
    rows, width = loads.shape
    dof = ref_blocks.shape[1]
    slots = densities.shape[1]
    cases = width // dof
    cap = rows // 4
    edge = ITERS * HALO
    span = rows + 2 * edge
    half = (span - 2 * HALO) // 2
    window = half + 2 * HALO
    tiles = width // TILE
    devices = lax.axis_size("sub")
    position = lax.axis_index("sub").astype(jnp.int32).reshape(1, 1)
    shape = jax.ShapeDtypeStruct
    up = [(i, i + 1) for i in range(devices - 1)]
    down = [(i + 1, i) for i in range(devices - 1)]
    across = [(i, (i + devices // 2) % devices) for i in range(devices)]

    block = shape((cap, width + META), F32)
    to_left, to_right, to_partner, meta = pl.pallas_call(
        functools.partial(pack_kernel, devices),
        out_shape=(block, block, block, shape((META, rows), F32)),
        in_specs=[SMEM] + [VMEM] * 5,
        out_specs=(VMEM,) * 4,
        compiler_params=PARAMS,
        name="pack",
    )(position, loads, row_ids.reshape(1, rows), densities.T, block_cols.T, block_types.T)

    from_right = lax.ppermute(to_left, "sub", down)
    from_left = lax.ppermute(to_right, "sub", up)
    from_partner = lax.ppermute(to_partner, "sub", across)

    border = shape((edge, width + META), F32)
    geo, field, geo_meta, head, tail = pl.pallas_call(
        functools.partial(arrange_kernel, dof, slots),
        out_shape=(
            shape((2 * rows, width), BF16),
            shape((rows, width), F32),
            shape((rows, META), F32),
            border,
            border,
        ),
        in_specs=[VMEM] * 5,
        out_specs=(VMEM,) * 5,
        compiler_params=PARAMS,
        name="arrange",
    )(loads, meta, from_left, from_right, from_partner)

    after = lax.ppermute(head, "sub", down)
    before = lax.ppermute(tail, "sub", up)

    basis, moments = pl.pallas_call(
        functools.partial(krylov_kernel, slots),
        out_shape=(
            shape((ITERS, 2 * rows, width), BF16),
            shape((devices, cases, META), F32),
        ),
        in_specs=[VMEM] * 6,
        out_specs=(VMEM,) * 2,
        scratch_shapes=[
            pltpu.VMEM((ITERS + 1, 2, tiles, span, TILE), BF16),
            pltpu.VMEM((span, META), F32),
            pltpu.VMEM((2, TYPES, half, 3 * window), BF16),
            pltpu.VMEM((3 * TYPES * TILE, TILE), BF16),
        ],
        compiler_params=PARAMS,
        name="krylov",
    )(before, field, geo_meta, after, ref_blocks, geo)

    moments = lax.all_to_all(moments, "sub", split_axis=0, concat_axis=0, tiled=True)

    return pl.pallas_call(
        functools.partial(finish_kernel, slots),
        out_shape=(shape((rows, width), F32), shape((rows, width), F32)),
        in_specs=[VMEM] * 4,
        out_specs=(VMEM,) * 2,
        compiler_params=PARAMS,
        name="finish",
    )(moments, ref_blocks, geo, basis)


def solution(mesh):
    placed = (
        P(("groups", "sub"), None),
        P(("groups", "sub")),
        P(("groups", "sub"), None),
        P(("groups", "sub"), None),
        P(("groups", "sub"), None),
        P(),
    )
    return jax.shard_map(
        on_device,
        mesh=mesh,
        in_specs=placed,
        out_specs=(P(("groups", "sub"), None), P(("groups", "sub"), None)),
        check_vma=False,
    )
```

```python
import functools

import jax
import jax.numpy as jnp
from jax import lax
from jax.experimental import pallas as pl
from jax.experimental.pallas import tpu as pltpu
from jax.sharding import PartitionSpec as P

HALO = 32
TYPES = 3
ITERS = 3
MASS_SHIFT = 0.5
META = 128
TILE = 256

F32 = jnp.float32
BF16 = jnp.bfloat16
VMEM = pl.BlockSpec(memory_space=pltpu.VMEM)
SMEM = pl.BlockSpec(memory_space=pltpu.SMEM)
HBM = pl.BlockSpec(memory_space=pltpu.HBM)
PARAMS = pltpu.CompilerParams(vmem_limit_bytes=40 * 1024 * 1024)


def dot(left, right):
    return jnp.dot(left, right, preferred_element_type=F32)


def dot_nt(left, right):
    return lax.dot_general(left, right, (((1,), (1,)), ((), ())), preferred_element_type=F32)


def dot_tn(left, right):
    return lax.dot_general(left, right, (((0,), (0,)), ((), ())), preferred_element_type=F32)


def halves(value):
    high = value.astype(BF16)
    return high, (value - high.astype(F32)).astype(BF16)


def iota(shape, axis):
    return lax.broadcasted_iota(jnp.int32, shape, axis)


def one_hot(condition):
    return jnp.where(condition, 1.0, 0.0).astype(BF16)


PACK_PARAMS = pltpu.CompilerParams(vmem_limit_bytes=62 * 1024 * 1024)


def basis_shift(blocks, slots):
    dof = blocks.shape[1]
    same = iota((dof, dof), 0) == iota((dof, dof), 1)
    total = sum(jnp.where(same, blocks[t], 0.0) for t in range(TYPES))
    mean = jnp.sum(jnp.sum(total, axis=1, keepdims=True), axis=0, keepdims=True) / (TYPES * dof)
    return MASS_SHIFT + 0.2 * slots * mean


def swap_blocks(piece):
    lane = iota(piece(0, 0).shape, 1)
    low = lane < META // 2
    out = []
    for tile in range(4):
        for part in range(2):
            first, second = piece(2 * part, tile // 2), piece(2 * part + 1, tile // 2)
            if tile % 2 == 0:
                second = pltpu.roll(second, META // 2, 1)
            else:
                first = pltpu.roll(first, META // 2, 1)
            out.append(jnp.where(low, first, second))
    return out


def given_to_gram():
    source, target = iota((TILE, TILE), 0), iota((TILE, TILE), 1)
    return one_hot((target // 16 == source % 16) & (target % 16 == source // 16))


def pack_kernel(devices, pos_ref, loads_hbm, rows_hbm, dens_hbm, cols_hbm, types_hbm,
                left_ref, right_ref, partner_ref, meta_ref,
                loads_ref, rows_ref, dens_ref, cols_ref, types_ref, sems):
    pairs = (
        (rows_hbm, rows_ref), (dens_hbm, dens_ref), (cols_hbm, cols_ref),
        (types_hbm, types_ref), (loads_hbm, loads_ref),
    )
    copies = [
        pltpu.make_async_copy(source, target, sems.at[number])
        for number, (source, target) in enumerate(pairs)
    ]
    for copy in copies:
        copy.start()
    for copy in copies[:4]:
        copy.wait()
    rows, width = loads_ref.shape
    slots = dens_ref.shape[0]
    cap = rows // 4
    pos = pos_ref[0, 0]
    ids = rows_ref[...]
    owner = lax.div(ids, jnp.int32(rows))
    local = (ids - owner * rows + 1).astype(F32)
    kept = owner == pos
    opposite = lax.rem(pos + devices // 2, jnp.int32(devices))
    goes = [owner == pos - 1, owner == pos + 1]
    goes.append((owner == opposite) & ~goes[0] & ~goes[1])
    flags = jnp.concatenate(
        [jnp.where(g, 1.0, 0.0) for g in goes] + [jnp.zeros((5, rows), F32)], axis=0
    )
    before = one_hot(iota((rows, rows), 0) < iota((rows, rows), 1))
    rank = dot(flags.astype(BF16), before).astype(jnp.int32)
    target = jnp.full((1, rows), -1, jnp.int32)
    for side in range(3):
        target = jnp.where(goes[side], rank[side:side + 1] + side * cap, target)
    pick = one_hot(iota((3 * cap, rows), 0) == target)

    density = dens_ref[...]
    kinds = types_ref[...]
    for kind in range(TYPES):
        meta_ref[kind * slots:(kind + 1) * slots, :] = jnp.where(kinds == kind, density, 0.0)
    meta_ref[3 * slots:4 * slots, :] = (cols_ref[...] - ids).astype(F32)
    meta_ref[4 * slots:, :] = jnp.zeros((META - 4 * slots, rows), F32)
    meta_ref[4 * slots:4 * slots + 1, :] = local
    meta_ref[4 * slots + 1:4 * slots + 2, :] = jnp.where(kept, local, 0.0)

    twice = jnp.concatenate([pick, pick], axis=1)
    meta = dot_nt(twice, jnp.concatenate(halves(meta_ref[...]), axis=1))
    copies[4].wait()
    body = dot(twice, jnp.concatenate(halves(loads_ref[...]), axis=0))
    for side, out_ref in enumerate((left_ref, right_ref, partner_ref)):
        out_ref[:, :width] = body[side * cap:(side + 1) * cap]
        out_ref[:, width:] = meta[side * cap:(side + 1) * cap]


def reorder(parts, tiles):
    count = parts[0].shape[0]
    tall = [p[:, t * TILE:(t + 1) * TILE] for t in range(tiles) for p in parts]
    moved = dot(jnp.concatenate(tall, axis=0), given_to_gram()).astype(BF16)
    return [
        jnp.concatenate(
            [moved[(2 * t + p) * count:(2 * t + p + 1) * count] for t in range(tiles)], axis=1
        )
        for p in range(2)
    ]


def prepare_kernel(slots, loads_ref, meta_ref, blocks_ref, kept_ref, kept_meta_ref, mixer_ref):
    rows, width = loads_ref.shape
    dof = blocks_ref.shape[1]
    tiles = width // TILE
    place = iota((rows, rows), 0) + 1
    own = one_hot(place == meta_ref[4 * slots + 1:4 * slots + 2, :].astype(jnp.int32))
    twice = jnp.concatenate([own, own], axis=1)
    kept_ref[...] = dot(twice, jnp.concatenate(reorder(halves(loads_ref[...]), tiles), axis=0))
    kept_meta_ref[...] = dot_nt(twice, jnp.concatenate(halves(meta_ref[...]), axis=1))

    def dof_of(lane):
        return lane // 64 * 16 + lane % 16

    fold = one_hot(dof_of(iota((TILE, dof), 0)) == iota((TILE, dof), 1))
    unfold = one_hot(dof_of(iota((dof, TILE), 1)) == iota((dof, TILE), 0))
    same_case = iota((TILE, TILE), 0) // 16 % 4 == iota((TILE, TILE), 1) // 16 % 4
    for kind in range(TYPES):
        for copies, part in zip(((0, 2), (1,)), halves(blocks_ref[kind])):
            wide = dot(dot_nt(fold, part).astype(BF16), unfold)
            wide = jnp.where(same_case, wide, 0.0).astype(BF16)
            for copy in copies:
                start = (copy * TYPES + kind) * TILE
                mixer_ref[start:start + TILE, :] = wide


def arrange_kernel(slots, kept_ref, kept_meta_ref, left_ref, right_ref, partner_ref,
                   geo_ref, field_ref, meta_ref, head_ref, tail_ref):
    rows, width = kept_ref.shape
    tiles = width // TILE
    edge = head_ref.shape[0]
    arrived = jnp.concatenate([left_ref[...], right_ref[...], partner_ref[...]], axis=0)
    count = arrived.shape[0]
    arrived_meta = arrived[:, width:]
    unit = one_hot(iota((8, META), 1) == 4 * slots)
    tags = dot_nt(unit, arrived_meta.astype(BF16))[0:1]
    other = one_hot(iota((rows, count), 0) + 1 == tags.astype(jnp.int32))
    twice = jnp.concatenate([other, other], axis=1)
    moved = reorder(halves(arrived[:, :width]), tiles)
    geo = kept_ref[...] + dot(twice, jnp.concatenate(moved, axis=0))
    meta = kept_meta_ref[...] + dot(twice, jnp.concatenate(halves(arrived_meta), axis=0))
    meta_ref[...] = meta
    head_ref[:, width:] = meta[:edge]
    tail_ref[:, width:] = meta[rows - edge:]

    def piece(tile, part):
        start = tile * TILE + part * META
        return geo[:, start:start + META]

    for number, value in enumerate(swap_blocks(piece)):
        lanes = slice(number * META, (number + 1) * META)
        head_ref[:, lanes] = value[:edge]
        tail_ref[:, lanes] = value[rows - edge:]
        inner = slice(number % 2 * META, (number % 2 + 1) * META)
        for part, half in enumerate(halves(value)):
            field_ref[part, number // 2, :, inner] = half
    for part, half in enumerate(halves(geo)):
        for tile in range(tiles):
            geo_ref[part, tile] = half[:, tile * TILE:(tile + 1) * TILE]


def stencil_rows(meta, slots, first):
    lane = iota((HALO, META), 1)
    spot = iota((HALO, TILE), 1)
    centre = iota((HALO, 1), 0) + first
    sums = [jnp.zeros((HALO, TILE), F32) for _ in range(TYPES)]
    for slot in range(slots):
        column = centre + meta[:, 3 * slots + slot:3 * slots + slot + 1].astype(jnp.int32)
        hit = spot == column
        for kind in range(TYPES):
            weight = meta[:, kind * slots + slot:kind * slots + slot + 1]
            sums[kind] += jnp.where(hit, weight, 0.0)
    out = []
    for kind in range(TYPES):
        inside = (lane >= kind * slots) & (lane < (kind + 1) * slots)
        total = jnp.sum(jnp.where(inside, meta, 0.0), axis=1, keepdims=True)
        high, low = halves(jnp.where(spot == centre, total, 0.0) - sums[kind])
        out.append(jnp.concatenate([high, high, low], axis=1))
    return out


def gathered(weights, near, fine):
    return halves(dot(weights, jnp.concatenate([near, fine, near], axis=0)))


def mixed(buckets, mixer_ref, count):
    highs = [buckets[0, kind, :count, :] for kind in range(TYPES)]
    lows = [buckets[1, kind, :count, :] for kind in range(TYPES)]
    return dot(jnp.concatenate(highs + highs + lows, axis=1), mixer_ref[...])


def interior_kernel(slots, field_ref, meta_ref, mixer_ref, blocks_ref,
                    inner_ref, weights_ref, stencil, buckets):
    tiles, rows = field_ref.shape[1:3]
    edge = ITERS * HALO
    shift = basis_shift(blocks_ref[...], slots)
    inside = rows - 2 * HALO

    def build(chunk, carry):
        first = pl.multiple_of(chunk * HALO, HALO)
        start = pl.multiple_of(chunk * HALO + HALO, HALO)
        for kind, value in enumerate(
            stencil_rows(meta_ref[pl.ds(start, HALO), :], slots, first + HALO)
        ):
            stencil[kind, pl.ds(first, HALO), :] = value
        return carry

    lax.fori_loop(0, inside // HALO, build, 0)

    def build_outer(chunk, carry):
        side = lax.div(chunk, jnp.int32(ITERS))
        first = pl.multiple_of(lax.rem(chunk, jnp.int32(ITERS)) * HALO, HALO)
        start = pl.multiple_of(first + side * (rows - edge), HALO)
        spot = jnp.where(side == 0, first + edge, first + rows - 2 * edge)
        for kind, value in enumerate(stencil_rows(meta_ref[pl.ds(start, HALO), :], slots, spot)):
            weights_ref[side, kind, pl.ds(first, HALO), :] = value
        return carry

    lax.fori_loop(0, 2 * ITERS, build_outer, 0)

    inner_ref[...] = jnp.zeros(inner_ref.shape, BF16)
    for step in range(ITERS):
        skip = HALO * step
        count = inside - 2 * skip
        begin = HALO + skip
        weights = jnp.concatenate(
            [stencil[kind, skip:inside - skip, :] for kind in range(TYPES)], axis=0
        )

        def read(part, tile, block):
            if step == 0:
                return field_ref[part, tile, block, :]
            return inner_ref[step - 1, part, tile, block, :]

        for tile in range(tiles):
            every = slice(0, rows)
            for part, half in enumerate(
                gathered(weights, read(0, tile, every), read(1, tile, every))
            ):
                for kind in range(TYPES):
                    buckets[part, kind, tile * count:(tile + 1) * count, :] = (
                        half[kind * count:(kind + 1) * count]
                    )
        applied = mixed(buckets, mixer_ref, tiles * count)
        block = slice(begin, begin + count)
        for tile in range(tiles):
            here = read(0, tile, block).astype(F32) + read(1, tile, block).astype(F32)
            value = applied[tile * count:(tile + 1) * count] + (MASS_SHIFT - shift) * here
            for part, half in enumerate(halves(value)):
                inner_ref[step, part, tile, block, :] = half


def sides_kernel(slots, before_ref, after_ref, field_ref, inner_ref, weights_ref, mixer_ref,
                 blocks_ref, geo_ref, basis_ref, moments_ref, v_refs, stencil, buckets):
    tiles, rows = field_ref.shape[1:3]
    width = tiles * TILE
    dof = blocks_ref.shape[1]
    cases = width // dof
    edge = ITERS * HALO
    span = rows + 2 * edge
    outer = edge - HALO
    count = edge
    shift = basis_shift(blocks_ref[...], slots)

    def build(chunk, carry):
        side = lax.div(chunk, jnp.int32(2))
        first = lax.rem(chunk, jnp.int32(2)) * HALO
        first = pl.multiple_of(first, HALO)
        place = pl.multiple_of(first + side * edge, HALO)
        meta = jnp.where(
            side == 0,
            before_ref[pl.ds(pl.multiple_of(first + HALO, HALO), HALO), width:],
            after_ref[pl.ds(first, HALO), width:],
        )
        spot = jnp.where(side == 0, first + HALO, first + rows - edge)
        for kind, value in enumerate(stencil_rows(meta, slots, spot)):
            stencil[side, kind, pl.ds(place, HALO), :] = value
        return carry

    lax.fori_loop(0, 4, build, 0)
    for kind in range(TYPES):
        stencil[0, kind, outer:, :] = weights_ref[0, kind]
        stencil[1, kind, :edge, :] = weights_ref[1, kind]

    for tile in range(tiles):
        lanes = slice(tile * TILE, (tile + 1) * TILE)
        for start, source in ((0, before_ref), (edge + rows, after_ref)):
            for part, half in enumerate(halves(source[:, lanes])):
                v_refs[0, part, tile, start:start + edge, :] = half
        for part in range(2):
            v_refs[0, part, tile, edge:edge + rows, :] = field_ref[part, tile]
            for step in range(1, ITERS + 1):
                begin = HALO * step
                v_refs[step, part, tile, edge + begin:edge + rows - begin, :] = (
                    inner_ref[step - 1, part, tile, begin:rows - begin, :]
                )
                if step < ITERS:
                    blank = jnp.zeros((begin, TILE), BF16)
                    v_refs[step, part, tile, :begin, :] = blank
                    v_refs[step, part, tile, span - begin:, :] = blank

    for step in range(ITERS):
        starts = (HALO * (step + 1), span - HALO * (step + 1) - count)
        for side in range(2):
            offset = HALO * step if side == 0 else outer - HALO * step
            weights = jnp.concatenate(
                [stencil[side, kind, offset:offset + count, :] for kind in range(TYPES)], axis=0
            )
            window = slice(0, TILE) if side == 0 else slice(span - TILE, span)
            for tile in range(tiles):
                row = (side * tiles + tile) * count
                for part, half in enumerate(
                    gathered(
                        weights, v_refs[step, 0, tile, window, :], v_refs[step, 1, tile, window, :]
                    )
                ):
                    for kind in range(TYPES):
                        buckets[part, kind, row:row + count, :] = (
                            half[kind * count:(kind + 1) * count]
                        )
        applied = mixed(buckets, mixer_ref, 2 * tiles * count)
        for side in range(2):
            block = slice(starts[side], starts[side] + count)
            for tile in range(tiles):
                row = (side * tiles + tile) * count
                here = (
                    v_refs[step, 0, tile, block, :].astype(F32)
                    + v_refs[step, 1, tile, block, :].astype(F32)
                )
                value = applied[row:row + count] + (MASS_SHIFT - shift) * here
                for part, half in enumerate(halves(value)):
                    v_refs[step + 1, part, tile, block, :] = half

    own = slice(edge, edge + rows)
    for step in range(1, ITERS + 1):

        def piece(tile, part):
            lanes = slice(part * META, (part + 1) * META)
            return (
                v_refs[step, 0, tile, own, lanes].astype(F32)
                + v_refs[step, 1, tile, own, lanes].astype(F32)
            )

        for number, value in enumerate(swap_blocks(piece)):
            lanes = slice(number % 2 * META, (number % 2 + 1) * META)
            for part, half in enumerate(halves(value)):
                basis_ref[step - 1, part, number // 2, :, lanes] = half

    def tall(step, part):
        if step == 0:
            return jnp.concatenate([geo_ref[part, tile] for tile in range(tiles)], axis=0)
        return jnp.concatenate([basis_ref[step - 1, part, tile] for tile in range(tiles)], axis=0)

    same_dof = iota((TILE, TILE), 0) % 16 == iota((TILE, TILE), 1) % 16
    sums = []
    for step in range(ITERS):
        high = dot_tn(
            tall(step, 0),
            jnp.concatenate([tall(step + k, part) for k in range(2) for part in range(2)], axis=1),
        )
        low = dot_tn(tall(step, 1), jnp.concatenate([tall(step + k, 0) for k in range(2)], axis=1))
        for k in range(2):
            gram = (
                high[:, 2 * k * TILE:(2 * k + 1) * TILE]
                + high[:, (2 * k + 1) * TILE:(2 * k + 2) * TILE]
                + low[:, k * TILE:(k + 1) * TILE]
            )
            gram = jnp.where(same_dof, gram, 0.0)
            sums.append(jnp.sum(gram.reshape(cases, TILE // cases, TILE), axis=1))
    rest = jnp.concatenate(sums, axis=0)
    pieces = []
    for _ in range(3):
        pieces.append(rest.astype(BF16))
        rest = rest - pieces[-1].astype(F32)
    collect = one_hot(iota((TILE, META), 0) // 16 == iota((TILE, META), 1) % 16)
    folded = dot(jnp.concatenate(pieces, axis=1), jnp.concatenate([collect] * 3, axis=0))
    group = iota((cases, META), 1) // cases
    moments = jnp.zeros((cases, META), F32)
    for number in range(2 * ITERS):
        part = folded[number * cases:(number + 1) * cases]
        moments = jnp.where(group == number, part, moments)
    for device in range(moments_ref.shape[0]):
        moments_ref[device] = moments


def finish_kernel(slots, moments_ref, blocks_ref, geo_ref, basis_ref, solution_ref, residual_ref):
    rows, width = solution_ref.shape
    dof = blocks_ref.shape[1]
    cases = width // dof
    tiles = width // TILE
    shift = basis_shift(blocks_ref[...], slots)
    moments = moments_ref[0]
    for device in range(1, moments_ref.shape[0]):
        moments = moments + moments_ref[device]
    group = iota((cases, META), 1) // cases
    system = []
    for row in range(ITERS):
        plain = moments if row == 0 else pltpu.roll(moments, META - cases * row, 1)
        ahead = pltpu.roll(moments, META - cases * (row + 1), 1)
        target = pltpu.roll(moments, cases * (ITERS - row), 1)
        system.append(jnp.where(group < ITERS, ahead + shift * plain, target))
    system = jnp.concatenate(system, axis=0)
    size = ITERS * cases
    index = iota((size, 1), 0)
    for pivot in range(size):
        column = jnp.broadcast_to(system[:, pivot:pivot + 1], (size, META))
        line = system[pivot:pivot + 1, :] / column[pivot:pivot + 1, :]
        system = jnp.where(index == pivot, line, system - column * line)

    unit = jnp.where(iota((cases, META), 1) % cases == iota((cases, META), 0), 1.0, 0.0)
    answers = []
    for row in range(ITERS):
        part = jnp.where(group == ITERS, system[row * cases:(row + 1) * cases], 0.0)
        step = cases
        while step < META:
            part = part + pltpu.roll(part, step, 1)
            step *= 2
        answers.append(part)
    left_over = [unit - shift * answers[0]]
    for row in range(1, ITERS):
        left_over.append(-(answers[row - 1] + shift * answers[row]))
    left_over.append(-answers[ITERS - 1])

    meets = iota((TILE, TILE), 0) % 16 == iota((TILE, TILE), 1) // 16

    def spread(parts):
        highs, lows = [], []
        for part in parts:
            tall = jnp.broadcast_to(part[:, None, :], (cases, TILE // cases, META))
            tall = tall.reshape(TILE, META)
            wide = jnp.concatenate([tall] * (TILE // META), axis=1)
            high, low = halves(jnp.where(meets, wide, 0.0))
            highs.append(high)
            lows.append(low)
        return jnp.concatenate(highs + highs + lows, axis=0)

    def tall(term, part):
        if term == 0:
            return jnp.concatenate([geo_ref[part, tile] for tile in range(tiles)], axis=0)
        return jnp.concatenate([basis_ref[term - 1, part, tile] for tile in range(tiles)], axis=0)

    for out_ref, matrix in ((solution_ref, spread(answers)), (residual_ref, spread(left_over))):
        terms = matrix.shape[0] // (3 * TILE)
        highs = [tall(term, 0) for term in range(terms)]
        lows = [tall(term, 1) for term in range(terms)]
        value = dot(jnp.concatenate(highs + lows + highs, axis=1), matrix)
        for tile in range(tiles):
            out_ref[:, tile * TILE:(tile + 1) * TILE] = value[tile * rows:(tile + 1) * rows]


def on_device(loads, row_ids, densities, block_cols, block_types, ref_blocks):
    rows, width = loads.shape
    slots = densities.shape[1]
    cases = width // ref_blocks.shape[1]
    cap = rows // 4
    edge = ITERS * HALO
    span = rows + 2 * edge
    tiles = width // TILE
    devices = lax.axis_size("sub")
    position = lax.axis_index("sub").astype(jnp.int32).reshape(1, 1)
    shape = jax.ShapeDtypeStruct
    up = [(i, i + 1) for i in range(devices - 1)]
    down = [(i + 1, i) for i in range(devices - 1)]
    across = [(i, (i + devices // 2) % devices) for i in range(devices)]

    block = shape((cap, width + META), F32)
    to_left, to_right, to_partner, meta = pl.pallas_call(
        functools.partial(pack_kernel, devices),
        out_shape=(block, block, block, shape((META, rows), F32)),
        in_specs=[SMEM] + [HBM] * 5,
        out_specs=(VMEM,) * 4,
        scratch_shapes=[
            pltpu.VMEM((rows, width), F32),
            pltpu.VMEM((1, rows), jnp.int32),
            pltpu.VMEM((slots, rows), F32),
            pltpu.VMEM((slots, rows), jnp.int32),
            pltpu.VMEM((slots, rows), jnp.int32),
            pltpu.SemaphoreType.DMA((5,)),
        ],
        compiler_params=PACK_PARAMS,
        name="pack",
    )(position, loads, row_ids.reshape(1, rows), densities.T, block_cols.T, block_types.T)

    from_partner = lax.ppermute(to_partner, "sub", across)
    from_left = lax.ppermute(to_right, "sub", up)
    from_right = lax.ppermute(to_left, "sub", down)

    mixer_shape = shape((3 * TYPES * TILE, TILE), BF16)
    kept, kept_meta, mixer = pl.pallas_call(
        functools.partial(prepare_kernel, slots),
        out_shape=(shape((rows, width), F32), shape((rows, META), F32), mixer_shape),
        in_specs=[VMEM] * 3,
        out_specs=(VMEM,) * 3,
        compiler_params=PARAMS,
        cost_estimate=pl.CostEstimate(
            flops=4_000_000_000, bytes_accessed=4_000_000, transcendentals=0
        ),
        name="prepare",
    )(loads, meta, ref_blocks)

    border = shape((edge, width + META), F32)
    pair = shape((2, tiles, rows, TILE), BF16)
    geo, field, geo_meta, head, tail = pl.pallas_call(
        functools.partial(arrange_kernel, slots),
        out_shape=(pair, pair, shape((rows, META), F32), border, border),
        in_specs=[VMEM] * 5,
        out_specs=(VMEM,) * 5,
        compiler_params=PARAMS,
        name="arrange",
    )(kept, kept_meta, from_left, from_right, from_partner)

    after = lax.ppermute(head, "sub", down)
    before = lax.ppermute(tail, "sub", up)

    basis_shape = shape((ITERS, 2, tiles, rows, TILE), BF16)
    inner, weights = pl.pallas_call(
        functools.partial(interior_kernel, slots),
        out_shape=(basis_shape, shape((2, TYPES, edge, 3 * TILE), BF16)),
        in_specs=[VMEM] * 4,
        out_specs=(VMEM,) * 2,
        scratch_shapes=[
            pltpu.VMEM((TYPES, rows - 2 * HALO, 3 * TILE), BF16),
            pltpu.VMEM((2, TYPES, tiles * (rows - 2 * HALO), TILE), BF16),
        ],
        compiler_params=PARAMS,
        cost_estimate=pl.CostEstimate(
            flops=10_000_000_000, bytes_accessed=8_000_000, transcendentals=0
        ),
        name="interior",
    )(field, geo_meta, mixer, ref_blocks)

    basis, moments = pl.pallas_call(
        functools.partial(sides_kernel, slots),
        out_shape=(basis_shape, shape((devices, cases, META), F32)),
        in_specs=[VMEM] * 8,
        out_specs=(VMEM,) * 2,
        scratch_shapes=[
            pltpu.VMEM((ITERS + 1, 2, tiles, span, TILE), BF16),
            pltpu.VMEM((2, TYPES, 2 * edge - HALO, 3 * TILE), BF16),
            pltpu.VMEM((2, TYPES, 2 * tiles * edge, TILE), BF16),
        ],
        compiler_params=PARAMS,
        name="sides",
    )(before, after, field, inner, weights, mixer, ref_blocks, geo)

    moments = lax.all_to_all(moments, "sub", split_axis=0, concat_axis=0, tiled=True)

    return pl.pallas_call(
        functools.partial(finish_kernel, slots),
        out_shape=(shape((rows, width), F32), shape((rows, width), F32)),
        in_specs=[VMEM] * 4,
        out_specs=(VMEM,) * 2,
        compiler_params=PARAMS,
        name="finish",
    )(moments, ref_blocks, geo, basis)


def solution(mesh):
    placed = (
        P(("groups", "sub"), None),
        P(("groups", "sub")),
        P(("groups", "sub"), None),
        P(("groups", "sub"), None),
        P(("groups", "sub"), None),
        P(),
    )
    return jax.shard_map(
        on_device,
        mesh=mesh,
        in_specs=placed,
        out_specs=(P(("groups", "sub"), None), P(("groups", "sub"), None)),
        check_vma=False,
    )
```

```python
import functools

import jax
import jax.numpy as jnp
from jax import lax
from jax.experimental import pallas as pl
from jax.experimental.pallas import tpu as pltpu
from jax.sharding import PartitionSpec as P

HALO = 32
TYPES = 3
ITERS = 3
MASS_SHIFT = 0.5
META = 128
TILE = 256

F32 = jnp.float32
BF16 = jnp.bfloat16
VMEM = pl.BlockSpec(memory_space=pltpu.VMEM)
SMEM = pl.BlockSpec(memory_space=pltpu.SMEM)
HBM = pl.BlockSpec(memory_space=pltpu.HBM)
PARAMS = pltpu.CompilerParams(vmem_limit_bytes=40 * 1024 * 1024)


def dot(left, right):
    return jnp.dot(left, right, preferred_element_type=F32)


def dot_nt(left, right):
    return lax.dot_general(left, right, (((1,), (1,)), ((), ())), preferred_element_type=F32)


def dot_tn(left, right):
    return lax.dot_general(left, right, (((0,), (0,)), ((), ())), preferred_element_type=F32)


def halves(value):
    high = value.astype(BF16)
    return high, (value - high.astype(F32)).astype(BF16)


def iota(shape, axis):
    return lax.broadcasted_iota(jnp.int32, shape, axis)


def one_hot(condition):
    return jnp.where(condition, 1.0, 0.0).astype(BF16)


PACK_PARAMS = pltpu.CompilerParams(vmem_limit_bytes=62 * 1024 * 1024)


def basis_shift(blocks, slots):
    dof = blocks.shape[1]
    same = iota((dof, dof), 0) == iota((dof, dof), 1)
    total = sum(jnp.where(same, blocks[t], 0.0) for t in range(TYPES))
    mean = jnp.sum(jnp.sum(total, axis=1, keepdims=True), axis=0, keepdims=True) / (TYPES * dof)
    return MASS_SHIFT + 0.2 * slots * mean


def swap_blocks(piece):
    lane = iota(piece(0, 0).shape, 1)
    low = lane < META // 2
    out = []
    for tile in range(4):
        for part in range(2):
            first, second = piece(2 * part, tile // 2), piece(2 * part + 1, tile // 2)
            if tile % 2 == 0:
                second = pltpu.roll(second, META // 2, 1)
            else:
                first = pltpu.roll(first, META // 2, 1)
            out.append(jnp.where(low, first, second))
    return out


def given_to_gram():
    source, target = iota((TILE, TILE), 0), iota((TILE, TILE), 1)
    return one_hot((target // 16 == source % 16) & (target % 16 == source // 16))


def peers(pos, devices):
    odd = lax.rem(pos, jnp.int32(2))
    return (
        pos + 1 - 2 * odd,
        pos - 1 + 2 * odd,
        lax.rem(pos + devices // 2, jnp.int32(devices)),
    )


def targets(pos, ids, rows, devices):
    cap = rows // 4
    owner = lax.div(ids, jnp.int32(rows))
    goes = []
    for peer in peers(pos, devices):
        here = owner == peer
        for other in goes:
            here = here & ~other
        goes.append(here)
    flags = jnp.concatenate(
        [jnp.where(g, 1.0, 0.0) for g in goes] + [jnp.zeros((5, rows), F32)], axis=0
    )
    before = one_hot(iota((rows, rows), 0) < iota((rows, rows), 1))
    rank = dot(flags.astype(BF16), before).astype(jnp.int32)
    target = jnp.full((1, rows), -1, jnp.int32)
    for side in range(3):
        target = jnp.where(goes[side], rank[side:side + 1] + side * cap, target)
    return target


def fill_block(pick, loads, meta, out_ref):
    width = loads.shape[1]
    twice = jnp.concatenate([pick, pick], axis=1)
    out_ref[:, width:] = dot_nt(twice, jnp.concatenate(halves(meta), axis=1))
    out_ref[:, :width] = dot(twice, jnp.concatenate(halves(loads), axis=0))


def pack_far_kernel(devices, pos_ref, loads_hbm, rows_hbm, dens_hbm, cols_hbm, types_hbm,
                    far_ref, meta_ref, target_ref,
                    loads_ref, rows_ref, dens_ref, cols_ref, types_ref, sems):
    pairs = (
        (rows_hbm, rows_ref), (dens_hbm, dens_ref), (cols_hbm, cols_ref),
        (types_hbm, types_ref), (loads_hbm, loads_ref),
    )
    copies = [
        pltpu.make_async_copy(source, target, sems.at[number])
        for number, (source, target) in enumerate(pairs)
    ]
    for copy in copies:
        copy.start()
    for copy in copies[:4]:
        copy.wait()
    rows = loads_ref.shape[0]
    slots = dens_ref.shape[0]
    cap = rows // 4
    pos = pos_ref[0, 0]
    ids = rows_ref[...]
    owner = lax.div(ids, jnp.int32(rows))
    local = (ids - owner * rows + 1).astype(F32)
    target = targets(pos, ids, rows, devices)
    target_ref[...] = jnp.broadcast_to(target, target_ref.shape)

    density = dens_ref[...]
    kinds = types_ref[...]
    for kind in range(TYPES):
        meta_ref[kind * slots:(kind + 1) * slots, :] = jnp.where(kinds == kind, density, 0.0)
    meta_ref[3 * slots:4 * slots, :] = (cols_ref[...] - ids).astype(F32)
    meta_ref[4 * slots:, :] = jnp.zeros((META - 4 * slots, rows), F32)
    meta_ref[4 * slots:4 * slots + 1, :] = local
    meta_ref[4 * slots + 1:4 * slots + 2, :] = jnp.where(owner == pos, local, 0.0)

    copies[4].wait()
    pick = one_hot(iota((cap, rows), 0) + 2 * cap == target)
    fill_block(pick, loads_ref[...], meta_ref[...], far_ref)


def pack_near_kernel(target_hbm, meta_hbm, loads_hbm, core_ref, chip_ref,
                     target_ref, meta_ref, loads_ref, sems):
    pairs = ((target_hbm, target_ref), (meta_hbm, meta_ref), (loads_hbm, loads_ref))
    copies = [
        pltpu.make_async_copy(source, target, sems.at[number])
        for number, (source, target) in enumerate(pairs)
    ]
    for copy in copies:
        copy.start()
    for copy in copies:
        copy.wait()
    rows = loads_ref.shape[0]
    cap = rows // 4
    for side, out_ref in enumerate((core_ref, chip_ref)):
        pick = one_hot(iota((cap, rows), 0) + side * cap == target_ref[0:1, :])
        fill_block(pick, loads_ref[...], meta_ref[...], out_ref)


def reorder(parts, tiles):
    count = parts[0].shape[0]
    tall = [p[:, t * TILE:(t + 1) * TILE] for t in range(tiles) for p in parts]
    moved = dot(jnp.concatenate(tall, axis=0), given_to_gram()).astype(BF16)
    return [
        jnp.concatenate(
            [moved[(2 * t + p) * count:(2 * t + p + 1) * count] for t in range(tiles)], axis=1
        )
        for p in range(2)
    ]


def prepare_kernel(slots, loads_ref, meta_ref, blocks_ref, kept_ref, kept_meta_ref, mixer_ref):
    rows, width = loads_ref.shape
    dof = blocks_ref.shape[1]
    tiles = width // TILE
    place = iota((rows, rows), 0) + 1
    own = one_hot(place == meta_ref[4 * slots + 1:4 * slots + 2, :].astype(jnp.int32))
    twice = jnp.concatenate([own, own], axis=1)
    kept_ref[...] = dot(twice, jnp.concatenate(reorder(halves(loads_ref[...]), tiles), axis=0))
    kept_meta_ref[...] = dot_nt(twice, jnp.concatenate(halves(meta_ref[...]), axis=1))

    def dof_of(lane):
        return lane // 64 * 16 + lane % 16

    fold = one_hot(dof_of(iota((TILE, dof), 0)) == iota((TILE, dof), 1))
    unfold = one_hot(dof_of(iota((dof, TILE), 1)) == iota((dof, TILE), 0))
    same_case = iota((TILE, TILE), 0) // 16 % 4 == iota((TILE, TILE), 1) // 16 % 4
    for kind in range(TYPES):
        for copies, part in zip(((0, 2), (1,)), halves(blocks_ref[kind])):
            wide = dot(dot_nt(fold, part).astype(BF16), unfold)
            wide = jnp.where(same_case, wide, 0.0).astype(BF16)
            for copy in copies:
                start = (copy * TYPES + kind) * TILE
                mixer_ref[start:start + TILE, :] = wide


def arrange_kernel(slots, pos_ref, kept_ref, kept_meta_ref, core_ref, chip_ref, far_ref,
                   geo_ref, field_ref, meta_ref, to_core_ref, to_chip_ref):
    rows, width = kept_ref.shape
    tiles = width // TILE
    edge = to_core_ref.shape[0]
    even = lax.rem(pos_ref[0, 0], jnp.int32(2)) == 0
    arrived = jnp.concatenate([core_ref[...], chip_ref[...], far_ref[...]], axis=0)
    count = arrived.shape[0]
    arrived_meta = arrived[:, width:]
    unit = one_hot(iota((8, META), 1) == 4 * slots)
    tags = dot_nt(unit, arrived_meta.astype(BF16))[0:1]
    other = one_hot(iota((rows, count), 0) + 1 == tags.astype(jnp.int32))
    twice = jnp.concatenate([other, other], axis=1)
    moved = reorder(halves(arrived[:, :width]), tiles)
    geo = kept_ref[...] + dot(twice, jnp.concatenate(moved, axis=0))
    meta = kept_meta_ref[...] + dot(twice, jnp.concatenate(halves(arrived_meta), axis=0))
    meta_ref[...] = meta

    def send(lanes, value):
        head, tail = value[:edge], value[rows - edge:]
        to_core_ref[:, lanes] = jnp.where(even, tail, head)
        to_chip_ref[:, lanes] = jnp.where(even, head, tail)

    send(slice(width, None), meta)

    def piece(tile, part):
        start = tile * TILE + part * META
        return geo[:, start:start + META]

    for number, value in enumerate(swap_blocks(piece)):
        lanes = slice(number * META, (number + 1) * META)
        send(lanes, value)
        inner = slice(number % 2 * META, (number % 2 + 1) * META)
        for part, half in enumerate(halves(value)):
            field_ref[part, number // 2, :, inner] = half
    for part, half in enumerate(halves(geo)):
        for tile in range(tiles):
            geo_ref[part, tile] = half[:, tile * TILE:(tile + 1) * TILE]


def stencil_rows(meta, slots, first):
    lane = iota((HALO, META), 1)
    spot = iota((HALO, TILE), 1)
    centre = iota((HALO, 1), 0) + first
    sums = [jnp.zeros((HALO, TILE), F32) for _ in range(TYPES)]
    for slot in range(slots):
        column = centre + meta[:, 3 * slots + slot:3 * slots + slot + 1].astype(jnp.int32)
        hit = spot == column
        for kind in range(TYPES):
            weight = meta[:, kind * slots + slot:kind * slots + slot + 1]
            sums[kind] += jnp.where(hit, weight, 0.0)
    out = []
    for kind in range(TYPES):
        inside = (lane >= kind * slots) & (lane < (kind + 1) * slots)
        total = jnp.sum(jnp.where(inside, meta, 0.0), axis=1, keepdims=True)
        high, low = halves(jnp.where(spot == centre, total, 0.0) - sums[kind])
        out.append(jnp.concatenate([high, high, low], axis=1))
    return out


def gathered(weights, near, fine):
    return halves(dot(weights, jnp.concatenate([near, fine, near], axis=0)))


def mixed(buckets, mixer_ref, count):
    highs = [buckets[0, kind, :count, :] for kind in range(TYPES)]
    lows = [buckets[1, kind, :count, :] for kind in range(TYPES)]
    return dot(jnp.concatenate(highs + highs + lows, axis=1), mixer_ref[...])


def interior_kernel(slots, field_ref, meta_ref, mixer_ref, blocks_ref,
                    inner_ref, weights_ref, stencil, buckets):
    tiles, rows = field_ref.shape[1:3]
    edge = ITERS * HALO
    shift = basis_shift(blocks_ref[...], slots)
    inside = rows - 2 * HALO

    def build(chunk, carry):
        first = pl.multiple_of(chunk * HALO, HALO)
        start = pl.multiple_of(chunk * HALO + HALO, HALO)
        for kind, value in enumerate(
            stencil_rows(meta_ref[pl.ds(start, HALO), :], slots, first + HALO)
        ):
            stencil[kind, pl.ds(first, HALO), :] = value
        return carry

    lax.fori_loop(0, inside // HALO, build, 0)

    def build_outer(chunk, carry):
        side = lax.div(chunk, jnp.int32(ITERS))
        first = pl.multiple_of(lax.rem(chunk, jnp.int32(ITERS)) * HALO, HALO)
        start = pl.multiple_of(first + side * (rows - edge), HALO)
        spot = jnp.where(side == 0, first + edge, first + rows - 2 * edge)
        for kind, value in enumerate(stencil_rows(meta_ref[pl.ds(start, HALO), :], slots, spot)):
            weights_ref[side, kind, pl.ds(first, HALO), :] = value
        return carry

    lax.fori_loop(0, 2 * ITERS, build_outer, 0)

    for step in range(ITERS - 1):
        begin = HALO * (step + 1)
        blank = jnp.zeros((begin, TILE), BF16)
        for part in range(2):
            for tile in range(tiles):
                inner_ref[step, part, tile, :begin, :] = blank
                inner_ref[step, part, tile, rows - begin:, :] = blank
    for step in range(ITERS):
        skip = HALO * step
        count = inside - 2 * skip
        begin = HALO + skip
        weights = jnp.concatenate(
            [stencil[kind, skip:inside - skip, :] for kind in range(TYPES)], axis=0
        )

        def read(part, tile, block):
            if step == 0:
                return field_ref[part, tile, block, :]
            return inner_ref[step - 1, part, tile, block, :]

        for tile in range(tiles):
            every = slice(0, rows)
            for part, half in enumerate(
                gathered(weights, read(0, tile, every), read(1, tile, every))
            ):
                for kind in range(TYPES):
                    buckets[part, kind, tile * count:(tile + 1) * count, :] = (
                        half[kind * count:(kind + 1) * count]
                    )
        applied = mixed(buckets, mixer_ref, tiles * count)
        block = slice(begin, begin + count)
        for tile in range(tiles):
            here = read(0, tile, block).astype(F32) + read(1, tile, block).astype(F32)
            value = applied[tile * count:(tile + 1) * count] + (MASS_SHIFT - shift) * here
            for part, half in enumerate(halves(value)):
                inner_ref[step, part, tile, block, :] = half


def sides_kernel(slots, pos_ref, core_ref, chip_ref, field_ref, inner_ref, weights_ref, mixer_ref,
                 blocks_ref, geo_ref, basis_ref, moments_ref, v_refs, meta_refs, stencil, buckets):
    tiles, rows = field_ref.shape[1:3]
    width = tiles * TILE
    dof = blocks_ref.shape[1]
    cases = width // dof
    edge = ITERS * HALO
    outer = edge - HALO
    count = edge
    rest = TILE - edge
    shift = basis_shift(blocks_ref[...], slots)
    even = lax.rem(pos_ref[0, 0], jnp.int32(2)) == 0

    for tile in range(tiles + 1):
        lanes = slice(tile * TILE, (tile + 1) * TILE) if tile < tiles else slice(width, None)
        core, chip = core_ref[:, lanes], chip_ref[:, lanes]
        for side, value in enumerate((jnp.where(even, chip, core), jnp.where(even, core, chip))):
            if tile == tiles:
                meta_refs[side] = value
            else:
                for part, half in enumerate(halves(value)):
                    v_refs[0, side, part, tile] = half

    def build(chunk, carry):
        side = lax.div(chunk, jnp.int32(2))
        first = pl.multiple_of(lax.rem(chunk, jnp.int32(2)) * HALO, HALO)
        start = pl.multiple_of(first + HALO * (1 - side), HALO)
        spot = jnp.where(side == 0, first + HALO, first + rows - edge)
        for kind, value in enumerate(
            stencil_rows(meta_refs[side, pl.ds(start, HALO), :], slots, spot)
        ):
            stencil[side, kind, pl.ds(first, HALO), :] = value
        return carry

    lax.fori_loop(0, 4, build, 0)

    def window(step, side, part, tile):
        near = v_refs[step, side, part, tile]
        if step == 0:
            if side == 0:
                return jnp.concatenate([near, field_ref[part, tile, :rest, :]], axis=0)
            return jnp.concatenate([field_ref[part, tile, rows - rest:, :], near], axis=0)
        blank = jnp.zeros((HALO * step, TILE), BF16)
        begin = HALO * step
        if side == 0:
            far = inner_ref[step - 1, part, tile, begin:rest, :]
            return jnp.concatenate([blank, near, far], axis=0)
        far = inner_ref[step - 1, part, tile, rows - rest:rows - begin, :]
        return jnp.concatenate([far, near, blank], axis=0)

    def weight_rows(step, side, kind):
        keep = outer - HALO * step
        if side == 0:
            pieces = [weights_ref[0, kind, :count - keep, :]]
            if keep:
                pieces.insert(0, stencil[0, kind, outer - keep:, :])
        else:
            pieces = [weights_ref[1, kind, keep:, :]]
            if keep:
                pieces.append(stencil[1, kind, :keep, :])
        return jnp.concatenate(pieces, axis=0)

    for step in range(ITERS):
        centres = []
        for side in range(2):
            weights = jnp.concatenate(
                [weight_rows(step, side, kind) for kind in range(TYPES)], axis=0
            )
            for tile in range(tiles):
                row = (side * tiles + tile) * count
                near, fine = (window(step, side, part, tile) for part in range(2))
                first = HALO * (step + 1) if side == 0 else TILE - HALO * (step + 1) - count
                centres.append((near[first:first + count], fine[first:first + count]))
                for part, half in enumerate(gathered(weights, near, fine)):
                    for kind in range(TYPES):
                        buckets[part, kind, row:row + count, :] = (
                            half[kind * count:(kind + 1) * count]
                        )
        applied = mixed(buckets, mixer_ref, 2 * tiles * count)
        for side in range(2):
            for tile in range(tiles):
                number = side * tiles + tile
                near, fine = centres[number]
                here = near.astype(F32) + fine.astype(F32)
                value = applied[number * count:(number + 1) * count] + (MASS_SHIFT - shift) * here
                for part, half in enumerate(halves(value)):
                    v_refs[step + 1, side, part, tile] = half

    for step in range(1, ITERS + 1):
        begin = HALO * step

        def piece(tile, part):
            lanes = slice(part * META, (part + 1) * META)
            high, low = (
                jnp.concatenate(
                    [
                        v_refs[step, 0, half, tile, count - begin:, lanes],
                        inner_ref[step - 1, half, tile, begin:rows - begin, lanes],
                        v_refs[step, 1, half, tile, :begin, lanes],
                    ],
                    axis=0,
                )
                for half in range(2)
            )
            return high.astype(F32) + low.astype(F32)

        for number, value in enumerate(swap_blocks(piece)):
            lanes = slice(number % 2 * META, (number % 2 + 1) * META)
            for part, half in enumerate(halves(value)):
                basis_ref[step - 1, part, number // 2, :, lanes] = half

    def tall(step, part):
        if step == 0:
            return jnp.concatenate([geo_ref[part, tile] for tile in range(tiles)], axis=0)
        return jnp.concatenate([basis_ref[step - 1, part, tile] for tile in range(tiles)], axis=0)

    same_dof = iota((TILE, TILE), 0) % 16 == iota((TILE, TILE), 1) % 16
    sums = []
    for step in range(ITERS):
        high = dot_tn(
            tall(step, 0),
            jnp.concatenate([tall(step + k, part) for k in range(2) for part in range(2)], axis=1),
        )
        low = dot_tn(tall(step, 1), jnp.concatenate([tall(step + k, 0) for k in range(2)], axis=1))
        for k in range(2):
            gram = (
                high[:, 2 * k * TILE:(2 * k + 1) * TILE]
                + high[:, (2 * k + 1) * TILE:(2 * k + 2) * TILE]
                + low[:, k * TILE:(k + 1) * TILE]
            )
            gram = jnp.where(same_dof, gram, 0.0)
            sums.append(jnp.sum(gram.reshape(cases, TILE // cases, TILE), axis=1))
    remainder = jnp.concatenate(sums, axis=0)
    pieces = []
    for _ in range(3):
        pieces.append(remainder.astype(BF16))
        remainder = remainder - pieces[-1].astype(F32)
    collect = one_hot(iota((TILE, META), 0) // 16 == iota((TILE, META), 1) % 16)
    folded = dot(jnp.concatenate(pieces, axis=1), jnp.concatenate([collect] * 3, axis=0))
    group = iota((cases, META), 1) // cases
    moments = jnp.zeros((cases, META), F32)
    for number in range(2 * ITERS):
        part = folded[number * cases:(number + 1) * cases]
        moments = jnp.where(group == number, part, moments)
    moments_ref[...] = moments


def refined_reciprocal(value):
    guess = pl.reciprocal(value, approx=True)
    for _ in range(2):
        guess = guess * (2.0 - value * guess)
    return guess


def finish_kernel(slots, moments_ref, blocks_ref, geo_ref, basis_ref, solution_ref, residual_ref):
    rows, width = solution_ref.shape
    dof = blocks_ref.shape[1]
    cases = width // dof
    tiles = width // TILE
    shift = basis_shift(blocks_ref[...], slots)
    moments = moments_ref[0]
    for device in range(1, moments_ref.shape[0]):
        moments = moments + moments_ref[device]
    group = iota((cases, META), 1) // cases
    system = []
    for row in range(ITERS):
        plain = moments if row == 0 else pltpu.roll(moments, META - cases * row, 1)
        ahead = pltpu.roll(moments, META - cases * (row + 1), 1)
        target = pltpu.roll(moments, cases * (ITERS - row), 1)
        system.append(jnp.where(group < ITERS, ahead + shift * plain, target))
    system = jnp.concatenate(system, axis=0)
    size = ITERS * cases
    index = iota((size, 1), 0)
    for pivot in range(0, size, 2):
        column_a = jnp.broadcast_to(system[:, pivot:pivot + 1], (size, META))
        column_b = jnp.broadcast_to(system[:, pivot + 1:pivot + 2], (size, META))
        line_a = system[pivot:pivot + 1, :]
        line_b = system[pivot + 1:pivot + 2, :]
        above = column_b[pivot:pivot + 1, :]
        inverse = refined_reciprocal(column_a[pivot:pivot + 1, :])
        factor = column_a[pivot + 1:pivot + 2, :] * inverse
        corner = column_b[pivot + 1:pivot + 2, :] - factor * above
        line_b = (line_b - factor * line_a) * refined_reciprocal(corner)
        line_a = (line_a - above * line_b) * inverse
        update = system - column_a * line_a - column_b * line_b
        system = jnp.where(index == pivot, line_a, jnp.where(index == pivot + 1, line_b, update))

    unit = jnp.where(iota((cases, META), 1) % cases == iota((cases, META), 0), 1.0, 0.0)
    answers = []
    for row in range(ITERS):
        part = jnp.where(group == ITERS, system[row * cases:(row + 1) * cases], 0.0)
        step = cases
        while step < META:
            part = part + pltpu.roll(part, step, 1)
            step *= 2
        answers.append(part)
    left_over = [unit - shift * answers[0]]
    for row in range(1, ITERS):
        left_over.append(-(answers[row - 1] + shift * answers[row]))
    left_over.append(-answers[ITERS - 1])

    meets = iota((TILE, TILE), 0) % 16 == iota((TILE, TILE), 1) // 16

    def spread(parts):
        highs, lows = [], []
        for part in parts:
            tall = jnp.broadcast_to(part[:, None, :], (cases, TILE // cases, META))
            tall = tall.reshape(TILE, META)
            wide = jnp.concatenate([tall] * (TILE // META), axis=1)
            high, low = halves(jnp.where(meets, wide, 0.0))
            highs.append(high)
            lows.append(low)
        return jnp.concatenate(highs + highs + lows, axis=0)

    def tall(term, part):
        if term == 0:
            return jnp.concatenate([geo_ref[part, tile] for tile in range(tiles)], axis=0)
        return jnp.concatenate([basis_ref[term - 1, part, tile] for tile in range(tiles)], axis=0)

    for out_ref, matrix in ((solution_ref, spread(answers)), (residual_ref, spread(left_over))):
        terms = matrix.shape[0] // (3 * TILE)
        highs = [tall(term, 0) for term in range(terms)]
        lows = [tall(term, 1) for term in range(terms)]
        value = dot(jnp.concatenate(highs + lows + highs, axis=1), matrix)
        for tile in range(tiles):
            out_ref[:, tile * TILE:(tile + 1) * TILE] = value[tile * rows:(tile + 1) * rows]


def on_device(loads, row_ids, densities, block_cols, block_types, ref_blocks):
    rows, width = loads.shape
    slots = densities.shape[1]
    cases = width // ref_blocks.shape[1]
    cap = rows // 4
    edge = ITERS * HALO
    tiles = width // TILE
    devices = lax.axis_size("sub")
    position = lax.axis_index("sub").astype(jnp.int32).reshape(1, 1)
    shape = jax.ShapeDtypeStruct
    same_chip = [(i, i ^ 1) for i in range(devices)]
    next_chip = [(i, i + 1) for i in range(1, devices - 1, 2)]
    next_chip += [(i + 1, i) for i in range(1, devices - 1, 2)]
    across = [(i, (i + devices // 2) % devices) for i in range(devices)]

    block = shape((cap, width + META), F32)
    to_far, meta, target = pl.pallas_call(
        functools.partial(pack_far_kernel, devices),
        out_shape=(block, shape((META, rows), F32), shape((8, rows), jnp.int32)),
        in_specs=[SMEM] + [HBM] * 5,
        out_specs=(VMEM,) * 3,
        scratch_shapes=[
            pltpu.VMEM((rows, width), F32),
            pltpu.VMEM((1, rows), jnp.int32),
            pltpu.VMEM((slots, rows), F32),
            pltpu.VMEM((slots, rows), jnp.int32),
            pltpu.VMEM((slots, rows), jnp.int32),
            pltpu.SemaphoreType.DMA((5,)),
        ],
        compiler_params=PACK_PARAMS,
        name="pack_far",
    )(position, loads, row_ids.reshape(1, rows), densities.T, block_cols.T, block_types.T)
    from_far = lax.ppermute(to_far, "sub", across)

    to_core, to_chip = pl.pallas_call(
        pack_near_kernel,
        out_shape=(block, block),
        in_specs=[HBM] * 3,
        out_specs=(VMEM,) * 2,
        scratch_shapes=[
            pltpu.VMEM((8, rows), jnp.int32),
            pltpu.VMEM((META, rows), F32),
            pltpu.VMEM((rows, width), F32),
            pltpu.SemaphoreType.DMA((3,)),
        ],
        compiler_params=PACK_PARAMS,
        name="pack_near",
    )(target, meta, loads)
    from_chip = lax.ppermute(to_chip, "sub", next_chip)
    from_core = lax.ppermute(to_core, "sub", same_chip)

    mixer_shape = shape((3 * TYPES * TILE, TILE), BF16)
    kept, kept_meta, mixer = pl.pallas_call(
        functools.partial(prepare_kernel, slots),
        out_shape=(shape((rows, width), F32), shape((rows, META), F32), mixer_shape),
        in_specs=[VMEM] * 3,
        out_specs=(VMEM,) * 3,
        compiler_params=PARAMS,
        cost_estimate=pl.CostEstimate(
            flops=4_000_000_000, bytes_accessed=4_000_000, transcendentals=0
        ),
        name="prepare",
    )(loads, meta, ref_blocks)

    border = shape((edge, width + META), F32)
    pair = shape((2, tiles, rows, TILE), BF16)
    geo, field, geo_meta, to_core, to_chip = pl.pallas_call(
        functools.partial(arrange_kernel, slots),
        out_shape=(pair, pair, shape((rows, META), F32), border, border),
        in_specs=[SMEM] + [VMEM] * 5,
        out_specs=(VMEM,) * 5,
        compiler_params=PARAMS,
        name="arrange",
    )(position, kept, kept_meta, from_core, from_chip, from_far)

    halo_chip = lax.ppermute(to_chip, "sub", next_chip)
    halo_core = lax.ppermute(to_core, "sub", same_chip)

    basis_shape = shape((ITERS, 2, tiles, rows, TILE), BF16)
    inner, weights = pl.pallas_call(
        functools.partial(interior_kernel, slots),
        out_shape=(basis_shape, shape((2, TYPES, edge, 3 * TILE), BF16)),
        in_specs=[VMEM] * 4,
        out_specs=(VMEM,) * 2,
        scratch_shapes=[
            pltpu.VMEM((TYPES, rows - 2 * HALO, 3 * TILE), BF16),
            pltpu.VMEM((2, TYPES, tiles * (rows - 2 * HALO), TILE), BF16),
        ],
        compiler_params=PARAMS,
        cost_estimate=pl.CostEstimate(
            flops=10_000_000_000, bytes_accessed=8_000_000, transcendentals=0
        ),
        name="interior",
    )(field, geo_meta, mixer, ref_blocks)

    basis, moments = pl.pallas_call(
        functools.partial(sides_kernel, slots),
        out_shape=(basis_shape, shape((cases, META), F32)),
        in_specs=[SMEM] + [VMEM] * 8,
        out_specs=(VMEM,) * 2,
        scratch_shapes=[
            pltpu.VMEM((ITERS + 1, 2, 2, tiles, edge, TILE), BF16),
            pltpu.VMEM((2, edge, META), F32),
            pltpu.VMEM((2, TYPES, edge - HALO, 3 * TILE), BF16),
            pltpu.VMEM((2, TYPES, 2 * tiles * edge, TILE), BF16),
        ],
        compiler_params=PARAMS,
        name="sides",
    )(position, halo_core, halo_chip, field, inner, weights, mixer, ref_blocks, geo)

    moments = lax.all_gather(moments, "sub")

    return pl.pallas_call(
        functools.partial(finish_kernel, slots),
        out_shape=(shape((rows, width), F32), shape((rows, width), F32)),
        in_specs=[VMEM] * 4,
        out_specs=(VMEM,) * 2,
        compiler_params=PARAMS,
        name="finish",
    )(moments, ref_blocks, geo, basis)


def solution(mesh):
    placed = (
        P(("groups", "sub"), None),
        P(("groups", "sub")),
        P(("groups", "sub"), None),
        P(("groups", "sub"), None),
        P(("groups", "sub"), None),
        P(),
    )
    return jax.shard_map(
        on_device,
        mesh=mesh,
        in_specs=placed,
        out_specs=(P(("groups", "sub"), None), P(("groups", "sub"), None)),
        check_vma=False,
    )
```

```python
import functools

import jax
import jax.numpy as jnp
from jax import lax
from jax.experimental import pallas as pl
from jax.experimental.pallas import tpu as pltpu
from jax.sharding import PartitionSpec as P

HALO = 32
TYPES = 3
ITERS = 3
MASS_SHIFT = 0.5
META = 128
TILE = 256

F32 = jnp.float32
BF16 = jnp.bfloat16
VMEM = pl.BlockSpec(memory_space=pltpu.VMEM)
SMEM = pl.BlockSpec(memory_space=pltpu.SMEM)
HBM = pl.BlockSpec(memory_space=pltpu.HBM)
PARAMS = pltpu.CompilerParams(vmem_limit_bytes=40 * 1024 * 1024)


def dot(left, right):
    return jnp.dot(left, right, preferred_element_type=F32)


def dot_nt(left, right):
    return lax.dot_general(left, right, (((1,), (1,)), ((), ())), preferred_element_type=F32)


def dot_tn(left, right):
    return lax.dot_general(left, right, (((0,), (0,)), ((), ())), preferred_element_type=F32)


def halves(value):
    high = value.astype(BF16)
    return high, (value - high.astype(F32)).astype(BF16)


def iota(shape, axis):
    return lax.broadcasted_iota(jnp.int32, shape, axis)


def one_hot(condition):
    return jnp.where(condition, 1.0, 0.0).astype(BF16)


PACK_PARAMS = pltpu.CompilerParams(vmem_limit_bytes=62 * 1024 * 1024)


def basis_shift(blocks, slots):
    dof = blocks.shape[1]
    same = iota((dof, dof), 0) == iota((dof, dof), 1)
    total = sum(jnp.where(same, blocks[t], 0.0) for t in range(TYPES))
    mean = jnp.sum(jnp.sum(total, axis=1, keepdims=True), axis=0, keepdims=True) / (TYPES * dof)
    return MASS_SHIFT + 0.2 * slots * mean


def swap_blocks(piece):
    lane = iota(piece(0, 0).shape, 1)
    low = lane < META // 2
    out = []
    for tile in range(4):
        for part in range(2):
            first, second = piece(2 * part, tile // 2), piece(2 * part + 1, tile // 2)
            if tile % 2 == 0:
                second = pltpu.roll(second, META // 2, 1)
            else:
                first = pltpu.roll(first, META // 2, 1)
            out.append(jnp.where(low, first, second))
    return out


def given_to_gram():
    source, target = iota((TILE, TILE), 0), iota((TILE, TILE), 1)
    return one_hot((target // 16 == source % 16) & (target % 16 == source // 16))


def peers(pos, devices):
    odd = lax.rem(pos, jnp.int32(2))
    return (
        pos + 1 - 2 * odd,
        pos - 1 + 2 * odd,
        lax.rem(pos + devices // 2, jnp.int32(devices)),
    )


def targets(pos, ids, rows, devices):
    cap = rows // 4
    owner = lax.div(ids, jnp.int32(rows))
    goes = []
    for peer in peers(pos, devices):
        here = owner == peer
        for other in goes:
            here = here & ~other
        goes.append(here)
    flags = jnp.concatenate(
        [jnp.where(g, 1.0, 0.0) for g in goes] + [jnp.zeros((5, rows), F32)], axis=0
    )
    before = one_hot(iota((rows, rows), 0) < iota((rows, rows), 1))
    rank = dot(flags.astype(BF16), before).astype(jnp.int32)
    target = jnp.full((1, rows), -1, jnp.int32)
    for side in range(3):
        target = jnp.where(goes[side], rank[side:side + 1] + side * cap, target)
    return target


def fill_block(pick, loads, meta, out_ref):
    width = loads.shape[1]
    cap = pick.shape[0]
    twice = jnp.concatenate([pick, pick], axis=1)
    notes = dot_nt(twice, jnp.concatenate(halves(meta), axis=1))
    body = dot(twice, jnp.concatenate(halves(loads), axis=0))
    parts = width // META
    for part in range(parts):
        out_ref[part * cap:(part + 1) * cap, :] = body[:, part * META:(part + 1) * META]
    out_ref[parts * cap:, :] = notes[:cap // 2] + pltpu.roll(notes[cap // 2:], META // 2, 1)


def read_block(ref, width):
    parts = width // META
    cap = ref.shape[0] * 2 // (2 * parts + 1)
    body = jnp.concatenate([ref[part * cap:(part + 1) * cap, :] for part in range(parts)], axis=1)
    notes = ref[parts * cap:, :]
    notes = jnp.concatenate([notes, pltpu.roll(notes, META // 2, 1)], axis=0)
    return body, jnp.where(iota(notes.shape, 1) < META // 2, notes, 0.0)


def pack_far_kernel(devices, pos_ref, loads_hbm, rows_hbm, dens_hbm, cols_hbm, types_hbm,
                    far_ref, meta_ref, target_ref,
                    loads_ref, rows_ref, dens_ref, cols_ref, types_ref, sems):
    pairs = (
        (rows_hbm, rows_ref), (dens_hbm, dens_ref), (cols_hbm, cols_ref),
        (types_hbm, types_ref), (loads_hbm, loads_ref),
    )
    copies = [
        pltpu.make_async_copy(source, target, sems.at[number])
        for number, (source, target) in enumerate(pairs)
    ]
    for copy in copies:
        copy.start()
    for copy in copies[:4]:
        copy.wait()
    rows = loads_ref.shape[0]
    slots = dens_ref.shape[0]
    cap = rows // 4
    pos = pos_ref[0, 0]
    ids = rows_ref[...]
    owner = lax.div(ids, jnp.int32(rows))
    local = (ids - owner * rows + 1).astype(F32)
    target = targets(pos, ids, rows, devices)
    target_ref[...] = jnp.broadcast_to(target, target_ref.shape)

    density = dens_ref[...]
    kinds = types_ref[...]
    for kind in range(TYPES):
        meta_ref[kind * slots:(kind + 1) * slots, :] = jnp.where(kinds == kind, density, 0.0)
    meta_ref[3 * slots:4 * slots, :] = (cols_ref[...] - ids).astype(F32)
    meta_ref[4 * slots:, :] = jnp.zeros((META - 4 * slots, rows), F32)
    meta_ref[4 * slots:4 * slots + 1, :] = local
    meta_ref[4 * slots + 1:4 * slots + 2, :] = jnp.where(owner == pos, local, 0.0)

    copies[4].wait()
    pick = one_hot(iota((cap, rows), 0) + 2 * cap == target)
    fill_block(pick, loads_ref[...], meta_ref[...], far_ref)


def pack_near_kernel(target_hbm, meta_hbm, loads_hbm, core_ref, chip_ref,
                     target_ref, meta_ref, loads_ref, sems):
    pairs = ((target_hbm, target_ref), (meta_hbm, meta_ref), (loads_hbm, loads_ref))
    copies = [
        pltpu.make_async_copy(source, target, sems.at[number])
        for number, (source, target) in enumerate(pairs)
    ]
    for copy in copies:
        copy.start()
    for copy in copies:
        copy.wait()
    rows = loads_ref.shape[0]
    cap = rows // 4
    for side, out_ref in enumerate((core_ref, chip_ref)):
        pick = one_hot(iota((cap, rows), 0) + side * cap == target_ref[0:1, :])
        fill_block(pick, loads_ref[...], meta_ref[...], out_ref)


def reorder(parts, tiles):
    count = parts[0].shape[0]
    tall = [p[:, t * TILE:(t + 1) * TILE] for t in range(tiles) for p in parts]
    moved = dot(jnp.concatenate(tall, axis=0), given_to_gram()).astype(BF16)
    return [
        jnp.concatenate(
            [moved[(2 * t + p) * count:(2 * t + p + 1) * count] for t in range(tiles)], axis=1
        )
        for p in range(2)
    ]


def stacked_tiles(value, tiles):
    return jnp.concatenate([value[:, t * TILE:(t + 1) * TILE] for t in range(tiles)], axis=0)


def folded_rows(gram, cases):
    same_dof = iota((TILE, TILE), 0) % 16 == iota((TILE, TILE), 1) % 16
    gram = jnp.where(same_dof, gram, 0.0)
    return jnp.sum(gram.reshape(cases, TILE // cases, TILE), axis=1)


def prepare_kernel(slots, loads_ref, meta_ref, blocks_ref,
                   kept_ref, kept_meta_ref, mixer_ref, first_ref):
    rows, width = loads_ref.shape
    dof = blocks_ref.shape[1]
    tiles = width // TILE
    place = iota((rows, rows), 0) + 1
    own = one_hot(place == meta_ref[4 * slots + 1:4 * slots + 2, :].astype(jnp.int32))
    twice = jnp.concatenate([own, own], axis=1)
    moved = reorder(halves(loads_ref[...]), tiles)
    kept_ref[...] = dot(twice, jnp.concatenate(moved, axis=0))
    high, low = (stacked_tiles(part, tiles) for part in moved)
    gram = dot_tn(high, jnp.concatenate([high, low], axis=1))
    cross = gram[:, TILE:]
    first_ref[...] = folded_rows(gram[:, :TILE] + cross + cross.T, width // dof)
    kept_meta_ref[...] = dot_nt(twice, jnp.concatenate(halves(meta_ref[...]), axis=1))

    def dof_of(lane):
        return lane // 64 * 16 + lane % 16

    fold = one_hot(dof_of(iota((TILE, dof), 0)) == iota((TILE, dof), 1))
    unfold = one_hot(dof_of(iota((dof, TILE), 1)) == iota((dof, TILE), 0))
    same_case = iota((TILE, TILE), 0) // 16 % 4 == iota((TILE, TILE), 1) // 16 % 4
    for kind in range(TYPES):
        for copies, part in zip(((0, 2), (1,)), halves(blocks_ref[kind])):
            wide = dot(dot_nt(fold, part).astype(BF16), unfold)
            wide = jnp.where(same_case, wide, 0.0).astype(BF16)
            for copy in copies:
                start = (copy * TYPES + kind) * TILE
                mixer_ref[start:start + TILE, :] = wide


def arrange_kernel(slots, pos_ref, kept_ref, kept_meta_ref, core_ref, chip_ref, far_ref,
                   geo_ref, field_ref, meta_ref, to_core_ref, to_chip_ref):
    rows, width = kept_ref.shape
    tiles = width // TILE
    edge = to_core_ref.shape[0]
    even = lax.rem(pos_ref[0, 0], jnp.int32(2)) == 0
    blocks = [read_block(ref, width) for ref in (core_ref, chip_ref, far_ref)]
    arrived = jnp.concatenate([block[0] for block in blocks], axis=0)
    arrived_meta = jnp.concatenate([block[1] for block in blocks], axis=0)
    count = arrived.shape[0]
    unit = one_hot(iota((8, META), 1) == 4 * slots)
    tags = dot_nt(unit, arrived_meta.astype(BF16))[0:1]
    other = one_hot(iota((rows, count), 0) + 1 == tags.astype(jnp.int32))
    twice = jnp.concatenate([other, other], axis=1)
    moved = reorder(halves(arrived), tiles)
    geo = kept_ref[...] + dot(twice, jnp.concatenate(moved, axis=0))
    meta = kept_meta_ref[...] + dot(twice, jnp.concatenate(halves(arrived_meta), axis=0))
    meta_ref[...] = meta

    def send(lanes, value):
        head, tail = value[:edge], value[rows - edge:]
        to_core_ref[:, lanes] = jnp.where(even, tail, head)
        to_chip_ref[:, lanes] = jnp.where(even, head, tail)

    send(slice(width, None), meta)

    def piece(tile, part):
        start = tile * TILE + part * META
        return geo[:, start:start + META]

    for number, value in enumerate(swap_blocks(piece)):
        lanes = slice(number * META, (number + 1) * META)
        send(lanes, value)
        inner = slice(number % 2 * META, (number % 2 + 1) * META)
        for part, half in enumerate(halves(value)):
            field_ref[part, number // 2, :, inner] = half
    for part, half in enumerate(halves(geo)):
        for tile in range(tiles):
            geo_ref[part, tile] = half[:, tile * TILE:(tile + 1) * TILE]


def stencil_rows(meta, slots, first):
    lane = iota((HALO, META), 1)
    spot = iota((HALO, TILE), 1)
    centre = iota((HALO, 1), 0) + first
    sums = [jnp.zeros((HALO, TILE), F32) for _ in range(TYPES)]
    for slot in range(slots):
        column = centre + meta[:, 3 * slots + slot:3 * slots + slot + 1].astype(jnp.int32)
        hit = spot == column
        for kind in range(TYPES):
            weight = meta[:, kind * slots + slot:kind * slots + slot + 1]
            sums[kind] += jnp.where(hit, weight, 0.0)
    out = []
    for kind in range(TYPES):
        inside = (lane >= kind * slots) & (lane < (kind + 1) * slots)
        total = jnp.sum(jnp.where(inside, meta, 0.0), axis=1, keepdims=True)
        high, low = halves(jnp.where(spot == centre, total, 0.0) - sums[kind])
        out.append(jnp.concatenate([high, high, low], axis=1))
    return out


def gathered(weights, near, fine):
    return halves(dot(weights, jnp.concatenate([near, fine, near], axis=0)))


def mixed(buckets, mixer_ref, count):
    highs = [buckets[0, kind, :count, :] for kind in range(TYPES)]
    lows = [buckets[1, kind, :count, :] for kind in range(TYPES)]
    return dot(jnp.concatenate(highs + highs + lows, axis=1), mixer_ref[...])


def interior_kernel(slots, field_ref, meta_ref, mixer_ref, blocks_ref,
                    inner_ref, weights_ref, stencil, buckets):
    tiles, rows = field_ref.shape[1:3]
    edge = ITERS * HALO
    shift = basis_shift(blocks_ref[...], slots)
    inside = rows - 2 * HALO

    def build(chunk, carry):
        first = pl.multiple_of(chunk * HALO, HALO)
        start = pl.multiple_of(chunk * HALO + HALO, HALO)
        for kind, value in enumerate(
            stencil_rows(meta_ref[pl.ds(start, HALO), :], slots, first + HALO)
        ):
            stencil[kind, pl.ds(first, HALO), :] = value
        return carry

    lax.fori_loop(0, inside // HALO, build, 0)

    def build_outer(chunk, carry):
        side = lax.div(chunk, jnp.int32(ITERS))
        first = pl.multiple_of(lax.rem(chunk, jnp.int32(ITERS)) * HALO, HALO)
        start = pl.multiple_of(first + side * (rows - edge), HALO)
        spot = jnp.where(side == 0, first + edge, first + rows - 2 * edge)
        for kind, value in enumerate(stencil_rows(meta_ref[pl.ds(start, HALO), :], slots, spot)):
            weights_ref[side, kind, pl.ds(first, HALO), :] = value
        return carry

    lax.fori_loop(0, 2 * ITERS, build_outer, 0)

    for step in range(ITERS - 1):
        begin = HALO * (step + 1)
        blank = jnp.zeros((begin, TILE), BF16)
        for part in range(2):
            for tile in range(tiles):
                inner_ref[step, part, tile, :begin, :] = blank
                inner_ref[step, part, tile, rows - begin:, :] = blank
    for step in range(ITERS):
        skip = HALO * step
        count = inside - 2 * skip
        begin = HALO + skip
        weights = jnp.concatenate(
            [stencil[kind, skip:inside - skip, :] for kind in range(TYPES)], axis=0
        )

        def read(part, tile, block):
            if step == 0:
                return field_ref[part, tile, block, :]
            return inner_ref[step - 1, part, tile, block, :]

        for tile in range(tiles):
            every = slice(0, rows)
            for part, half in enumerate(
                gathered(weights, read(0, tile, every), read(1, tile, every))
            ):
                for kind in range(TYPES):
                    buckets[part, kind, tile * count:(tile + 1) * count, :] = (
                        half[kind * count:(kind + 1) * count]
                    )
        applied = mixed(buckets, mixer_ref, tiles * count)
        block = slice(begin, begin + count)
        for tile in range(tiles):
            here = read(0, tile, block).astype(F32) + read(1, tile, block).astype(F32)
            value = applied[tile * count:(tile + 1) * count] + (MASS_SHIFT - shift) * here
            for part, half in enumerate(halves(value)):
                inner_ref[step, part, tile, block, :] = half


def sides_kernel(slots, pos_ref, core_ref, chip_ref, field_ref, inner_ref, weights_ref, mixer_ref,
                 blocks_ref, geo_ref, first_ref, basis_ref, moments_ref, v_refs, meta_refs, stencil, buckets):
    tiles, rows = field_ref.shape[1:3]
    width = tiles * TILE
    dof = blocks_ref.shape[1]
    cases = width // dof
    edge = ITERS * HALO
    outer = edge - HALO
    count = edge
    rest = TILE - edge
    shift = basis_shift(blocks_ref[...], slots)
    even = lax.rem(pos_ref[0, 0], jnp.int32(2)) == 0

    for tile in range(tiles + 1):
        lanes = slice(tile * TILE, (tile + 1) * TILE) if tile < tiles else slice(width, None)
        core, chip = core_ref[:, lanes], chip_ref[:, lanes]
        for side, value in enumerate((jnp.where(even, chip, core), jnp.where(even, core, chip))):
            if tile == tiles:
                meta_refs[side] = value
            else:
                for part, half in enumerate(halves(value)):
                    v_refs[0, side, part, tile] = half

    def build(chunk, carry):
        side = lax.div(chunk, jnp.int32(2))
        first = pl.multiple_of(lax.rem(chunk, jnp.int32(2)) * HALO, HALO)
        start = pl.multiple_of(first + HALO * (1 - side), HALO)
        spot = jnp.where(side == 0, first + HALO, first + rows - edge)
        for kind, value in enumerate(
            stencil_rows(meta_refs[side, pl.ds(start, HALO), :], slots, spot)
        ):
            stencil[side, kind, pl.ds(first, HALO), :] = value
        return carry

    lax.fori_loop(0, 4, build, 0)

    def window(step, side, part, tile):
        near = v_refs[step, side, part, tile]
        if step == 0:
            if side == 0:
                return jnp.concatenate([near, field_ref[part, tile, :rest, :]], axis=0)
            return jnp.concatenate([field_ref[part, tile, rows - rest:, :], near], axis=0)
        blank = jnp.zeros((HALO * step, TILE), BF16)
        begin = HALO * step
        if side == 0:
            far = inner_ref[step - 1, part, tile, begin:rest, :]
            return jnp.concatenate([blank, near, far], axis=0)
        far = inner_ref[step - 1, part, tile, rows - rest:rows - begin, :]
        return jnp.concatenate([far, near, blank], axis=0)

    def weight_rows(step, side, kind):
        keep = outer - HALO * step
        if side == 0:
            pieces = [weights_ref[0, kind, :count - keep, :]]
            if keep:
                pieces.insert(0, stencil[0, kind, outer - keep:, :])
        else:
            pieces = [weights_ref[1, kind, keep:, :]]
            if keep:
                pieces.append(stencil[1, kind, :keep, :])
        return jnp.concatenate(pieces, axis=0)

    for step in range(ITERS):
        centres = []
        for side in range(2):
            weights = jnp.concatenate(
                [weight_rows(step, side, kind) for kind in range(TYPES)], axis=0
            )
            for tile in range(tiles):
                row = (side * tiles + tile) * count
                near, fine = (window(step, side, part, tile) for part in range(2))
                first = HALO * (step + 1) if side == 0 else TILE - HALO * (step + 1) - count
                centres.append((near[first:first + count], fine[first:first + count]))
                for part, half in enumerate(gathered(weights, near, fine)):
                    for kind in range(TYPES):
                        buckets[part, kind, row:row + count, :] = (
                            half[kind * count:(kind + 1) * count]
                        )
        applied = mixed(buckets, mixer_ref, 2 * tiles * count)
        for side in range(2):
            for tile in range(tiles):
                number = side * tiles + tile
                near, fine = centres[number]
                here = near.astype(F32) + fine.astype(F32)
                value = applied[number * count:(number + 1) * count] + (MASS_SHIFT - shift) * here
                for part, half in enumerate(halves(value)):
                    v_refs[step + 1, side, part, tile] = half

    for step in range(1, ITERS + 1):
        begin = HALO * step

        def piece(tile, part):
            lanes = slice(part * META, (part + 1) * META)
            high, low = (
                jnp.concatenate(
                    [
                        v_refs[step, 0, half, tile, count - begin:, lanes],
                        inner_ref[step - 1, half, tile, begin:rows - begin, lanes],
                        v_refs[step, 1, half, tile, :begin, lanes],
                    ],
                    axis=0,
                )
                for half in range(2)
            )
            return high.astype(F32) + low.astype(F32)

        for number, value in enumerate(swap_blocks(piece)):
            lanes = slice(number % 2 * META, (number % 2 + 1) * META)
            for part, half in enumerate(halves(value)):
                basis_ref[step - 1, part, number // 2, :, lanes] = half

    def tall(step, part):
        if step == 0:
            return jnp.concatenate([geo_ref[part, tile] for tile in range(tiles)], axis=0)
        return jnp.concatenate([basis_ref[step - 1, part, tile] for tile in range(tiles)], axis=0)

    sums = [first_ref[...]]
    for step in range(ITERS):
        others = [tall(step + 1, 0), tall(step + 1, 1)]
        if step > 0:
            others += [tall(step, 0), tall(step, 1)]
        high = dot_tn(tall(step, 0), jnp.concatenate(others, axis=1))
        if step > 0:
            cross = high[:, 3 * TILE:]
            sums.append(folded_rows(high[:, 2 * TILE:3 * TILE] + cross + cross.T, cases))
        low = dot_tn(tall(step, 1), tall(step + 1, 0))
        sums.append(folded_rows(high[:, :TILE] + high[:, TILE:2 * TILE] + low, cases))
    remainder = jnp.concatenate(sums, axis=0)
    pieces = []
    for _ in range(3):
        pieces.append(remainder.astype(BF16))
        remainder = remainder - pieces[-1].astype(F32)
    collect = one_hot(iota((TILE, META), 0) // 16 == iota((TILE, META), 1) % 16)
    folded = dot(jnp.concatenate(pieces, axis=1), jnp.concatenate([collect] * 3, axis=0))
    group = iota((cases, META), 1) // cases
    moments = jnp.zeros((cases, META), F32)
    for number in range(2 * ITERS):
        part = folded[number * cases:(number + 1) * cases]
        moments = jnp.where(group == number, part, moments)
    moments_ref[...] = moments


def refined_reciprocal(value):
    guess = pl.reciprocal(value, approx=True)
    for _ in range(2):
        guess = guess * (2.0 - value * guess)
    return guess


def finish_kernel(slots, blocks_ref, geo_ref, basis_ref, *refs):
    moment_refs = refs[:-4]
    solution_hbm, residual_hbm, out_refs, sems = refs[-4:]
    rows, width = out_refs.shape[1:]
    dof = blocks_ref.shape[1]
    cases = width // dof
    tiles = width // TILE
    shift = basis_shift(blocks_ref[...], slots)
    moments = moment_refs[0][...]
    for ref in moment_refs[1:]:
        moments = moments + ref[...]
    group = iota((cases, META), 1) // cases
    system = []
    for row in range(ITERS):
        plain = moments if row == 0 else pltpu.roll(moments, META - cases * row, 1)
        ahead = pltpu.roll(moments, META - cases * (row + 1), 1)
        target = pltpu.roll(moments, cases * (ITERS - row), 1)
        system.append(jnp.where(group < ITERS, ahead + shift * plain, target))
    system = jnp.concatenate(system, axis=0)
    size = ITERS * cases
    index = iota((size, 1), 0)
    for pivot in range(0, size, 2):
        column_a = jnp.broadcast_to(system[:, pivot:pivot + 1], (size, META))
        column_b = jnp.broadcast_to(system[:, pivot + 1:pivot + 2], (size, META))
        line_a = system[pivot:pivot + 1, :]
        line_b = system[pivot + 1:pivot + 2, :]
        above = column_b[pivot:pivot + 1, :]
        inverse = refined_reciprocal(column_a[pivot:pivot + 1, :])
        factor = column_a[pivot + 1:pivot + 2, :] * inverse
        corner = column_b[pivot + 1:pivot + 2, :] - factor * above
        line_b = (line_b - factor * line_a) * refined_reciprocal(corner)
        line_a = (line_a - above * line_b) * inverse
        update = system - column_a * line_a - column_b * line_b
        system = jnp.where(index == pivot, line_a, jnp.where(index == pivot + 1, line_b, update))

    unit = jnp.where(iota((cases, META), 1) % cases == iota((cases, META), 0), 1.0, 0.0)
    answers = []
    for row in range(ITERS):
        part = jnp.where(group == ITERS, system[row * cases:(row + 1) * cases], 0.0)
        step = cases
        while step < META:
            part = part + pltpu.roll(part, step, 1)
            step *= 2
        answers.append(part)
    left_over = [unit - shift * answers[0]]
    for row in range(1, ITERS):
        left_over.append(-(answers[row - 1] + shift * answers[row]))
    left_over.append(-answers[ITERS - 1])

    meets = iota((TILE, TILE), 0) % 16 == iota((TILE, TILE), 1) // 16

    def spread(parts):
        highs, lows = [], []
        for part in parts:
            tall = jnp.broadcast_to(part[:, None, :], (cases, TILE // cases, META))
            tall = tall.reshape(TILE, META)
            wide = jnp.concatenate([tall] * (TILE // META), axis=1)
            high, low = halves(jnp.where(meets, wide, 0.0))
            highs.append(high)
            lows.append(low)
        return jnp.concatenate(highs + highs + lows, axis=0)

    def tall(term, part):
        if term == 0:
            return jnp.concatenate([geo_ref[part, tile] for tile in range(tiles)], axis=0)
        return jnp.concatenate([basis_ref[term - 1, part, tile] for tile in range(tiles)], axis=0)

    copies = []
    for number, (out_hbm, parts) in enumerate(
        ((solution_hbm, answers), (residual_hbm, left_over))
    ):
        matrix = spread(parts)
        terms = matrix.shape[0] // (3 * TILE)
        highs = [tall(term, 0) for term in range(terms)]
        lows = [tall(term, 1) for term in range(terms)]
        value = dot(jnp.concatenate(highs + lows + highs, axis=1), matrix)
        for tile in range(tiles):
            lanes = slice(tile * TILE, (tile + 1) * TILE)
            out_refs[number, :, lanes] = value[tile * rows:(tile + 1) * rows]
        copies.append(pltpu.make_async_copy(out_refs.at[number], out_hbm, sems.at[number]))
        copies[number].start()
    for copy in copies:
        copy.wait()


def on_device(loads, row_ids, densities, block_cols, block_types, ref_blocks):
    rows, width = loads.shape
    slots = densities.shape[1]
    cases = width // ref_blocks.shape[1]
    cap = rows // 4
    edge = ITERS * HALO
    tiles = width // TILE
    devices = lax.axis_size("sub")
    position = lax.axis_index("sub").astype(jnp.int32).reshape(1, 1)
    shape = jax.ShapeDtypeStruct
    same_chip = [(i, i ^ 1) for i in range(devices)]
    next_chip = [(i, i + 1) for i in range(1, devices - 1, 2)]
    next_chip += [(i + 1, i) for i in range(1, devices - 1, 2)]
    across = [(i, (i + devices // 2) % devices) for i in range(devices)]

    block = shape((cap * width // META + cap // 2, META), F32)
    to_far, meta, target = pl.pallas_call(
        functools.partial(pack_far_kernel, devices),
        out_shape=(block, shape((META, rows), F32), shape((8, rows), jnp.int32)),
        in_specs=[SMEM] + [HBM] * 5,
        out_specs=(VMEM,) * 3,
        scratch_shapes=[
            pltpu.VMEM((rows, width), F32),
            pltpu.VMEM((1, rows), jnp.int32),
            pltpu.VMEM((slots, rows), F32),
            pltpu.VMEM((slots, rows), jnp.int32),
            pltpu.VMEM((slots, rows), jnp.int32),
            pltpu.SemaphoreType.DMA((5,)),
        ],
        compiler_params=PACK_PARAMS,
        name="pack_far",
    )(position, loads, row_ids.reshape(1, rows), densities.T, block_cols.T, block_types.T)
    from_far = lax.ppermute(to_far, "sub", across)

    to_core, to_chip = pl.pallas_call(
        pack_near_kernel,
        out_shape=(block, block),
        in_specs=[HBM] * 3,
        out_specs=(VMEM,) * 2,
        scratch_shapes=[
            pltpu.VMEM((8, rows), jnp.int32),
            pltpu.VMEM((META, rows), F32),
            pltpu.VMEM((rows, width), F32),
            pltpu.SemaphoreType.DMA((3,)),
        ],
        compiler_params=PACK_PARAMS,
        name="pack_near",
    )(target, meta, loads)
    from_chip = lax.ppermute(to_chip, "sub", next_chip)
    from_core = lax.ppermute(to_core, "sub", same_chip)

    mixer_shape = shape((3 * TYPES * TILE, TILE), BF16)
    kept, kept_meta, mixer, first = pl.pallas_call(
        functools.partial(prepare_kernel, slots),
        out_shape=(
            shape((rows, width), F32),
            shape((rows, META), F32),
            mixer_shape,
            shape((cases, TILE), F32),
        ),
        in_specs=[VMEM] * 3,
        out_specs=(VMEM,) * 4,
        compiler_params=PARAMS,
        cost_estimate=pl.CostEstimate(
            flops=4_000_000_000, bytes_accessed=4_000_000, transcendentals=0
        ),
        name="prepare",
    )(loads, meta, ref_blocks)

    border = shape((edge, width + META), F32)
    pair = shape((2, tiles, rows, TILE), BF16)
    geo, field, geo_meta, to_core, to_chip = pl.pallas_call(
        functools.partial(arrange_kernel, slots),
        out_shape=(pair, pair, shape((rows, META), F32), border, border),
        in_specs=[SMEM] + [VMEM] * 5,
        out_specs=(VMEM,) * 5,
        compiler_params=PARAMS,
        name="arrange",
    )(position, kept, kept_meta, from_core, from_chip, from_far)

    halo_chip = lax.ppermute(to_chip, "sub", next_chip)
    halo_core = lax.ppermute(to_core, "sub", same_chip)

    basis_shape = shape((ITERS, 2, tiles, rows, TILE), BF16)
    inner, weights = pl.pallas_call(
        functools.partial(interior_kernel, slots),
        out_shape=(basis_shape, shape((2, TYPES, edge, 3 * TILE), BF16)),
        in_specs=[VMEM] * 4,
        out_specs=(VMEM,) * 2,
        scratch_shapes=[
            pltpu.VMEM((TYPES, rows - 2 * HALO, 3 * TILE), BF16),
            pltpu.VMEM((2, TYPES, tiles * (rows - 2 * HALO), TILE), BF16),
        ],
        compiler_params=PARAMS,
        cost_estimate=pl.CostEstimate(
            flops=10_000_000_000, bytes_accessed=8_000_000, transcendentals=0
        ),
        name="interior",
    )(field, geo_meta, mixer, ref_blocks)

    basis, moments = pl.pallas_call(
        functools.partial(sides_kernel, slots),
        out_shape=(basis_shape, shape((cases, META), F32)),
        in_specs=[SMEM] + [VMEM] * 9,
        out_specs=(VMEM,) * 2,
        scratch_shapes=[
            pltpu.VMEM((ITERS + 1, 2, 2, tiles, edge, TILE), BF16),
            pltpu.VMEM((2, edge, META), F32),
            pltpu.VMEM((2, TYPES, edge - HALO, 3 * TILE), BF16),
            pltpu.VMEM((2, TYPES, 2 * tiles * edge, TILE), BF16),
        ],
        compiler_params=PARAMS,
        name="sides",
    )(position, halo_core, halo_chip, field, inner, weights, mixer, ref_blocks, geo, first)

    bits = devices.bit_length() - 1
    gathered_moments = [moments]
    for low, high in ((0, bits // 2), (bits // 2, bits)):
        partial = sum(gathered_moments[1:], gathered_moments[0])
        gathered_moments = [partial]
        for mask in range(1, 1 << (high - low)):
            swap = [(i, i ^ (mask << low)) for i in range(devices)]
            gathered_moments.append(lax.ppermute(partial, "sub", swap))

    return pl.pallas_call(
        functools.partial(finish_kernel, slots),
        out_shape=(shape((rows, width), F32), shape((rows, width), F32)),
        in_specs=[VMEM] * (3 + len(gathered_moments)),
        out_specs=(HBM,) * 2,
        scratch_shapes=[pltpu.VMEM((2, rows, width), F32), pltpu.SemaphoreType.DMA((2,))],
        compiler_params=PARAMS,
        name="finish",
    )(ref_blocks, geo, basis, *gathered_moments)


def solution(mesh):
    placed = (
        P(("groups", "sub"), None),
        P(("groups", "sub")),
        P(("groups", "sub"), None),
        P(("groups", "sub"), None),
        P(("groups", "sub"), None),
        P(),
    )
    return jax.shard_map(
        on_device,
        mesh=mesh,
        in_specs=placed,
        out_specs=(P(("groups", "sub"), None), P(("groups", "sub"), None)),
        check_vma=False,
    )
```

```python
import functools

import jax
import jax.numpy as jnp
from jax import lax
from jax.experimental import pallas as pl
from jax.experimental.pallas import tpu as pltpu
from jax.sharding import PartitionSpec as P

HALO = 32
TYPES = 3
ITERS = 3
MASS_SHIFT = 0.5
META = 128
TILE = 256

F32 = jnp.float32
BF16 = jnp.bfloat16
VMEM = pl.BlockSpec(memory_space=pltpu.VMEM)
SMEM = pl.BlockSpec(memory_space=pltpu.SMEM)
HBM = pl.BlockSpec(memory_space=pltpu.HBM)
PARAMS = pltpu.CompilerParams(vmem_limit_bytes=40 * 1024 * 1024)


def dot(left, right):
    return jnp.dot(left, right, preferred_element_type=F32)


def dot_nt(left, right):
    return lax.dot_general(left, right, (((1,), (1,)), ((), ())), preferred_element_type=F32)


def dot_tn(left, right):
    return lax.dot_general(left, right, (((0,), (0,)), ((), ())), preferred_element_type=F32)


def halves(value):
    high = value.astype(BF16)
    return high, (value - high.astype(F32)).astype(BF16)


def iota(shape, axis):
    return lax.broadcasted_iota(jnp.int32, shape, axis)


def one_hot(condition):
    return jnp.where(condition, 1.0, 0.0).astype(BF16)


PACK_PARAMS = pltpu.CompilerParams(vmem_limit_bytes=62 * 1024 * 1024)


def basis_shift(blocks, slots):
    dof = blocks.shape[1]
    same = iota((dof, dof), 0) == iota((dof, dof), 1)
    total = sum(jnp.where(same, blocks[t], 0.0) for t in range(TYPES))
    mean = jnp.sum(jnp.sum(total, axis=1, keepdims=True), axis=0, keepdims=True) / (TYPES * dof)
    return MASS_SHIFT + 0.2 * slots * mean


def swap_blocks(piece):
    lane = iota(piece(0, 0).shape, 1)
    low = lane < META // 2
    out = []
    for tile in range(4):
        for part in range(2):
            first, second = piece(2 * part, tile // 2), piece(2 * part + 1, tile // 2)
            if tile % 2 == 0:
                second = pltpu.roll(second, META // 2, 1)
            else:
                first = pltpu.roll(first, META // 2, 1)
            out.append(jnp.where(low, first, second))
    return out


def given_to_gram():
    source, target = iota((TILE, TILE), 0), iota((TILE, TILE), 1)
    return one_hot((target // 16 == source % 16) & (target % 16 == source // 16))


def peers(pos, devices):
    odd = lax.rem(pos, jnp.int32(2))
    return (
        pos + 1 - 2 * odd,
        pos - 1 + 2 * odd,
        lax.rem(pos + devices // 2, jnp.int32(devices)),
    )


def far_first(pos, devices):
    half = devices // 2
    group = (pos % half + 1) // 2 % max(half // 2, 1)
    return group % 2 == 1


def targets(pos, ids, rows, devices):
    cap = rows // 4
    owner = lax.div(ids, jnp.int32(rows))
    goes = []
    for peer in peers(pos, devices):
        here = owner == peer
        for other in goes:
            here = here & ~other
        goes.append(here)
    flags = jnp.concatenate(
        [jnp.where(g, 1.0, 0.0) for g in goes] + [jnp.zeros((5, rows), F32)], axis=0
    )
    before = one_hot(iota((rows, rows), 0) < iota((rows, rows), 1))
    rank = dot(flags.astype(BF16), before).astype(jnp.int32)
    target = jnp.full((1, rows), -1, jnp.int32)
    for side in range(3):
        target = jnp.where(goes[side], rank[side:side + 1] + side * cap, target)
    return target


def fill_block(pick, loads, meta, out_ref):
    width = loads.shape[1]
    cap = pick.shape[0]
    twice = jnp.concatenate([pick, pick], axis=1)
    notes = dot_nt(twice, jnp.concatenate(halves(meta), axis=1))
    body = dot(twice, jnp.concatenate(halves(loads), axis=0))
    parts = width // META
    for part in range(parts):
        out_ref[part * cap:(part + 1) * cap, :] = body[:, part * META:(part + 1) * META]
    out_ref[parts * cap:, :] = notes[:cap // 2] + pltpu.roll(notes[cap // 2:], META // 2, 1)


def read_block(ref, width):
    parts = width // META
    cap = ref.shape[0] * 2 // (2 * parts + 1)
    body = jnp.concatenate([ref[part * cap:(part + 1) * cap, :] for part in range(parts)], axis=1)
    notes = ref[parts * cap:, :]
    notes = jnp.concatenate([notes, pltpu.roll(notes, META // 2, 1)], axis=0)
    return body, jnp.where(iota(notes.shape, 1) < META // 2, notes, 0.0)


def pack_first_kernel(devices, pos_ref, loads_hbm, rows_hbm, dens_hbm, cols_hbm, types_hbm,
                      first_ref, meta_ref, target_ref,
                      loads_ref, rows_ref, dens_ref, cols_ref, types_ref, sems):
    pairs = (
        (rows_hbm, rows_ref), (dens_hbm, dens_ref), (cols_hbm, cols_ref),
        (types_hbm, types_ref), (loads_hbm, loads_ref),
    )
    copies = [
        pltpu.make_async_copy(source, target, sems.at[number])
        for number, (source, target) in enumerate(pairs)
    ]
    for copy in copies:
        copy.start()
    for copy in copies[:4]:
        copy.wait()
    rows = loads_ref.shape[0]
    slots = dens_ref.shape[0]
    cap = rows // 4
    pos = pos_ref[0, 0]
    ids = rows_ref[...]
    owner = lax.div(ids, jnp.int32(rows))
    local = (ids - owner * rows + 1).astype(F32)
    target = targets(pos, ids, rows, devices)
    target_ref[...] = jnp.broadcast_to(target, target_ref.shape)

    density = dens_ref[...]
    kinds = types_ref[...]
    for kind in range(TYPES):
        meta_ref[kind * slots:(kind + 1) * slots, :] = jnp.where(kinds == kind, density, 0.0)
    meta_ref[3 * slots:4 * slots, :] = (cols_ref[...] - ids).astype(F32)
    meta_ref[4 * slots:, :] = jnp.zeros((META - 4 * slots, rows), F32)
    meta_ref[4 * slots:4 * slots + 1, :] = local
    meta_ref[4 * slots + 1:4 * slots + 2, :] = jnp.where(owner == pos, local, 0.0)

    copies[4].wait()
    side = jnp.where(far_first(pos, devices), 2, 1)
    pick = one_hot(iota((cap, rows), 0) + side * cap == target)
    fill_block(pick, loads_ref[...], meta_ref[...], first_ref)


def pack_second_kernel(devices, pos_ref, target_hbm, meta_hbm, loads_hbm, core_ref, second_ref,
                       target_ref, meta_ref, loads_ref, sems):
    pairs = ((target_hbm, target_ref), (meta_hbm, meta_ref), (loads_hbm, loads_ref))
    copies = [
        pltpu.make_async_copy(source, target, sems.at[number])
        for number, (source, target) in enumerate(pairs)
    ]
    for copy in copies:
        copy.start()
    for copy in copies:
        copy.wait()
    rows = loads_ref.shape[0]
    cap = rows // 4
    late = jnp.where(far_first(pos_ref[0, 0], devices), 1, 2)
    for side, out_ref in ((late, second_ref), (0, core_ref)):
        pick = one_hot(iota((cap, rows), 0) + side * cap == target_ref[0:1, :])
        fill_block(pick, loads_ref[...], meta_ref[...], out_ref)


def reorder(parts, tiles):
    count = parts[0].shape[0]
    tall = [p[:, t * TILE:(t + 1) * TILE] for t in range(tiles) for p in parts]
    moved = dot(jnp.concatenate(tall, axis=0), given_to_gram()).astype(BF16)
    return [
        jnp.concatenate(
            [moved[(2 * t + p) * count:(2 * t + p + 1) * count] for t in range(tiles)], axis=1
        )
        for p in range(2)
    ]


def stacked_tiles(value, tiles):
    return jnp.concatenate([value[:, t * TILE:(t + 1) * TILE] for t in range(tiles)], axis=0)


def folded_rows(gram, cases):
    same_dof = iota((TILE, TILE), 0) % 16 == iota((TILE, TILE), 1) % 16
    gram = jnp.where(same_dof, gram, 0.0)
    return jnp.sum(gram.reshape(cases, TILE // cases, TILE), axis=1)


def prepare_kernel(slots, loads_ref, meta_ref, blocks_ref,
                   kept_ref, kept_meta_ref, mixer_ref, first_ref):
    rows, width = loads_ref.shape
    dof = blocks_ref.shape[1]
    tiles = width // TILE
    place = iota((rows, rows), 0) + 1
    own = one_hot(place == meta_ref[4 * slots + 1:4 * slots + 2, :].astype(jnp.int32))
    twice = jnp.concatenate([own, own], axis=1)
    moved = reorder(halves(loads_ref[...]), tiles)
    kept_ref[...] = dot(twice, jnp.concatenate(moved, axis=0))
    high, low = (stacked_tiles(part, tiles) for part in moved)
    gram = dot_tn(high, jnp.concatenate([high, low], axis=1))
    cross = gram[:, TILE:]
    first_ref[...] = folded_rows(gram[:, :TILE] + cross + cross.T, width // dof)
    kept_meta_ref[...] = dot_nt(twice, jnp.concatenate(halves(meta_ref[...]), axis=1))

    def dof_of(lane):
        return lane // 64 * 16 + lane % 16

    fold = one_hot(dof_of(iota((TILE, dof), 0)) == iota((TILE, dof), 1))
    unfold = one_hot(dof_of(iota((dof, TILE), 1)) == iota((dof, TILE), 0))
    same_case = iota((TILE, TILE), 0) // 16 % 4 == iota((TILE, TILE), 1) // 16 % 4
    for kind in range(TYPES):
        for copies, part in zip(((0, 2), (1,)), halves(blocks_ref[kind])):
            wide = dot(dot_nt(fold, part).astype(BF16), unfold)
            wide = jnp.where(same_case, wide, 0.0).astype(BF16)
            for copy in copies:
                start = (copy * TYPES + kind) * TILE
                mixer_ref[start:start + TILE, :] = wide


def arrange_kernel(slots, pos_ref, kept_ref, kept_meta_ref, core_ref, first_ref, second_ref,
                   geo_ref, field_ref, meta_ref, to_core_ref, to_chip_ref):
    rows, width = kept_ref.shape
    tiles = width // TILE
    edge = to_core_ref.shape[0]
    even = lax.rem(pos_ref[0, 0], jnp.int32(2)) == 0
    blocks = [read_block(ref, width) for ref in (core_ref, first_ref, second_ref)]
    arrived = jnp.concatenate([block[0] for block in blocks], axis=0)
    arrived_meta = jnp.concatenate([block[1] for block in blocks], axis=0)
    count = arrived.shape[0]
    unit = one_hot(iota((8, META), 1) == 4 * slots)
    tags = dot_nt(unit, arrived_meta.astype(BF16))[0:1]
    other = one_hot(iota((rows, count), 0) + 1 == tags.astype(jnp.int32))
    twice = jnp.concatenate([other, other], axis=1)
    moved = reorder(halves(arrived), tiles)
    geo = kept_ref[...] + dot(twice, jnp.concatenate(moved, axis=0))
    meta = kept_meta_ref[...] + dot(twice, jnp.concatenate(halves(arrived_meta), axis=0))
    meta_ref[...] = meta

    def send(lanes, value):
        head, tail = value[:edge], value[rows - edge:]
        to_core_ref[:, lanes] = jnp.where(even, tail, head)
        to_chip_ref[:, lanes] = jnp.where(even, head, tail)

    send(slice(width, None), meta)

    def piece(tile, part):
        start = tile * TILE + part * META
        return geo[:, start:start + META]

    for number, value in enumerate(swap_blocks(piece)):
        lanes = slice(number * META, (number + 1) * META)
        send(lanes, value)
        inner = slice(number % 2 * META, (number % 2 + 1) * META)
        for part, half in enumerate(halves(value)):
            field_ref[part, number // 2, :, inner] = half
    for part, half in enumerate(halves(geo)):
        for tile in range(tiles):
            geo_ref[part, tile] = half[:, tile * TILE:(tile + 1) * TILE]


def stencil_rows(meta, slots, first):
    lane = iota((HALO, META), 1)
    spot = iota((HALO, TILE), 1)
    centre = iota((HALO, 1), 0) + first
    sums = [jnp.zeros((HALO, TILE), F32) for _ in range(TYPES)]
    for slot in range(slots):
        column = centre + meta[:, 3 * slots + slot:3 * slots + slot + 1].astype(jnp.int32)
        hit = spot == column
        for kind in range(TYPES):
            weight = meta[:, kind * slots + slot:kind * slots + slot + 1]
            sums[kind] += jnp.where(hit, weight, 0.0)
    out = []
    for kind in range(TYPES):
        inside = (lane >= kind * slots) & (lane < (kind + 1) * slots)
        total = jnp.sum(jnp.where(inside, meta, 0.0), axis=1, keepdims=True)
        high, low = halves(jnp.where(spot == centre, total, 0.0) - sums[kind])
        out.append(jnp.concatenate([high, high, low], axis=1))
    return out


def gathered(weights, near, fine):
    return halves(dot(weights, jnp.concatenate([near, fine, near], axis=0)))


def mixed(buckets, mixer_ref, count):
    highs = [buckets[0, kind, :count, :] for kind in range(TYPES)]
    lows = [buckets[1, kind, :count, :] for kind in range(TYPES)]
    return dot(jnp.concatenate(highs + highs + lows, axis=1), mixer_ref[...])


def interior_kernel(slots, field_ref, meta_ref, mixer_ref, blocks_ref,
                    inner_ref, weights_ref, stencil, buckets):
    tiles, rows = field_ref.shape[1:3]
    edge = ITERS * HALO
    shift = basis_shift(blocks_ref[...], slots)
    inside = rows - 2 * HALO

    def build(chunk, carry):
        first = pl.multiple_of(chunk * HALO, HALO)
        start = pl.multiple_of(chunk * HALO + HALO, HALO)
        for kind, value in enumerate(
            stencil_rows(meta_ref[pl.ds(start, HALO), :], slots, first + HALO)
        ):
            stencil[kind, pl.ds(first, HALO), :] = value
        return carry

    lax.fori_loop(0, inside // HALO, build, 0)

    def build_outer(side, chunk):
        first = chunk * HALO
        start = first + side * (rows - edge)
        spot = first + edge if side == 0 else first + rows - 2 * edge
        for kind, value in enumerate(stencil_rows(meta_ref[start:start + HALO, :], slots, spot)):
            weights_ref[side, kind, first:first + HALO, :] = value

    for step in range(ITERS - 1):
        begin = HALO * (step + 1)
        blank = jnp.zeros((begin, TILE), BF16)
        for part in range(2):
            for tile in range(tiles):
                inner_ref[step, part, tile, :begin, :] = blank
                inner_ref[step, part, tile, rows - begin:, :] = blank
    for step in range(ITERS):
        skip = HALO * step
        count = inside - 2 * skip
        begin = HALO + skip
        weights = jnp.concatenate(
            [stencil[kind, skip:inside - skip, :] for kind in range(TYPES)], axis=0
        )

        def read(part, tile, block):
            if step == 0:
                return field_ref[part, tile, block, :]
            return inner_ref[step - 1, part, tile, block, :]

        for tile in range(tiles):
            every = slice(0, rows)
            for part, half in enumerate(
                gathered(weights, read(0, tile, every), read(1, tile, every))
            ):
                for kind in range(TYPES):
                    buckets[part, kind, tile * count:(tile + 1) * count, :] = (
                        half[kind * count:(kind + 1) * count]
                    )
        for side in range(2):
            build_outer(side, step)
        applied = mixed(buckets, mixer_ref, tiles * count)
        block = slice(begin, begin + count)
        for tile in range(tiles):
            here = read(0, tile, block).astype(F32) + read(1, tile, block).astype(F32)
            value = applied[tile * count:(tile + 1) * count] + (MASS_SHIFT - shift) * here
            for part, half in enumerate(halves(value)):
                inner_ref[step, part, tile, block, :] = half


def sides_kernel(slots, pos_ref, core_ref, chip_ref, field_ref, inner_ref, weights_ref, mixer_ref,
                 blocks_ref, geo_ref, first_ref, basis_ref, moments_ref, v_refs, meta_refs, stencil, buckets):
    tiles, rows = field_ref.shape[1:3]
    width = tiles * TILE
    dof = blocks_ref.shape[1]
    cases = width // dof
    edge = ITERS * HALO
    outer = edge - HALO
    count = edge
    rest = TILE - edge
    shift = basis_shift(blocks_ref[...], slots)
    even = lax.rem(pos_ref[0, 0], jnp.int32(2)) == 0

    for tile in range(tiles + 1):
        lanes = slice(tile * TILE, (tile + 1) * TILE) if tile < tiles else slice(width, None)
        core, chip = core_ref[:, lanes], chip_ref[:, lanes]
        for side, value in enumerate((jnp.where(even, chip, core), jnp.where(even, core, chip))):
            if tile == tiles:
                meta_refs[side] = value
            else:
                for part, half in enumerate(halves(value)):
                    v_refs[0, side, part, tile] = half

    def build(side):
        for first in range(0, outer, HALO):
            start = first + HALO * (1 - side)
            spot = first + HALO if side == 0 else first + rows - edge
            for kind, value in enumerate(
                stencil_rows(meta_refs[side, start:start + HALO, :], slots, spot)
            ):
                stencil[side, kind, first:first + HALO, :] = value

    def window(step, side, part, tile):
        near = v_refs[step, side, part, tile]
        if step == 0:
            if side == 0:
                return jnp.concatenate([near, field_ref[part, tile, :rest, :]], axis=0)
            return jnp.concatenate([field_ref[part, tile, rows - rest:, :], near], axis=0)
        blank = jnp.zeros((HALO * step, TILE), BF16)
        begin = HALO * step
        if side == 0:
            far = inner_ref[step - 1, part, tile, begin:rest, :]
            return jnp.concatenate([blank, near, far], axis=0)
        far = inner_ref[step - 1, part, tile, rows - rest:rows - begin, :]
        return jnp.concatenate([far, near, blank], axis=0)

    def weight_rows(step, side, kind):
        keep = outer - HALO * step
        if side == 0:
            pieces = [weights_ref[0, kind, :count - keep, :]]
            if keep:
                pieces.insert(0, stencil[0, kind, outer - keep:, :])
        else:
            pieces = [weights_ref[1, kind, keep:, :]]
            if keep:
                pieces.append(stencil[1, kind, :keep, :])
        return jnp.concatenate(pieces, axis=0)

    def convert(step):
        begin = HALO * step
        for half in range(2):

            def piece(tile, part):
                lanes = slice(part * META, (part + 1) * META)
                return jnp.concatenate(
                    [
                        v_refs[step, 0, half, tile, count - begin:, lanes],
                        inner_ref[step - 1, half, tile, begin:rows - begin, lanes],
                        v_refs[step, 1, half, tile, :begin, lanes],
                    ],
                    axis=0,
                )

            for number, value in enumerate(swap_blocks(piece)):
                lanes = slice(number % 2 * META, (number % 2 + 1) * META)
                basis_ref[step - 1, half, number // 2, :, lanes] = value

    def tall(step, part):
        if step == 0:
            return jnp.concatenate([geo_ref[part, tile] for tile in range(tiles)], axis=0)
        return jnp.concatenate([basis_ref[step - 1, part, tile] for tile in range(tiles)], axis=0)

    def mixed_gram(high, low):
        return folded_rows(high[:, :TILE] + high[:, TILE:] + low, cases)

    def even_gram(high):
        cross = high[:, TILE:]
        return folded_rows(high[:, :TILE] + cross + cross.T, cases)

    sums = [first_ref[...]]
    for step in range(ITERS):
        centres = []
        for side in range(2):
            if step == 0:
                build(side)
            weights = jnp.concatenate(
                [weight_rows(step, side, kind) for kind in range(TYPES)], axis=0
            )
            for tile in range(tiles):
                row = (side * tiles + tile) * count
                near, fine = (window(step, side, part, tile) for part in range(2))
                first = HALO * (step + 1) if side == 0 else TILE - HALO * (step + 1) - count
                centres.append((near[first:first + count], fine[first:first + count]))
                for part, half in enumerate(gathered(weights, near, fine)):
                    for kind in range(TYPES):
                        buckets[part, kind, row:row + count, :] = (
                            half[kind * count:(kind + 1) * count]
                        )
        applied = mixed(buckets, mixer_ref, 2 * tiles * count)
        for side in range(2):
            for tile in range(tiles):
                number = side * tiles + tile
                near, fine = centres[number]
                here = near.astype(F32) + fine.astype(F32)
                value = applied[number * count:(number + 1) * count] + (MASS_SHIFT - shift) * here
                for part, half in enumerate(halves(value)):
                    v_refs[step + 1, side, part, tile] = half

        convert(step + 1)
        if step == 1:
            others = [tall(k, part) for k in range(3) for part in range(2)]
            high = dot_tn(tall(1, 0), jnp.concatenate(others, axis=1))
            low = dot_tn(tall(1, 1), jnp.concatenate([others[0], others[4]], axis=1))
            sums.append(mixed_gram(high[:, :2 * TILE], low[:, :TILE]))
            sums.append(even_gram(high[:, 2 * TILE:4 * TILE]))
            sums.append(mixed_gram(high[:, 4 * TILE:], low[:, TILE:]))
        elif step == 2:
            others = [tall(k, part) for k in range(2, 4) for part in range(2)]
            high = dot_tn(tall(2, 0), jnp.concatenate(others, axis=1))
            low = dot_tn(tall(2, 1), others[2])
            sums.append(even_gram(high[:, :2 * TILE]))
            sums.append(mixed_gram(high[:, 2 * TILE:], low))

    remainder = jnp.concatenate(sums, axis=0)
    pieces = []
    for _ in range(3):
        pieces.append(remainder.astype(BF16))
        remainder = remainder - pieces[-1].astype(F32)
    collect = one_hot(iota((TILE, META), 0) // 16 == iota((TILE, META), 1) % 16)
    folded = dot(jnp.concatenate(pieces, axis=1), jnp.concatenate([collect] * 3, axis=0))
    group = iota((cases, META), 1) // cases
    moments = jnp.zeros((cases, META), F32)
    for number in range(2 * ITERS):
        part = folded[number * cases:(number + 1) * cases]
        moments = jnp.where(group == number, part, moments)
    moments_ref[...] = moments


def refined_reciprocal(value):
    guess = pl.reciprocal(value, approx=True)
    for _ in range(2):
        guess = guess * (2.0 - value * guess)
    return guess


def finish_kernel(slots, blocks_ref, geo_ref, basis_ref, *refs):
    moment_refs = refs[:-4]
    solution_hbm, residual_hbm, out_refs, sems = refs[-4:]
    rows, width = out_refs.shape[1:]
    dof = blocks_ref.shape[1]
    cases = width // dof
    tiles = width // TILE
    shift = basis_shift(blocks_ref[...], slots)
    moments = moment_refs[0][...]
    for ref in moment_refs[1:]:
        moments = moments + ref[...]
    group = iota((cases, META), 1) // cases
    system = []
    for row in range(ITERS):
        plain = moments if row == 0 else pltpu.roll(moments, META - cases * row, 1)
        ahead = pltpu.roll(moments, META - cases * (row + 1), 1)
        target = pltpu.roll(moments, cases * (ITERS - row), 1)
        system.append(jnp.where(group < ITERS, ahead + shift * plain, target))
    system = jnp.concatenate(system, axis=0)
    size = ITERS * cases
    index = iota((size, 1), 0)
    for pivot in range(0, size, 2):
        column_a = jnp.broadcast_to(system[:, pivot:pivot + 1], (size, META))
        column_b = jnp.broadcast_to(system[:, pivot + 1:pivot + 2], (size, META))
        line_a = system[pivot:pivot + 1, :]
        line_b = system[pivot + 1:pivot + 2, :]
        above = column_b[pivot:pivot + 1, :]
        inverse = refined_reciprocal(column_a[pivot:pivot + 1, :])
        factor = column_a[pivot + 1:pivot + 2, :] * inverse
        corner = column_b[pivot + 1:pivot + 2, :] - factor * above
        line_b = (line_b - factor * line_a) * refined_reciprocal(corner)
        line_a = (line_a - above * line_b) * inverse
        update = system - column_a * line_a - column_b * line_b
        system = jnp.where(index == pivot, line_a, jnp.where(index == pivot + 1, line_b, update))

    unit = jnp.where(iota((cases, META), 1) % cases == iota((cases, META), 0), 1.0, 0.0)
    answers = []
    for row in range(ITERS):
        part = jnp.where(group == ITERS, system[row * cases:(row + 1) * cases], 0.0)
        step = cases
        while step < META:
            part = part + pltpu.roll(part, step, 1)
            step *= 2
        answers.append(part)
    left_over = [unit - shift * answers[0]]
    for row in range(1, ITERS):
        left_over.append(-(answers[row - 1] + shift * answers[row]))
    left_over.append(-answers[ITERS - 1])

    meets = iota((TILE, TILE), 0) % 16 == iota((TILE, TILE), 1) // 16

    def spread(parts):
        highs, lows = [], []
        for part in parts:
            tall = jnp.broadcast_to(part[:, None, :], (cases, TILE // cases, META))
            tall = tall.reshape(TILE, META)
            wide = jnp.concatenate([tall] * (TILE // META), axis=1)
            high, low = halves(jnp.where(meets, wide, 0.0))
            highs.append(high)
            lows.append(low)
        return jnp.concatenate(highs + highs + lows, axis=0)

    def tall(term, part):
        if term == 0:
            return jnp.concatenate([geo_ref[part, tile] for tile in range(tiles)], axis=0)
        return jnp.concatenate([basis_ref[term - 1, part, tile] for tile in range(tiles)], axis=0)

    copies = []
    for number, (out_hbm, parts) in enumerate(
        ((solution_hbm, answers), (residual_hbm, left_over))
    ):
        matrix = spread(parts)
        terms = matrix.shape[0] // (3 * TILE)
        highs = [tall(term, 0) for term in range(terms)]
        lows = [tall(term, 1) for term in range(terms)]
        value = dot(jnp.concatenate(highs + lows + highs, axis=1), matrix)
        for tile in range(tiles):
            lanes = slice(tile * TILE, (tile + 1) * TILE)
            out_refs[number, :, lanes] = value[tile * rows:(tile + 1) * rows]
        copies.append(pltpu.make_async_copy(out_refs.at[number], out_hbm, sems.at[number]))
        copies[number].start()
    for copy in copies:
        copy.wait()


def on_device(loads, row_ids, densities, block_cols, block_types, ref_blocks):
    rows, width = loads.shape
    slots = densities.shape[1]
    cases = width // ref_blocks.shape[1]
    cap = rows // 4
    edge = ITERS * HALO
    tiles = width // TILE
    devices = lax.axis_size("sub")
    position = lax.axis_index("sub").astype(jnp.int32).reshape(1, 1)
    shape = jax.ShapeDtypeStruct
    same_chip = [(i, i ^ 1) for i in range(devices)]
    next_chip = [(i, i + 1) for i in range(1, devices - 1, 2)]
    next_chip += [(i + 1, i) for i in range(1, devices - 1, 2)]
    neighbour = dict(next_chip)
    rounds = [[], []]
    for i in range(devices):
        early = 0 if far_first(i, devices) else 1
        rounds[early].append((i, (i + devices // 2) % devices))
        if i in neighbour:
            rounds[1 - early].append((i, neighbour[i]))

    block = shape((cap * width // META + cap // 2, META), F32)
    to_first, meta, target = pl.pallas_call(
        functools.partial(pack_first_kernel, devices),
        out_shape=(block, shape((META, rows), F32), shape((8, rows), jnp.int32)),
        in_specs=[SMEM] + [HBM] * 5,
        out_specs=(VMEM,) * 3,
        scratch_shapes=[
            pltpu.VMEM((rows, width), F32),
            pltpu.VMEM((1, rows), jnp.int32),
            pltpu.VMEM((slots, rows), F32),
            pltpu.VMEM((slots, rows), jnp.int32),
            pltpu.VMEM((slots, rows), jnp.int32),
            pltpu.SemaphoreType.DMA((5,)),
        ],
        compiler_params=PACK_PARAMS,
        name="pack_first",
    )(position, loads, row_ids.reshape(1, rows), densities.T, block_cols.T, block_types.T)
    from_first = lax.ppermute(to_first, "sub", rounds[0])

    to_core, to_second = pl.pallas_call(
        functools.partial(pack_second_kernel, devices),
        out_shape=(block, block),
        in_specs=[SMEM] + [HBM] * 3,
        out_specs=(VMEM,) * 2,
        scratch_shapes=[
            pltpu.VMEM((8, rows), jnp.int32),
            pltpu.VMEM((META, rows), F32),
            pltpu.VMEM((rows, width), F32),
            pltpu.SemaphoreType.DMA((3,)),
        ],
        compiler_params=PACK_PARAMS,
        name="pack_second",
    )(position, target, meta, loads)
    from_second = lax.ppermute(to_second, "sub", rounds[1])
    from_core = lax.ppermute(to_core, "sub", same_chip)

    mixer_shape = shape((3 * TYPES * TILE, TILE), BF16)
    kept, kept_meta, mixer, first = pl.pallas_call(
        functools.partial(prepare_kernel, slots),
        out_shape=(
            shape((rows, width), F32),
            shape((rows, META), F32),
            mixer_shape,
            shape((cases, TILE), F32),
        ),
        in_specs=[VMEM] * 3,
        out_specs=(VMEM,) * 4,
        compiler_params=PARAMS,
        cost_estimate=pl.CostEstimate(
            flops=4_000_000_000, bytes_accessed=4_000_000, transcendentals=0
        ),
        name="prepare",
    )(loads, meta, ref_blocks)

    border = shape((edge, width + META), F32)
    pair = shape((2, tiles, rows, TILE), BF16)
    geo, field, geo_meta, to_core, to_chip = pl.pallas_call(
        functools.partial(arrange_kernel, slots),
        out_shape=(pair, pair, shape((rows, META), F32), border, border),
        in_specs=[SMEM] + [VMEM] * 5,
        out_specs=(VMEM,) * 5,
        compiler_params=PARAMS,
        name="arrange",
    )(position, kept, kept_meta, from_core, from_first, from_second)

    halo_chip = lax.ppermute(to_chip, "sub", next_chip)
    halo_core = lax.ppermute(to_core, "sub", same_chip)

    basis_shape = shape((ITERS, 2, tiles, rows, TILE), BF16)
    inner, weights = pl.pallas_call(
        functools.partial(interior_kernel, slots),
        out_shape=(basis_shape, shape((2, TYPES, edge, 3 * TILE), BF16)),
        in_specs=[VMEM] * 4,
        out_specs=(VMEM,) * 2,
        scratch_shapes=[
            pltpu.VMEM((TYPES, rows - 2 * HALO, 3 * TILE), BF16),
            pltpu.VMEM((2, TYPES, tiles * (rows - 2 * HALO), TILE), BF16),
        ],
        compiler_params=PARAMS,
        cost_estimate=pl.CostEstimate(
            flops=10_000_000_000, bytes_accessed=8_000_000, transcendentals=0
        ),
        name="interior",
    )(field, geo_meta, mixer, ref_blocks)

    basis, moments = pl.pallas_call(
        functools.partial(sides_kernel, slots),
        out_shape=(basis_shape, shape((cases, META), F32)),
        in_specs=[SMEM] + [VMEM] * 9,
        out_specs=(VMEM,) * 2,
        scratch_shapes=[
            pltpu.VMEM((ITERS + 1, 2, 2, tiles, edge, TILE), BF16),
            pltpu.VMEM((2, edge, META), F32),
            pltpu.VMEM((2, TYPES, edge - HALO, 3 * TILE), BF16),
            pltpu.VMEM((2, TYPES, 2 * tiles * edge, TILE), BF16),
        ],
        compiler_params=PARAMS,
        name="sides",
    )(position, halo_core, halo_chip, field, inner, weights, mixer, ref_blocks, geo, first)

    bits = devices.bit_length() - 1
    gathered_moments = [moments]
    for low, high in ((0, bits // 2), (bits // 2, bits)):
        partial = sum(gathered_moments[1:], gathered_moments[0])
        gathered_moments = [partial]
        for mask in range(1, 1 << (high - low)):
            swap = [(i, i ^ (mask << low)) for i in range(devices)]
            gathered_moments.append(lax.ppermute(partial, "sub", swap))

    return pl.pallas_call(
        functools.partial(finish_kernel, slots),
        out_shape=(shape((rows, width), F32), shape((rows, width), F32)),
        in_specs=[VMEM] * (3 + len(gathered_moments)),
        out_specs=(HBM,) * 2,
        scratch_shapes=[pltpu.VMEM((2, rows, width), F32), pltpu.SemaphoreType.DMA((2,))],
        compiler_params=PARAMS,
        name="finish",
    )(ref_blocks, geo, basis, *gathered_moments)


def solution(mesh):
    placed = (
        P(("groups", "sub"), None),
        P(("groups", "sub")),
        P(("groups", "sub"), None),
        P(("groups", "sub"), None),
        P(("groups", "sub"), None),
        P(),
    )
    return jax.shard_map(
        on_device,
        mesh=mesh,
        in_specs=placed,
        out_specs=(P(("groups", "sub"), None), P(("groups", "sub"), None)),
        check_vma=False,
    )
```

```python
import functools

import jax
import jax.numpy as jnp
from jax import lax
from jax.experimental import pallas as pl
from jax.experimental.pallas import tpu as pltpu
from jax.sharding import PartitionSpec as P

HALO = 32
TYPES = 3
ITERS = 3
MASS_SHIFT = 0.5
META = 128
TILE = 256

F32 = jnp.float32
BF16 = jnp.bfloat16
VMEM = pl.BlockSpec(memory_space=pltpu.VMEM)
SMEM = pl.BlockSpec(memory_space=pltpu.SMEM)
HBM = pl.BlockSpec(memory_space=pltpu.HBM)
PARAMS = pltpu.CompilerParams(vmem_limit_bytes=40 * 1024 * 1024)


def dot(left, right):
    return jnp.dot(left, right, preferred_element_type=F32)


def dot_nt(left, right):
    return lax.dot_general(left, right, (((1,), (1,)), ((), ())), preferred_element_type=F32)


def dot_tn(left, right):
    return lax.dot_general(left, right, (((0,), (0,)), ((), ())), preferred_element_type=F32)


def halves(value):
    high = value.astype(BF16)
    return high, (value - high.astype(F32)).astype(BF16)


def iota(shape, axis):
    return lax.broadcasted_iota(jnp.int32, shape, axis)


def one_hot(condition):
    return jnp.where(condition, 1.0, 0.0).astype(BF16)


PACK_PARAMS = pltpu.CompilerParams(vmem_limit_bytes=62 * 1024 * 1024)


def basis_shift(blocks, slots):
    dof = blocks.shape[1]
    same = iota((dof, dof), 0) == iota((dof, dof), 1)
    total = sum(jnp.where(same, blocks[t], 0.0) for t in range(TYPES))
    mean = jnp.sum(jnp.sum(total, axis=1, keepdims=True), axis=0, keepdims=True) / (TYPES * dof)
    return MASS_SHIFT + 0.2 * slots * mean


def swap_blocks(piece):
    lane = iota(piece(0, 0).shape, 1)
    low = lane < META // 2
    out = []
    for tile in range(4):
        for part in range(2):
            first, second = piece(2 * part, tile // 2), piece(2 * part + 1, tile // 2)
            if tile % 2 == 0:
                second = pltpu.roll(second, META // 2, 1)
            else:
                first = pltpu.roll(first, META // 2, 1)
            out.append(jnp.where(low, first, second))
    return out


def given_to_gram():
    source, target = iota((TILE, TILE), 0), iota((TILE, TILE), 1)
    return one_hot((target // 16 == source % 16) & (target % 16 == source // 16))


def peers(pos, devices):
    odd = lax.rem(pos, jnp.int32(2))
    return (
        pos + 1 - 2 * odd,
        pos - 1 + 2 * odd,
        lax.rem(pos + devices // 2, jnp.int32(devices)),
    )


def far_first(pos, devices):
    half = devices // 2
    group = (pos % half + 1) // 2 % max(half // 2, 1)
    return group % 2 == 1


def targets(pos, ids, rows, devices):
    cap = rows // 4
    owner = lax.div(ids, jnp.int32(rows))
    goes = []
    for peer in peers(pos, devices):
        here = owner == peer
        for other in goes:
            here = here & ~other
        goes.append(here)
    flags = jnp.concatenate(
        [jnp.where(g, 1.0, 0.0) for g in goes] + [jnp.zeros((5, rows), F32)], axis=0
    )
    before = one_hot(iota((rows, rows), 0) < iota((rows, rows), 1))
    rank = dot(flags.astype(BF16), before).astype(jnp.int32)
    target = jnp.full((1, rows), -1, jnp.int32)
    for side in range(3):
        target = jnp.where(goes[side], rank[side:side + 1] + side * cap, target)
    return target


def fill_block(pick, loads, meta, out_refs):
    width = loads.shape[1]
    cap = pick.shape[0]
    twice = jnp.concatenate([pick, pick], axis=1)
    notes = dot_nt(twice, jnp.concatenate(halves(meta), axis=1))
    notes = notes[:cap // 2] + pltpu.roll(notes[cap // 2:], META // 2, 1)
    body = dot(twice, jnp.concatenate(halves(loads), axis=0))
    parts = width // META // len(out_refs)
    few = cap // 2 // len(out_refs)
    for number, out_ref in enumerate(out_refs):
        for part in range(parts):
            start = (number * parts + part) * META
            out_ref[part * cap:(part + 1) * cap, :] = body[:, start:start + META]
        out_ref[parts * cap:, :] = notes[number * few:(number + 1) * few]


def read_block(refs, width):
    parts = width // META // len(refs)
    few = refs[0].shape[0] // (2 * parts * len(refs) + 1)
    cap = 2 * few * len(refs)
    body = jnp.concatenate(
        [ref[part * cap:(part + 1) * cap, :] for ref in refs for part in range(parts)], axis=1
    )
    notes = jnp.concatenate([ref[parts * cap:, :] for ref in refs], axis=0)
    notes = jnp.concatenate([notes, pltpu.roll(notes, META // 2, 1)], axis=0)
    return body, jnp.where(iota(notes.shape, 1) < META // 2, notes, 0.0)


def pack_kernel(devices, pos_ref, loads_hbm, rows_hbm, dens_hbm, cols_hbm, types_hbm,
                first_a, first_b, second_a, second_b, core_ref, meta_ref,
                loads_ref, rows_ref, dens_ref, cols_ref, types_ref, sems):
    pairs = (
        (rows_hbm, rows_ref), (dens_hbm, dens_ref), (cols_hbm, cols_ref),
        (types_hbm, types_ref), (loads_hbm, loads_ref),
    )
    copies = [
        pltpu.make_async_copy(source, target, sems.at[number])
        for number, (source, target) in enumerate(pairs)
    ]
    for copy in copies:
        copy.start()
    for copy in copies[:4]:
        copy.wait()
    rows = loads_ref.shape[0]
    slots = dens_ref.shape[0]
    cap = rows // 4
    pos = pos_ref[0, 0]
    ids = rows_ref[...]
    owner = lax.div(ids, jnp.int32(rows))
    local = (ids - owner * rows + 1).astype(F32)
    target = targets(pos, ids, rows, devices)

    density = dens_ref[...]
    kinds = types_ref[...]
    for kind in range(TYPES):
        meta_ref[kind * slots:(kind + 1) * slots, :] = jnp.where(kinds == kind, density, 0.0)
    meta_ref[3 * slots:4 * slots, :] = (cols_ref[...] - ids).astype(F32)
    meta_ref[4 * slots:, :] = jnp.zeros((META - 4 * slots, rows), F32)
    meta_ref[4 * slots:4 * slots + 1, :] = local
    meta_ref[4 * slots + 1:4 * slots + 2, :] = jnp.where(owner == pos, local, 0.0)

    copies[4].wait()
    early = jnp.where(far_first(pos, devices), 2, 1)
    for side, refs in ((early, (first_a, first_b)), (3 - early, (second_a, second_b)), (0, (core_ref,))):
        pick = one_hot(iota((cap, rows), 0) + side * cap == target)
        fill_block(pick, loads_ref[...], meta_ref[...], refs)


def reorder(parts, tiles):
    count = parts[0].shape[0]
    tall = [p[:, t * TILE:(t + 1) * TILE] for t in range(tiles) for p in parts]
    moved = dot(jnp.concatenate(tall, axis=0), given_to_gram()).astype(BF16)
    return [
        jnp.concatenate(
            [moved[(2 * t + p) * count:(2 * t + p + 1) * count] for t in range(tiles)], axis=1
        )
        for p in range(2)
    ]


def stacked_tiles(value, tiles):
    return jnp.concatenate([value[:, t * TILE:(t + 1) * TILE] for t in range(tiles)], axis=0)


def folded_rows(gram, cases):
    same_dof = iota((TILE, TILE), 0) % 16 == iota((TILE, TILE), 1) % 16
    gram = jnp.where(same_dof, gram, 0.0)
    return jnp.sum(gram.reshape(cases, TILE // cases, TILE), axis=1)


def prepare_kernel(slots, loads_ref, meta_ref, blocks_ref,
                   kept_ref, kept_meta_ref, mixer_ref, first_ref):
    rows, width = loads_ref.shape
    dof = blocks_ref.shape[1]
    tiles = width // TILE
    place = iota((rows, rows), 0) + 1
    own = one_hot(place == meta_ref[4 * slots + 1:4 * slots + 2, :].astype(jnp.int32))
    twice = jnp.concatenate([own, own], axis=1)
    moved = reorder(halves(loads_ref[...]), tiles)
    kept_ref[...] = dot(twice, jnp.concatenate(moved, axis=0))
    high, low = (stacked_tiles(part, tiles) for part in moved)
    gram = dot_tn(high, jnp.concatenate([high, low], axis=1))
    cross = gram[:, TILE:]
    first_ref[...] = folded_rows(gram[:, :TILE] + cross + cross.T, width // dof)
    kept_meta_ref[...] = dot_nt(twice, jnp.concatenate(halves(meta_ref[...]), axis=1))

    def dof_of(lane):
        return lane // 64 * 16 + lane % 16

    fold = one_hot(dof_of(iota((TILE, dof), 0)) == iota((TILE, dof), 1))
    unfold = one_hot(dof_of(iota((dof, TILE), 1)) == iota((dof, TILE), 0))
    same_case = iota((TILE, TILE), 0) // 16 % 4 == iota((TILE, TILE), 1) // 16 % 4
    for kind in range(TYPES):
        for copies, part in zip(((0, 2), (1,)), halves(blocks_ref[kind])):
            wide = dot(dot_nt(fold, part).astype(BF16), unfold)
            wide = jnp.where(same_case, wide, 0.0).astype(BF16)
            for copy in copies:
                start = (copy * TYPES + kind) * TILE
                mixer_ref[start:start + TILE, :] = wide


def arrange_kernel(slots, pos_ref, first_a, first_b, second_a, second_b, core_ref,
                   kept_ref, kept_meta_ref, geo_ref, field_ref, meta_ref, to_core_ref, to_chip_ref):
    rows, width = kept_ref.shape
    tiles = width // TILE
    edge = to_core_ref.shape[0]
    even = lax.rem(pos_ref[0, 0], jnp.int32(2)) == 0
    groups = ((first_a, first_b), (second_a, second_b), (core_ref,))
    blocks = [read_block(refs, width) for refs in groups]
    arrived = jnp.concatenate([block[0] for block in blocks], axis=0)
    arrived_meta = jnp.concatenate([block[1] for block in blocks], axis=0)
    count = arrived.shape[0]
    unit = one_hot(iota((8, META), 1) == 4 * slots)
    tags = dot_nt(unit, arrived_meta.astype(BF16))[0:1]
    other = one_hot(iota((rows, count), 0) + 1 == tags.astype(jnp.int32))
    twice = jnp.concatenate([other, other], axis=1)
    moved = reorder(halves(arrived), tiles)
    geo = kept_ref[...] + dot(twice, jnp.concatenate(moved, axis=0))
    meta = kept_meta_ref[...] + dot(twice, jnp.concatenate(halves(arrived_meta), axis=0))
    meta_ref[...] = meta

    def send(lanes, value):
        head, tail = value[:edge], value[rows - edge:]
        to_core_ref[:, lanes] = jnp.where(even, tail, head)
        to_chip_ref[:, lanes] = jnp.where(even, head, tail)

    send(slice(width, None), meta)

    def piece(tile, part):
        start = tile * TILE + part * META
        return geo[:, start:start + META]

    for number, value in enumerate(swap_blocks(piece)):
        lanes = slice(number * META, (number + 1) * META)
        send(lanes, value)
        inner = slice(number % 2 * META, (number % 2 + 1) * META)
        for part, half in enumerate(halves(value)):
            field_ref[part, number // 2, :, inner] = half
    for part, half in enumerate(halves(geo)):
        for tile in range(tiles):
            geo_ref[part, tile] = half[:, tile * TILE:(tile + 1) * TILE]


def stencil_rows(meta, slots, first):
    lane = iota((HALO, META), 1)
    spot = iota((HALO, TILE), 1)
    centre = iota((HALO, 1), 0) + first
    sums = [jnp.zeros((HALO, TILE), F32) for _ in range(TYPES)]
    for slot in range(slots):
        column = centre + meta[:, 3 * slots + slot:3 * slots + slot + 1].astype(jnp.int32)
        hit = spot == column
        for kind in range(TYPES):
            weight = meta[:, kind * slots + slot:kind * slots + slot + 1]
            sums[kind] += jnp.where(hit, weight, 0.0)
    out = []
    for kind in range(TYPES):
        inside = (lane >= kind * slots) & (lane < (kind + 1) * slots)
        total = jnp.sum(jnp.where(inside, meta, 0.0), axis=1, keepdims=True)
        high, low = halves(jnp.where(spot == centre, total, 0.0) - sums[kind])
        out.append(jnp.concatenate([high, high, low], axis=1))
    return out


def gathered(weights, near, fine):
    parts = [near, fine, near]
    spare = weights.shape[1] - 3 * near.shape[0]
    if spare:
        parts.append(jnp.zeros((spare, near.shape[1]), BF16))
    return halves(dot(weights, jnp.concatenate(parts, axis=0)))


def mixed(buckets, mixer_ref, count):
    highs = [buckets[0, kind, :count, :] for kind in range(TYPES)]
    lows = [buckets[1, kind, :count, :] for kind in range(TYPES)]
    return dot(jnp.concatenate(highs + highs + lows, axis=1), mixer_ref[...])


def interior_kernel(slots, field_ref, meta_ref, mixer_ref, blocks_ref,
                    inner_ref, weights_ref, stencil, buckets):
    tiles, rows = field_ref.shape[1:3]
    edge = ITERS * HALO
    shift = basis_shift(blocks_ref[...], slots)
    inside = rows - 2 * HALO

    def build(chunk, carry):
        first = pl.multiple_of(chunk * HALO, HALO)
        start = pl.multiple_of(chunk * HALO + HALO, HALO)
        for kind, value in enumerate(
            stencil_rows(meta_ref[pl.ds(start, HALO), :], slots, first + HALO)
        ):
            stencil[kind, pl.ds(first, HALO), :] = value
        return carry

    lax.fori_loop(0, inside // HALO, build, 0)

    def build_outer(side, chunk):
        first = chunk * HALO
        start = first + side * (rows - edge)
        spot = first + edge if side == 0 else first + rows - 2 * edge
        for kind, value in enumerate(stencil_rows(meta_ref[start:start + HALO, :], slots, spot)):
            weights_ref[side, kind, first:first + HALO, :] = value

    for step in range(ITERS - 1):
        begin = HALO * (step + 1)
        blank = jnp.zeros((begin, TILE), BF16)
        for part in range(2):
            for tile in range(tiles):
                inner_ref[step, part, tile, :begin, :] = blank
                inner_ref[step, part, tile, rows - begin:, :] = blank
    for step in range(ITERS):
        skip = HALO * step
        count = inside - 2 * skip
        begin = HALO + skip
        weights = jnp.concatenate(
            [stencil[kind, skip:inside - skip, :] for kind in range(TYPES)], axis=0
        )

        def read(part, tile, block):
            if step == 0:
                return field_ref[part, tile, block, :]
            return inner_ref[step - 1, part, tile, block, :]

        for tile in range(tiles):
            every = slice(0, rows)
            for part, half in enumerate(
                gathered(weights, read(0, tile, every), read(1, tile, every))
            ):
                for kind in range(TYPES):
                    buckets[part, kind, tile * count:(tile + 1) * count, :] = (
                        half[kind * count:(kind + 1) * count]
                    )
        for side in range(2):
            build_outer(side, step)
        applied = mixed(buckets, mixer_ref, tiles * count)
        block = slice(begin, begin + count)
        for tile in range(tiles):
            here = read(0, tile, block).astype(F32) + read(1, tile, block).astype(F32)
            value = applied[tile * count:(tile + 1) * count] + (MASS_SHIFT - shift) * here
            for part, half in enumerate(halves(value)):
                inner_ref[step, part, tile, block, :] = half


def sides_kernel(slots, pos_ref, core_ref, chip_ref, field_ref, inner_ref, weights_ref, mixer_ref,
                 blocks_ref, geo_ref, first_ref, basis_ref, moments_ref, v_refs, meta_refs, stencil, buckets):
    tiles, rows = field_ref.shape[1:3]
    width = tiles * TILE
    dof = blocks_ref.shape[1]
    cases = width // dof
    edge = ITERS * HALO
    outer = edge - HALO
    count = edge
    rest = TILE - edge
    shift = basis_shift(blocks_ref[...], slots)
    even = lax.rem(pos_ref[0, 0], jnp.int32(2)) == 0

    for tile in range(tiles + 1):
        lanes = slice(tile * TILE, (tile + 1) * TILE) if tile < tiles else slice(width, None)
        core, chip = core_ref[:, lanes], chip_ref[:, lanes]
        for side, value in enumerate((jnp.where(even, chip, core), jnp.where(even, core, chip))):
            if tile == tiles:
                meta_refs[side] = value
            else:
                for part, half in enumerate(halves(value)):
                    v_refs[0, side, part, tile] = half

    def build(side):
        for first in range(0, outer, HALO):
            start = first + HALO * (1 - side)
            spot = first + HALO if side == 0 else first + rows - edge
            for kind, value in enumerate(
                stencil_rows(meta_refs[side, start:start + HALO, :], slots, spot)
            ):
                stencil[side, kind, first:first + HALO, :] = value

    reach = count + 2 * HALO

    def window(step, side, part, tile):
        near = v_refs[step, side, part, tile]
        begin = HALO * step
        if side == 0:
            block = slice(begin, begin + reach - count)
        else:
            block = slice(rows - begin - (reach - count), rows - begin)
        if step == 0:
            far = field_ref[part, tile, block, :]
        else:
            far = inner_ref[step - 1, part, tile, block, :]
        return jnp.concatenate([near, far] if side == 0 else [far, near], axis=0)

    def weight_rows(step, side, kind):
        keep = outer - HALO * step
        if side == 0:
            pieces = [weights_ref[0, kind, :count - keep, :]]
            if keep:
                pieces.insert(0, stencil[0, kind, outer - keep:, :])
        else:
            pieces = [weights_ref[1, kind, keep:, :]]
            if keep:
                pieces.append(stencil[1, kind, :keep, :])
        rows_all = jnp.concatenate(pieces, axis=0)
        first = HALO * step if side == 0 else TILE - reach - HALO * step
        high = rows_all[:, first:first + reach]
        low = rows_all[:, 2 * TILE + first:2 * TILE + first + reach]
        blank = jnp.zeros((count, 2 * TILE - 3 * reach), BF16)
        return jnp.concatenate([high, high, low, blank], axis=1)

    def convert(step):
        begin = HALO * step
        for half in range(2):

            def piece(tile, part):
                lanes = slice(part * META, (part + 1) * META)
                return jnp.concatenate(
                    [
                        v_refs[step, 0, half, tile, count - begin:, lanes],
                        inner_ref[step - 1, half, tile, begin:rows - begin, lanes],
                        v_refs[step, 1, half, tile, :begin, lanes],
                    ],
                    axis=0,
                )

            for number, value in enumerate(swap_blocks(piece)):
                lanes = slice(number % 2 * META, (number % 2 + 1) * META)
                basis_ref[step - 1, half, number // 2, :, lanes] = value

    def tall(step, part):
        if step == 0:
            return jnp.concatenate([geo_ref[part, tile] for tile in range(tiles)], axis=0)
        return jnp.concatenate([basis_ref[step - 1, part, tile] for tile in range(tiles)], axis=0)

    def even_gram(high):
        cross = high[:, TILE:]
        return folded_rows(high[:, :TILE] + cross + cross.T, cases)

    sums = [first_ref[...]]
    for step in range(ITERS):
        centres = []
        for side in range(2):
            if step == 0:
                build(side)
            weights = jnp.concatenate(
                [weight_rows(step, side, kind) for kind in range(TYPES)], axis=0
            )
            for tile in range(tiles):
                row = (side * tiles + tile) * count
                near, fine = (window(step, side, part, tile) for part in range(2))
                centres.append((near[HALO:HALO + count], fine[HALO:HALO + count]))
                for part, half in enumerate(gathered(weights, near, fine)):
                    for kind in range(TYPES):
                        buckets[part, kind, row:row + count, :] = (
                            half[kind * count:(kind + 1) * count]
                        )
        applied = mixed(buckets, mixer_ref, 2 * tiles * count)
        for side in range(2):
            for tile in range(tiles):
                number = side * tiles + tile
                near, fine = centres[number]
                here = near.astype(F32) + fine.astype(F32)
                value = applied[number * count:(number + 1) * count] + (MASS_SHIFT - shift) * here
                for part, half in enumerate(halves(value)):
                    v_refs[step + 1, side, part, tile] = half

        convert(step + 1)
        if step == 0:
            left = jnp.concatenate([tall(1, 0), tall(1, 1)], axis=1)
            high = dot_tn(left, tall(0, 0))
            fine = dot_tn(tall(1, 0), jnp.concatenate([tall(0, 1), tall(1, 0), tall(1, 1)], axis=1))
            sums.append(folded_rows(high[:TILE] + high[TILE:] + fine[:, :TILE], cases))
            sums.append(even_gram(fine[:, TILE:]))
        elif step == 1:
            left = jnp.concatenate([tall(1, 0), tall(2, 0), tall(1, 1)], axis=1)
            high = dot_tn(left, tall(2, 0))
            fine = dot_tn(left[:, :2 * TILE], tall(2, 1))
            sums.append(folded_rows(high[:TILE] + high[2 * TILE:] + fine[:TILE], cases))
            sums.append(
                even_gram(jnp.concatenate([high[TILE:2 * TILE], fine[TILE:]], axis=1))
            )
        else:
            left = jnp.concatenate([tall(2, 0), tall(2, 1)], axis=1)
            high = dot_tn(left, tall(3, 0))
            fine = dot_tn(tall(2, 0), tall(3, 1))
            sums.append(folded_rows(high[:TILE] + high[TILE:] + fine, cases))

    remainder = jnp.concatenate(sums, axis=0)
    pieces = []
    for _ in range(3):
        pieces.append(remainder.astype(BF16))
        remainder = remainder - pieces[-1].astype(F32)
    collect = one_hot(iota((TILE, META), 0) // 16 == iota((TILE, META), 1) % 16)
    folded = dot(jnp.concatenate(pieces, axis=1), jnp.concatenate([collect] * 3, axis=0))
    group = iota((cases, META), 1) // cases
    moments = jnp.zeros((cases, META), F32)
    for number in range(2 * ITERS):
        part = folded[number * cases:(number + 1) * cases]
        moments = jnp.where(group == number, part, moments)
    moments_ref[...] = moments


def refined_reciprocal(value):
    guess = pl.reciprocal(value, approx=True)
    for _ in range(2):
        guess = guess * (2.0 - value * guess)
    return guess


def finish_kernel(slots, blocks_ref, geo_ref, basis_ref, *refs):
    moment_refs = refs[:-4]
    solution_hbm, residual_hbm, out_refs, sems = refs[-4:]
    rows, width = out_refs.shape[1:]
    dof = blocks_ref.shape[1]
    cases = width // dof
    tiles = width // TILE
    shift = basis_shift(blocks_ref[...], slots)
    moments = moment_refs[0][...]
    for ref in moment_refs[1:]:
        moments = moments + ref[...]
    group = iota((cases, META), 1) // cases
    system = []
    for row in range(ITERS):
        plain = moments if row == 0 else pltpu.roll(moments, META - cases * row, 1)
        ahead = pltpu.roll(moments, META - cases * (row + 1), 1)
        target = pltpu.roll(moments, cases * (ITERS - row), 1)
        system.append(jnp.where(group < ITERS, ahead + shift * plain, target))
    system = jnp.concatenate(system, axis=0)
    size = ITERS * cases
    index = iota((size, 1), 0)
    for pivot in range(0, size, 2):
        column_a = jnp.broadcast_to(system[:, pivot:pivot + 1], (size, META))
        column_b = jnp.broadcast_to(system[:, pivot + 1:pivot + 2], (size, META))
        line_a = system[pivot:pivot + 1, :]
        line_b = system[pivot + 1:pivot + 2, :]
        above = column_b[pivot:pivot + 1, :]
        inverse = refined_reciprocal(column_a[pivot:pivot + 1, :])
        factor = column_a[pivot + 1:pivot + 2, :] * inverse
        corner = column_b[pivot + 1:pivot + 2, :] - factor * above
        line_b = (line_b - factor * line_a) * refined_reciprocal(corner)
        line_a = (line_a - above * line_b) * inverse
        update = system - column_a * line_a - column_b * line_b
        system = jnp.where(index == pivot, line_a, jnp.where(index == pivot + 1, line_b, update))

    unit = jnp.where(iota((cases, META), 1) % cases == iota((cases, META), 0), 1.0, 0.0)
    answers = []
    for row in range(ITERS):
        part = jnp.where(group == ITERS, system[row * cases:(row + 1) * cases], 0.0)
        step = cases
        while step < META:
            part = part + pltpu.roll(part, step, 1)
            step *= 2
        answers.append(part)
    left_over = [unit - shift * answers[0]]
    for row in range(1, ITERS):
        left_over.append(-(answers[row - 1] + shift * answers[row]))
    left_over.append(-answers[ITERS - 1])

    meets = iota((TILE, TILE), 0) % 16 == iota((TILE, TILE), 1) // 16

    def spread(parts):
        highs, lows = [], []
        for part in parts:
            tall = jnp.broadcast_to(part[:, None, :], (cases, TILE // cases, META))
            tall = tall.reshape(TILE, META)
            wide = jnp.concatenate([tall] * (TILE // META), axis=1)
            high, low = halves(jnp.where(meets, wide, 0.0))
            highs.append(high)
            lows.append(low)
        return jnp.concatenate(highs + highs + lows, axis=0)

    def tall(term, part):
        if term == 0:
            return jnp.concatenate([geo_ref[part, tile] for tile in range(tiles)], axis=0)
        return jnp.concatenate([basis_ref[term - 1, part, tile] for tile in range(tiles)], axis=0)

    copies = []
    for number, (out_hbm, parts) in enumerate(
        ((solution_hbm, answers), (residual_hbm, left_over))
    ):
        matrix = spread(parts)
        terms = matrix.shape[0] // (3 * TILE)
        highs = [tall(term, 0) for term in range(terms)]
        lows = [tall(term, 1) for term in range(terms)]
        value = dot(jnp.concatenate(highs + lows + highs, axis=1), matrix)
        for tile in range(tiles):
            lanes = slice(tile * TILE, (tile + 1) * TILE)
            out_refs[number, :, lanes] = value[tile * rows:(tile + 1) * rows]
        copies.append(pltpu.make_async_copy(out_refs.at[number], out_hbm, sems.at[number]))
        copies[number].start()
    for copy in copies:
        copy.wait()


def on_device(loads, row_ids, densities, block_cols, block_types, ref_blocks):
    rows, width = loads.shape
    slots = densities.shape[1]
    cases = width // ref_blocks.shape[1]
    cap = rows // 4
    edge = ITERS * HALO
    tiles = width // TILE
    devices = lax.axis_size("sub")
    position = lax.axis_index("sub").astype(jnp.int32).reshape(1, 1)
    shape = jax.ShapeDtypeStruct
    same_chip = [(i, i ^ 1) for i in range(devices)]
    next_chip = [(i, i + 1) for i in range(1, devices - 1, 2)]
    next_chip += [(i + 1, i) for i in range(1, devices - 1, 2)]
    neighbour = dict(next_chip)
    rounds = [[], []]
    for i in range(devices):
        early = 0 if far_first(i, devices) else 1
        rounds[early].append((i, (i + devices // 2) % devices))
        if i in neighbour:
            rounds[1 - early].append((i, neighbour[i]))

    length = cap * width // META + cap // 2
    whole, piece = shape((length, META), F32), shape((length // 2, META), F32)
    *outgoing, meta = pl.pallas_call(
        functools.partial(pack_kernel, devices),
        out_shape=(piece, piece, piece, piece, whole, shape((META, rows), F32)),
        in_specs=[SMEM] + [HBM] * 5,
        out_specs=(VMEM,) * 6,
        scratch_shapes=[
            pltpu.VMEM((rows, width), F32),
            pltpu.VMEM((1, rows), jnp.int32),
            pltpu.VMEM((slots, rows), F32),
            pltpu.VMEM((slots, rows), jnp.int32),
            pltpu.VMEM((slots, rows), jnp.int32),
            pltpu.SemaphoreType.DMA((5,)),
        ],
        compiler_params=PACK_PARAMS,
        name="pack",
    )(position, loads, row_ids.reshape(1, rows), densities.T, block_cols.T, block_types.T)
    routes = (rounds[0], rounds[0], rounds[1], rounds[1], same_chip)
    incoming = [lax.ppermute(part, "sub", route) for part, route in zip(outgoing, routes)]

    mixer_shape = shape((3 * TYPES * TILE, TILE), BF16)
    kept, kept_meta, mixer, first = pl.pallas_call(
        functools.partial(prepare_kernel, slots),
        out_shape=(
            shape((rows, width), F32),
            shape((rows, META), F32),
            mixer_shape,
            shape((cases, TILE), F32),
        ),
        in_specs=[VMEM] * 3,
        out_specs=(VMEM,) * 4,
        compiler_params=PARAMS,
        cost_estimate=pl.CostEstimate(
            flops=4_000_000_000, bytes_accessed=4_000_000, transcendentals=0
        ),
        name="prepare",
    )(loads, meta, ref_blocks)

    border = shape((edge, width + META), F32)
    pair = shape((2, tiles, rows, TILE), BF16)
    geo, field, geo_meta, to_core, to_chip = pl.pallas_call(
        functools.partial(arrange_kernel, slots),
        out_shape=(pair, pair, shape((rows, META), F32), border, border),
        in_specs=[SMEM] + [VMEM] * 7,
        out_specs=(VMEM,) * 5,
        compiler_params=PARAMS,
        name="arrange",
    )(position, *incoming, kept, kept_meta)

    halo_chip = lax.ppermute(to_chip, "sub", next_chip)
    halo_core = lax.ppermute(to_core, "sub", same_chip)

    basis_shape = shape((ITERS, 2, tiles, rows, TILE), BF16)
    inner, weights = pl.pallas_call(
        functools.partial(interior_kernel, slots),
        out_shape=(basis_shape, shape((2, TYPES, edge, 3 * TILE), BF16)),
        in_specs=[VMEM] * 4,
        out_specs=(VMEM,) * 2,
        scratch_shapes=[
            pltpu.VMEM((TYPES, rows - 2 * HALO, 3 * TILE), BF16),
            pltpu.VMEM((2, TYPES, tiles * (rows - 2 * HALO), TILE), BF16),
        ],
        compiler_params=PARAMS,
        cost_estimate=pl.CostEstimate(
            flops=10_000_000_000, bytes_accessed=8_000_000, transcendentals=0
        ),
        name="interior",
    )(field, geo_meta, mixer, ref_blocks)

    basis, moments = pl.pallas_call(
        functools.partial(sides_kernel, slots),
        out_shape=(basis_shape, shape((cases, META), F32)),
        in_specs=[SMEM] + [VMEM] * 9,
        out_specs=(VMEM,) * 2,
        scratch_shapes=[
            pltpu.VMEM((ITERS + 1, 2, 2, tiles, edge, TILE), BF16),
            pltpu.VMEM((2, edge, META), F32),
            pltpu.VMEM((2, TYPES, edge - HALO, 3 * TILE), BF16),
            pltpu.VMEM((2, TYPES, 2 * tiles * edge, TILE), BF16),
        ],
        compiler_params=PARAMS,
        name="sides",
    )(position, halo_core, halo_chip, field, inner, weights, mixer, ref_blocks, geo, first)

    bits = devices.bit_length() - 1
    gathered_moments = [moments]
    for low, high in ((0, bits // 2), (bits // 2, bits)):
        partial = sum(gathered_moments[1:], gathered_moments[0])
        gathered_moments = [partial]
        for mask in range(1, 1 << (high - low)):
            swap = [(i, i ^ (mask << low)) for i in range(devices)]
            gathered_moments.append(lax.ppermute(partial, "sub", swap))

    return pl.pallas_call(
        functools.partial(finish_kernel, slots),
        out_shape=(shape((rows, width), F32), shape((rows, width), F32)),
        in_specs=[VMEM] * (3 + len(gathered_moments)),
        out_specs=(HBM,) * 2,
        scratch_shapes=[pltpu.VMEM((2, rows, width), F32), pltpu.SemaphoreType.DMA((2,))],
        compiler_params=PARAMS,
        name="finish",
    )(ref_blocks, geo, basis, *gathered_moments)


def solution(mesh):
    placed = (
        P(("groups", "sub"), None),
        P(("groups", "sub")),
        P(("groups", "sub"), None),
        P(("groups", "sub"), None),
        P(("groups", "sub"), None),
        P(),
    )
    return jax.shard_map(
        on_device,
        mesh=mesh,
        in_specs=placed,
        out_specs=(P(("groups", "sub"), None), P(("groups", "sub"), None)),
        check_vma=False,
    )
```

```python
import functools

import jax
import jax.numpy as jnp
from jax import lax
from jax.experimental import pallas as pl
from jax.experimental.pallas import tpu as pltpu
from jax.sharding import PartitionSpec as P

HALO = 32
TYPES = 3
ITERS = 3
MASS_SHIFT = 0.5
META = 128
TILE = 256

F32 = jnp.float32
BF16 = jnp.bfloat16
VMEM = pl.BlockSpec(memory_space=pltpu.VMEM)
SMEM = pl.BlockSpec(memory_space=pltpu.SMEM)
HBM = pl.BlockSpec(memory_space=pltpu.HBM)
PARAMS = pltpu.CompilerParams(vmem_limit_bytes=40 * 1024 * 1024)


def dot(left, right):
    return jnp.dot(left, right, preferred_element_type=F32)


def dot_nt(left, right):
    return lax.dot_general(left, right, (((1,), (1,)), ((), ())), preferred_element_type=F32)


def dot_tn(left, right):
    return lax.dot_general(left, right, (((0,), (0,)), ((), ())), preferred_element_type=F32)


def halves(value):
    high = value.astype(BF16)
    return high, (value - high.astype(F32)).astype(BF16)


def iota(shape, axis):
    return lax.broadcasted_iota(jnp.int32, shape, axis)


def one_hot(condition):
    return jnp.where(condition, 1.0, 0.0).astype(BF16)


PACK_PARAMS = pltpu.CompilerParams(vmem_limit_bytes=62 * 1024 * 1024)


def basis_shift(blocks, slots):
    dof = blocks.shape[1]
    same = iota((dof, dof), 0) == iota((dof, dof), 1)
    total = sum(jnp.where(same, blocks[t], 0.0) for t in range(TYPES))
    mean = jnp.sum(jnp.sum(total, axis=1, keepdims=True), axis=0, keepdims=True) / (TYPES * dof)
    return MASS_SHIFT + 0.2 * slots * mean


def swap_blocks(piece):
    lane = iota(piece(0, 0).shape, 1)
    low = lane < META // 2
    out = []
    for tile in range(4):
        for part in range(2):
            first, second = piece(2 * part, tile // 2), piece(2 * part + 1, tile // 2)
            if tile % 2 == 0:
                second = pltpu.roll(second, META // 2, 1)
            else:
                first = pltpu.roll(first, META // 2, 1)
            out.append(jnp.where(low, first, second))
    return out


def given_to_gram():
    source, target = iota((TILE, TILE), 0), iota((TILE, TILE), 1)
    return one_hot((target // 16 == source % 16) & (target % 16 == source // 16))


def peers(pos, devices):
    odd = lax.rem(pos, jnp.int32(2))
    return (
        pos + 1 - 2 * odd,
        pos - 1 + 2 * odd,
        lax.rem(pos + devices // 2, jnp.int32(devices)),
    )


def far_first(pos, devices):
    half = devices // 2
    group = (pos % half + 1) // 2 % max(half // 2, 1)
    return group % 2 == 1


def targets(pos, ids, rows, devices):
    cap = rows // 4
    owner = lax.div(ids, jnp.int32(rows))
    goes = []
    for peer in peers(pos, devices):
        here = owner == peer
        for other in goes:
            here = here & ~other
        goes.append(here)
    flags = jnp.concatenate(
        [jnp.where(g, 1.0, 0.0) for g in goes] + [jnp.zeros((5, rows), F32)], axis=0
    )
    before = one_hot(iota((rows, rows), 0) < iota((rows, rows), 1))
    rank = dot(flags.astype(BF16), before).astype(jnp.int32)
    target = jnp.full((1, rows), -1, jnp.int32)
    for side in range(3):
        target = jnp.where(goes[side], rank[side:side + 1] + side * cap, target)
    return target


def fill_block(pick, loads, meta, out_ref):
    width = loads.shape[1]
    cap = pick.shape[0]
    twice = jnp.concatenate([pick, pick], axis=1)
    notes = dot_nt(twice, jnp.concatenate(halves(meta), axis=1))
    body = dot(twice, jnp.concatenate(halves(loads), axis=0))
    parts = width // META
    for part in range(parts):
        out_ref[part * cap:(part + 1) * cap, :] = body[:, part * META:(part + 1) * META]
    out_ref[parts * cap:, :] = notes[:cap // 2] + pltpu.roll(notes[cap // 2:], META // 2, 1)


def read_block(ref, width):
    parts = width // META
    cap = ref.shape[0] * 2 // (2 * parts + 1)
    body = jnp.concatenate([ref[part * cap:(part + 1) * cap, :] for part in range(parts)], axis=1)
    notes = ref[parts * cap:, :]
    notes = jnp.concatenate([notes, pltpu.roll(notes, META // 2, 1)], axis=0)
    return body, jnp.where(iota(notes.shape, 1) < META // 2, notes, 0.0)


def pack_first_kernel(devices, pos_ref, loads_hbm, rows_hbm, dens_hbm, cols_hbm, types_hbm,
                      first_ref, meta_ref, target_ref,
                      loads_ref, rows_ref, dens_ref, cols_ref, types_ref, sems):
    pairs = (
        (rows_hbm, rows_ref), (dens_hbm, dens_ref), (cols_hbm, cols_ref),
        (types_hbm, types_ref), (loads_hbm, loads_ref),
    )
    copies = [
        pltpu.make_async_copy(source, target, sems.at[number])
        for number, (source, target) in enumerate(pairs)
    ]
    for copy in copies:
        copy.start()
    for copy in copies[:4]:
        copy.wait()
    rows = loads_ref.shape[0]
    slots = dens_ref.shape[0]
    cap = rows // 4
    pos = pos_ref[0, 0]
    ids = rows_ref[...]
    owner = lax.div(ids, jnp.int32(rows))
    local = (ids - owner * rows + 1).astype(F32)
    target = targets(pos, ids, rows, devices)
    target_ref[...] = jnp.broadcast_to(target, target_ref.shape)

    density = dens_ref[...]
    kinds = types_ref[...]
    for kind in range(TYPES):
        meta_ref[kind * slots:(kind + 1) * slots, :] = jnp.where(kinds == kind, density, 0.0)
    meta_ref[3 * slots:4 * slots, :] = (cols_ref[...] - ids).astype(F32)
    meta_ref[4 * slots:, :] = jnp.zeros((META - 4 * slots, rows), F32)
    meta_ref[4 * slots:4 * slots + 1, :] = local
    meta_ref[4 * slots + 1:4 * slots + 2, :] = jnp.where(owner == pos, local, 0.0)

    copies[4].wait()
    side = jnp.where(far_first(pos, devices), 2, 1)
    pick = one_hot(iota((cap, rows), 0) + side * cap == target)
    fill_block(pick, loads_ref[...], meta_ref[...], first_ref)


def pack_second_kernel(devices, pos_ref, target_hbm, meta_hbm, loads_hbm, core_ref, second_ref,
                       target_ref, meta_ref, loads_ref, sems):
    pairs = ((target_hbm, target_ref), (meta_hbm, meta_ref), (loads_hbm, loads_ref))
    copies = [
        pltpu.make_async_copy(source, target, sems.at[number])
        for number, (source, target) in enumerate(pairs)
    ]
    for copy in copies:
        copy.start()
    for copy in copies:
        copy.wait()
    rows = loads_ref.shape[0]
    cap = rows // 4
    late = jnp.where(far_first(pos_ref[0, 0], devices), 1, 2)
    for side, out_ref in ((late, second_ref), (0, core_ref)):
        pick = one_hot(iota((cap, rows), 0) + side * cap == target_ref[0:1, :])
        fill_block(pick, loads_ref[...], meta_ref[...], out_ref)


def reorder(parts, tiles):
    count = parts[0].shape[0]
    tall = [p[:, t * TILE:(t + 1) * TILE] for t in range(tiles) for p in parts]
    moved = dot(jnp.concatenate(tall, axis=0), given_to_gram()).astype(BF16)
    return [
        jnp.concatenate(
            [moved[(2 * t + p) * count:(2 * t + p + 1) * count] for t in range(tiles)], axis=1
        )
        for p in range(2)
    ]


def stacked_tiles(value, tiles):
    return jnp.concatenate([value[:, t * TILE:(t + 1) * TILE] for t in range(tiles)], axis=0)


def folded_rows(gram, cases):
    same_dof = iota((TILE, TILE), 0) % 16 == iota((TILE, TILE), 1) % 16
    gram = jnp.where(same_dof, gram, 0.0)
    return jnp.sum(gram.reshape(cases, TILE // cases, TILE), axis=1)


def prepare_kernel(slots, loads_ref, meta_ref, blocks_ref,
                   kept_ref, kept_meta_ref, mixer_ref, first_ref):
    rows, width = loads_ref.shape
    dof = blocks_ref.shape[1]
    tiles = width // TILE
    place = iota((rows, rows), 0) + 1
    own = one_hot(place == meta_ref[4 * slots + 1:4 * slots + 2, :].astype(jnp.int32))
    twice = jnp.concatenate([own, own], axis=1)
    moved = reorder(halves(loads_ref[...]), tiles)
    kept_ref[...] = dot(twice, jnp.concatenate(moved, axis=0))
    high, low = (stacked_tiles(part, tiles) for part in moved)
    gram = dot_tn(high, jnp.concatenate([high, low], axis=1))
    cross = gram[:, TILE:]
    first_ref[...] = folded_rows(gram[:, :TILE] + cross + cross.T, width // dof)
    kept_meta_ref[...] = dot_nt(twice, jnp.concatenate(halves(meta_ref[...]), axis=1))

    def dof_of(lane):
        return lane // 64 * 16 + lane % 16

    fold = one_hot(dof_of(iota((TILE, dof), 0)) == iota((TILE, dof), 1))
    unfold = one_hot(dof_of(iota((dof, TILE), 1)) == iota((dof, TILE), 0))
    same_case = iota((TILE, TILE), 0) // 16 % 4 == iota((TILE, TILE), 1) // 16 % 4
    for kind in range(TYPES):
        for copies, part in zip(((0, 2), (1,)), halves(blocks_ref[kind])):
            wide = dot(dot_nt(fold, part).astype(BF16), unfold)
            wide = jnp.where(same_case, wide, 0.0).astype(BF16)
            for copy in copies:
                start = (copy * TYPES + kind) * TILE
                mixer_ref[start:start + TILE, :] = wide


def arrange_kernel(slots, pos_ref, kept_ref, kept_meta_ref, core_ref, first_ref, second_ref,
                   geo_ref, field_ref, meta_ref, to_core_ref, to_chip_ref):
    rows, width = kept_ref.shape
    tiles = width // TILE
    edge = to_core_ref.shape[0]
    even = lax.rem(pos_ref[0, 0], jnp.int32(2)) == 0
    blocks = [read_block(ref, width) for ref in (core_ref, first_ref, second_ref)]
    arrived = jnp.concatenate([block[0] for block in blocks], axis=0)
    arrived_meta = jnp.concatenate([block[1] for block in blocks], axis=0)
    count = arrived.shape[0]
    unit = one_hot(iota((8, META), 1) == 4 * slots)
    tags = dot_nt(unit, arrived_meta.astype(BF16))[0:1]
    other = one_hot(iota((rows, count), 0) + 1 == tags.astype(jnp.int32))
    twice = jnp.concatenate([other, other], axis=1)
    moved = reorder(halves(arrived), tiles)
    geo = kept_ref[...] + dot(twice, jnp.concatenate(moved, axis=0))
    meta = kept_meta_ref[...] + dot(twice, jnp.concatenate(halves(arrived_meta), axis=0))
    meta_ref[...] = meta

    def send(lanes, value):
        head, tail = value[:edge], value[rows - edge:]
        to_core_ref[:, lanes] = jnp.where(even, tail, head)
        to_chip_ref[:, lanes] = jnp.where(even, head, tail)

    send(slice(width, None), meta)

    def piece(tile, part):
        start = tile * TILE + part * META
        return geo[:, start:start + META]

    for number, value in enumerate(swap_blocks(piece)):
        lanes = slice(number * META, (number + 1) * META)
        send(lanes, value)
        inner = slice(number % 2 * META, (number % 2 + 1) * META)
        for part, half in enumerate(halves(value)):
            field_ref[part, number // 2, :, inner] = half
    for part, half in enumerate(halves(geo)):
        for tile in range(tiles):
            geo_ref[part, tile] = half[:, tile * TILE:(tile + 1) * TILE]


def stencil_rows(meta, slots, first):
    lane = iota((HALO, META), 1)
    spot = iota((HALO, TILE), 1)
    centre = iota((HALO, 1), 0) + first
    sums = [jnp.zeros((HALO, TILE), F32) for _ in range(TYPES)]
    for slot in range(slots):
        column = centre + meta[:, 3 * slots + slot:3 * slots + slot + 1].astype(jnp.int32)
        hit = spot == column
        for kind in range(TYPES):
            weight = meta[:, kind * slots + slot:kind * slots + slot + 1]
            sums[kind] += jnp.where(hit, weight, 0.0)
    out = []
    for kind in range(TYPES):
        inside = (lane >= kind * slots) & (lane < (kind + 1) * slots)
        total = jnp.sum(jnp.where(inside, meta, 0.0), axis=1, keepdims=True)
        high, low = halves(jnp.where(spot == centre, total, 0.0) - sums[kind])
        out.append(jnp.concatenate([high, high, low], axis=1))
    return out


def gathered(weights, near, fine):
    parts = [near, fine, near]
    spare = weights.shape[1] - 3 * near.shape[0]
    if spare:
        parts.append(jnp.zeros((spare, near.shape[1]), BF16))
    return halves(dot(weights, jnp.concatenate(parts, axis=0)))


def mixed(buckets, mixer_ref, count):
    highs = [buckets[0, kind, :count, :] for kind in range(TYPES)]
    lows = [buckets[1, kind, :count, :] for kind in range(TYPES)]
    return dot(jnp.concatenate(highs + highs + lows, axis=1), mixer_ref[...])


def interior_kernel(slots, field_ref, meta_ref, mixer_ref, blocks_ref,
                    inner_ref, weights_ref, stencil, buckets):
    tiles, rows = field_ref.shape[1:3]
    edge = ITERS * HALO
    shift = basis_shift(blocks_ref[...], slots)
    inside = rows - 2 * HALO

    for first in range(0, inside, HALO):
        start = first + HALO
        for kind, value in enumerate(
            stencil_rows(meta_ref[start:start + HALO, :], slots, first + HALO)
        ):
            stencil[kind, first:first + HALO, :] = value

    def build_outer(side, chunk):
        first = chunk * HALO
        start = first + side * (rows - edge)
        spot = first + edge if side == 0 else first + rows - 2 * edge
        for kind, value in enumerate(stencil_rows(meta_ref[start:start + HALO, :], slots, spot)):
            weights_ref[side, kind, first:first + HALO, :] = value

    for step in range(ITERS - 1):
        begin = HALO * (step + 1)
        blank = jnp.zeros((begin, TILE), BF16)
        for part in range(2):
            for tile in range(tiles):
                inner_ref[step, part, tile, :begin, :] = blank
                inner_ref[step, part, tile, rows - begin:, :] = blank
    for step in range(ITERS):
        skip = HALO * step
        count = inside - 2 * skip
        begin = HALO + skip
        weights = jnp.concatenate(
            [stencil[kind, skip:inside - skip, :] for kind in range(TYPES)], axis=0
        )

        def read(part, tile, block):
            if step == 0:
                return field_ref[part, tile, block, :]
            return inner_ref[step - 1, part, tile, block, :]

        for tile in range(tiles):
            every = slice(0, rows)
            for part, half in enumerate(
                gathered(weights, read(0, tile, every), read(1, tile, every))
            ):
                for kind in range(TYPES):
                    buckets[part, kind, tile * count:(tile + 1) * count, :] = (
                        half[kind * count:(kind + 1) * count]
                    )
        for side in range(2):
            build_outer(side, step)
        applied = mixed(buckets, mixer_ref, tiles * count)
        block = slice(begin, begin + count)
        for tile in range(tiles):
            here = read(0, tile, block).astype(F32) + read(1, tile, block).astype(F32)
            value = applied[tile * count:(tile + 1) * count] + (MASS_SHIFT - shift) * here
            for part, half in enumerate(halves(value)):
                inner_ref[step, part, tile, block, :] = half


def sides_kernel(slots, pos_ref, core_ref, chip_ref, field_ref, inner_ref, weights_ref, mixer_ref,
                 blocks_ref, geo_ref, first_ref, basis_ref, moments_ref, v_refs, meta_refs, stencil, buckets):
    tiles, rows = field_ref.shape[1:3]
    width = tiles * TILE
    dof = blocks_ref.shape[1]
    cases = width // dof
    edge = ITERS * HALO
    outer = edge - HALO
    count = edge
    shift = basis_shift(blocks_ref[...], slots)
    even = lax.rem(pos_ref[0, 0], jnp.int32(2)) == 0

    for tile in range(tiles + 1):
        lanes = slice(tile * TILE, (tile + 1) * TILE) if tile < tiles else slice(width, None)
        core, chip = core_ref[:, lanes], chip_ref[:, lanes]
        for side, value in enumerate((jnp.where(even, chip, core), jnp.where(even, core, chip))):
            if tile == tiles:
                meta_refs[side] = value
            else:
                for part, half in enumerate(halves(value)):
                    v_refs[0, side, part, tile] = half

    def build(side):
        for first in range(0, outer, HALO):
            start = first + HALO * (1 - side)
            spot = first + HALO if side == 0 else first + rows - edge
            for kind, value in enumerate(
                stencil_rows(meta_refs[side, start:start + HALO, :], slots, spot)
            ):
                stencil[side, kind, first:first + HALO, :] = value

    reach = count + 2 * HALO

    def window(step, side, part, tile):
        near = v_refs[step, side, part, tile]
        begin = HALO * step
        if side == 0:
            block = slice(begin, begin + reach - count)
        else:
            block = slice(rows - begin - (reach - count), rows - begin)
        if step == 0:
            far = field_ref[part, tile, block, :]
        else:
            far = inner_ref[step - 1, part, tile, block, :]
        return jnp.concatenate([near, far] if side == 0 else [far, near], axis=0)

    def weight_rows(step, side, kind):
        keep = outer - HALO * step
        if side == 0:
            pieces = [weights_ref[0, kind, :count - keep, :]]
            if keep:
                pieces.insert(0, stencil[0, kind, outer - keep:, :])
        else:
            pieces = [weights_ref[1, kind, keep:, :]]
            if keep:
                pieces.append(stencil[1, kind, :keep, :])
        rows_all = jnp.concatenate(pieces, axis=0)
        first = HALO * step if side == 0 else TILE - reach - HALO * step
        high = rows_all[:, first:first + reach]
        low = rows_all[:, 2 * TILE + first:2 * TILE + first + reach]
        blank = jnp.zeros((count, 2 * TILE - 3 * reach), BF16)
        return jnp.concatenate([high, high, low, blank], axis=1)

    def convert(step):
        begin = HALO * step
        for half in range(2):

            def piece(tile, part):
                lanes = slice(part * META, (part + 1) * META)
                return jnp.concatenate(
                    [
                        v_refs[step, 0, half, tile, count - begin:, lanes],
                        inner_ref[step - 1, half, tile, begin:rows - begin, lanes],
                        v_refs[step, 1, half, tile, :begin, lanes],
                    ],
                    axis=0,
                )

            for number, value in enumerate(swap_blocks(piece)):
                lanes = slice(number % 2 * META, (number % 2 + 1) * META)
                basis_ref[step - 1, half, number // 2, :, lanes] = value

    def tall(step, part):
        if step == 0:
            return jnp.concatenate([geo_ref[part, tile] for tile in range(tiles)], axis=0)
        return jnp.concatenate([basis_ref[step - 1, part, tile] for tile in range(tiles)], axis=0)

    def even_gram(high):
        cross = high[:, TILE:]
        return folded_rows(high[:, :TILE] + cross + cross.T, cases)

    sums = [first_ref[...]]
    for step in range(ITERS):
        centres = []
        for side in range(2):
            if step == 0:
                build(side)
            weights = jnp.concatenate(
                [weight_rows(step, side, kind) for kind in range(TYPES)], axis=0
            )
            for tile in range(tiles):
                row = (side * tiles + tile) * count
                near, fine = (window(step, side, part, tile) for part in range(2))
                centres.append((near[HALO:HALO + count], fine[HALO:HALO + count]))
                for part, half in enumerate(gathered(weights, near, fine)):
                    for kind in range(TYPES):
                        buckets[part, kind, row:row + count, :] = (
                            half[kind * count:(kind + 1) * count]
                        )
        applied = mixed(buckets, mixer_ref, 2 * tiles * count)
        for side in range(2):
            for tile in range(tiles):
                number = side * tiles + tile
                near, fine = centres[number]
                here = near.astype(F32) + fine.astype(F32)
                value = applied[number * count:(number + 1) * count] + (MASS_SHIFT - shift) * here
                for part, half in enumerate(halves(value)):
                    v_refs[step + 1, side, part, tile] = half

        convert(step + 1)
        if step == 0:
            flat = [tall(1, part).T for part in range(2)]
            left = jnp.concatenate(flat, axis=0)
            high = dot(left, tall(0, 0))
            fine = dot(
                flat[0], jnp.concatenate([tall(0, 1), tall(1, 0), tall(1, 1)], axis=1)
            )
            sums.append(folded_rows(high[:TILE] + high[TILE:] + fine[:, :TILE], cases))
            sums.append(even_gram(fine[:, TILE:]))
        elif step == 1:
            next_flat = [tall(2, part).T for part in range(2)]
            high = dot(jnp.concatenate([flat[0], next_flat[0], flat[1]], axis=0), tall(2, 0))
            fine = dot(jnp.concatenate([flat[0], next_flat[0]], axis=0), tall(2, 1))
            sums.append(folded_rows(high[:TILE] + high[2 * TILE:] + fine[:TILE], cases))
            sums.append(
                even_gram(jnp.concatenate([high[TILE:2 * TILE], fine[TILE:]], axis=1))
            )
        else:
            high = dot(jnp.concatenate(next_flat, axis=0), tall(3, 0))
            fine = dot(next_flat[0], tall(3, 1))
            sums.append(folded_rows(high[:TILE] + high[TILE:] + fine, cases))

    remainder = jnp.concatenate(sums, axis=0)
    pieces = []
    for _ in range(3):
        pieces.append(remainder.astype(BF16))
        remainder = remainder - pieces[-1].astype(F32)
    collect = one_hot(iota((TILE, META), 0) // 16 == iota((TILE, META), 1) % 16)
    folded = dot(jnp.concatenate(pieces, axis=1), jnp.concatenate([collect] * 3, axis=0))
    group = iota((cases, META), 1) // cases
    moments = jnp.zeros((cases, META), F32)
    for number in range(2 * ITERS):
        part = folded[number * cases:(number + 1) * cases]
        moments = jnp.where(group == number, part, moments)
    moments_ref[...] = moments


def refined_reciprocal(value):
    guess = pl.reciprocal(value, approx=True)
    for _ in range(2):
        guess = guess * (2.0 - value * guess)
    return guess


def finish_kernel(slots, blocks_ref, geo_ref, basis_ref, *refs):
    moment_refs = refs[:-4]
    solution_hbm, residual_hbm, out_refs, sems = refs[-4:]
    rows, width = out_refs.shape[1:]
    dof = blocks_ref.shape[1]
    cases = width // dof
    tiles = width // TILE
    shift = basis_shift(blocks_ref[...], slots)
    moments = moment_refs[0][...]
    for ref in moment_refs[1:]:
        moments = moments + ref[...]
    group = iota((cases, META), 1) // cases
    system = []
    for row in range(ITERS):
        plain = moments if row == 0 else pltpu.roll(moments, META - cases * row, 1)
        ahead = pltpu.roll(moments, META - cases * (row + 1), 1)
        target = pltpu.roll(moments, cases * (ITERS - row), 1)
        system.append(jnp.where(group < ITERS, ahead + shift * plain, target))
    system = jnp.concatenate(system, axis=0)
    size = ITERS * cases
    index = iota((size, 1), 0)
    for pivot in range(0, size, 2):
        column_a = jnp.broadcast_to(system[:, pivot:pivot + 1], (size, META))
        column_b = jnp.broadcast_to(system[:, pivot + 1:pivot + 2], (size, META))
        line_a = system[pivot:pivot + 1, :]
        line_b = system[pivot + 1:pivot + 2, :]
        above = column_b[pivot:pivot + 1, :]
        inverse = refined_reciprocal(column_a[pivot:pivot + 1, :])
        factor = column_a[pivot + 1:pivot + 2, :] * inverse
        corner = column_b[pivot + 1:pivot + 2, :] - factor * above
        line_b = (line_b - factor * line_a) * refined_reciprocal(corner)
        line_a = (line_a - above * line_b) * inverse
        update = system - column_a * line_a - column_b * line_b
        system = jnp.where(index == pivot, line_a, jnp.where(index == pivot + 1, line_b, update))

    unit = jnp.where(iota((cases, META), 1) % cases == iota((cases, META), 0), 1.0, 0.0)
    answers = []
    for row in range(ITERS):
        part = jnp.where(group == ITERS, system[row * cases:(row + 1) * cases], 0.0)
        step = cases
        while step < META:
            part = part + pltpu.roll(part, step, 1)
            step *= 2
        answers.append(part)
    left_over = [unit - shift * answers[0]]
    for row in range(1, ITERS):
        left_over.append(-(answers[row - 1] + shift * answers[row]))
    left_over.append(-answers[ITERS - 1])

    meets = iota((TILE, TILE), 0) % 16 == iota((TILE, TILE), 1) // 16

    def spread(parts):
        highs, lows = [], []
        for part in parts:
            tall = jnp.broadcast_to(part[:, None, :], (cases, TILE // cases, META))
            tall = tall.reshape(TILE, META)
            wide = jnp.concatenate([tall] * (TILE // META), axis=1)
            high, low = halves(jnp.where(meets, wide, 0.0))
            highs.append(high)
            lows.append(low)
        return jnp.concatenate(highs + highs + lows, axis=0)

    def tall(term, part):
        if term == 0:
            return jnp.concatenate([geo_ref[part, tile] for tile in range(tiles)], axis=0)
        return jnp.concatenate([basis_ref[term - 1, part, tile] for tile in range(tiles)], axis=0)

    copies = []
    for number, (out_hbm, parts) in enumerate(
        ((solution_hbm, answers), (residual_hbm, left_over))
    ):
        matrix = spread(parts)
        terms = matrix.shape[0] // (3 * TILE)
        highs = [tall(term, 0) for term in range(terms)]
        lows = [tall(term, 1) for term in range(terms)]
        value = dot(jnp.concatenate(highs + lows + highs, axis=1), matrix)
        for tile in range(tiles):
            lanes = slice(tile * TILE, (tile + 1) * TILE)
            out_refs[number, :, lanes] = value[tile * rows:(tile + 1) * rows]
        copies.append(pltpu.make_async_copy(out_refs.at[number], out_hbm, sems.at[number]))
        copies[number].start()
    for copy in copies:
        copy.wait()


def on_device(loads, row_ids, densities, block_cols, block_types, ref_blocks):
    rows, width = loads.shape
    slots = densities.shape[1]
    cases = width // ref_blocks.shape[1]
    cap = rows // 4
    edge = ITERS * HALO
    tiles = width // TILE
    devices = lax.axis_size("sub")
    position = lax.axis_index("sub").astype(jnp.int32).reshape(1, 1)
    shape = jax.ShapeDtypeStruct
    same_chip = [(i, i ^ 1) for i in range(devices)]
    next_chip = [(i, i + 1) for i in range(1, devices - 1, 2)]
    next_chip += [(i + 1, i) for i in range(1, devices - 1, 2)]
    neighbour = dict(next_chip)
    rounds = [[], []]
    for i in range(devices):
        early = 0 if far_first(i, devices) else 1
        rounds[early].append((i, (i + devices // 2) % devices))
        if i in neighbour:
            rounds[1 - early].append((i, neighbour[i]))

    block = shape((cap * width // META + cap // 2, META), F32)
    to_first, meta, target = pl.pallas_call(
        functools.partial(pack_first_kernel, devices),
        out_shape=(block, shape((META, rows), F32), shape((8, rows), jnp.int32)),
        in_specs=[SMEM] + [HBM] * 5,
        out_specs=(VMEM,) * 3,
        scratch_shapes=[
            pltpu.VMEM((rows, width), F32),
            pltpu.VMEM((1, rows), jnp.int32),
            pltpu.VMEM((slots, rows), F32),
            pltpu.VMEM((slots, rows), jnp.int32),
            pltpu.VMEM((slots, rows), jnp.int32),
            pltpu.SemaphoreType.DMA((5,)),
        ],
        compiler_params=PACK_PARAMS,
        name="pack_first",
    )(position, loads, row_ids.reshape(1, rows), densities.T, block_cols.T, block_types.T)
    from_first = lax.ppermute(to_first, "sub", rounds[0])

    to_core, to_second = pl.pallas_call(
        functools.partial(pack_second_kernel, devices),
        out_shape=(block, block),
        in_specs=[SMEM] + [HBM] * 3,
        out_specs=(VMEM,) * 2,
        scratch_shapes=[
            pltpu.VMEM((8, rows), jnp.int32),
            pltpu.VMEM((META, rows), F32),
            pltpu.VMEM((rows, width), F32),
            pltpu.SemaphoreType.DMA((3,)),
        ],
        compiler_params=PACK_PARAMS,
        name="pack_second",
    )(position, target, meta, loads)
    from_second = lax.ppermute(to_second, "sub", rounds[1])
    from_core = lax.ppermute(to_core, "sub", same_chip)

    mixer_shape = shape((3 * TYPES * TILE, TILE), BF16)
    kept, kept_meta, mixer, first = pl.pallas_call(
        functools.partial(prepare_kernel, slots),
        out_shape=(
            shape((rows, width), F32),
            shape((rows, META), F32),
            mixer_shape,
            shape((cases, TILE), F32),
        ),
        in_specs=[VMEM] * 3,
        out_specs=(VMEM,) * 4,
        compiler_params=PARAMS,
        cost_estimate=pl.CostEstimate(
            flops=4_000_000_000, bytes_accessed=4_000_000, transcendentals=0
        ),
        name="prepare",
    )(loads, meta, ref_blocks)

    border = shape((edge, width + META), F32)
    pair = shape((2, tiles, rows, TILE), BF16)
    geo, field, geo_meta, to_core, to_chip = pl.pallas_call(
        functools.partial(arrange_kernel, slots),
        out_shape=(pair, pair, shape((rows, META), F32), border, border),
        in_specs=[SMEM] + [VMEM] * 5,
        out_specs=(VMEM,) * 5,
        compiler_params=PARAMS,
        name="arrange",
    )(position, kept, kept_meta, from_core, from_first, from_second)

    halo_chip = lax.ppermute(to_chip, "sub", next_chip)
    halo_core = lax.ppermute(to_core, "sub", same_chip)

    basis_shape = shape((ITERS, 2, tiles, rows, TILE), BF16)
    inner, weights = pl.pallas_call(
        functools.partial(interior_kernel, slots),
        out_shape=(basis_shape, shape((2, TYPES, edge, 3 * TILE), BF16)),
        in_specs=[VMEM] * 4,
        out_specs=(VMEM,) * 2,
        scratch_shapes=[
            pltpu.VMEM((TYPES, rows - 2 * HALO, 3 * TILE), BF16),
            pltpu.VMEM((2, TYPES, tiles * (rows - 2 * HALO), TILE), BF16),
        ],
        compiler_params=PARAMS,
        cost_estimate=pl.CostEstimate(
            flops=10_000_000_000, bytes_accessed=8_000_000, transcendentals=0
        ),
        name="interior",
    )(field, geo_meta, mixer, ref_blocks)

    basis, moments = pl.pallas_call(
        functools.partial(sides_kernel, slots),
        out_shape=(basis_shape, shape((cases, META), F32)),
        in_specs=[SMEM] + [VMEM] * 9,
        out_specs=(VMEM,) * 2,
        scratch_shapes=[
            pltpu.VMEM((ITERS + 1, 2, 2, tiles, edge, TILE), BF16),
            pltpu.VMEM((2, edge, META), F32),
            pltpu.VMEM((2, TYPES, edge - HALO, 3 * TILE), BF16),
            pltpu.VMEM((2, TYPES, 2 * tiles * edge, TILE), BF16),
        ],
        compiler_params=PARAMS,
        name="sides",
    )(position, halo_core, halo_chip, field, inner, weights, mixer, ref_blocks, geo, first)

    bits = devices.bit_length() - 1
    gathered_moments = [moments]
    for low, high in ((0, 1), (1, bits // 2), (bits // 2, bits)):
        partial = sum(gathered_moments[1:], gathered_moments[0])
        gathered_moments = [partial]
        for mask in range(1, 1 << (high - low)):
            swap = [(i, i ^ (mask << low)) for i in range(devices)]
            gathered_moments.append(lax.ppermute(partial, "sub", swap))

    return pl.pallas_call(
        functools.partial(finish_kernel, slots),
        out_shape=(shape((rows, width), F32), shape((rows, width), F32)),
        in_specs=[VMEM] * (3 + len(gathered_moments)),
        out_specs=(HBM,) * 2,
        scratch_shapes=[pltpu.VMEM((2, rows, width), F32), pltpu.SemaphoreType.DMA((2,))],
        compiler_params=PARAMS,
        name="finish",
    )(ref_blocks, geo, basis, *gathered_moments)


def solution(mesh):
    placed = (
        P(("groups", "sub"), None),
        P(("groups", "sub")),
        P(("groups", "sub"), None),
        P(("groups", "sub"), None),
        P(("groups", "sub"), None),
        P(),
    )
    return jax.shard_map(
        on_device,
        mesh=mesh,
        in_specs=placed,
        out_specs=(P(("groups", "sub"), None), P(("groups", "sub"), None)),
        check_vma=False,
    )
```

```python
import functools

import jax
import jax.numpy as jnp
from jax import lax
from jax.experimental import pallas as pl
from jax.experimental.pallas import tpu as pltpu
from jax.sharding import PartitionSpec as P

HALO = 32
TYPES = 3
ITERS = 3
MASS_SHIFT = 0.5
META = 128
TILE = 256

F32 = jnp.float32
BF16 = jnp.bfloat16
VMEM = pl.BlockSpec(memory_space=pltpu.VMEM)
SMEM = pl.BlockSpec(memory_space=pltpu.SMEM)
HBM = pl.BlockSpec(memory_space=pltpu.HBM)
PARAMS = pltpu.CompilerParams(vmem_limit_bytes=40 * 1024 * 1024)


def dot(left, right):
    return jnp.dot(left, right, preferred_element_type=F32)


def dot_nt(left, right):
    return lax.dot_general(left, right, (((1,), (1,)), ((), ())), preferred_element_type=F32)


def dot_tn(left, right):
    return lax.dot_general(left, right, (((0,), (0,)), ((), ())), preferred_element_type=F32)


def halves(value):
    high = value.astype(BF16)
    return high, (value - high.astype(F32)).astype(BF16)


def iota(shape, axis):
    return lax.broadcasted_iota(jnp.int32, shape, axis)


def one_hot(condition):
    return jnp.where(condition, 1.0, 0.0).astype(BF16)


PACK_PARAMS = pltpu.CompilerParams(vmem_limit_bytes=62 * 1024 * 1024)


def basis_shift(blocks, slots):
    dof = blocks.shape[1]
    same = iota((dof, dof), 0) == iota((dof, dof), 1)
    total = sum(jnp.where(same, blocks[t], 0.0) for t in range(TYPES))
    mean = jnp.sum(jnp.sum(total, axis=1, keepdims=True), axis=0, keepdims=True) / (TYPES * dof)
    return MASS_SHIFT + 0.2 * slots * mean


def swap_blocks(piece):
    lane = iota(piece(0, 0).shape, 1)
    low = lane < META // 2
    out = []
    for tile in range(4):
        for part in range(2):
            first, second = piece(2 * part, tile // 2), piece(2 * part + 1, tile // 2)
            if tile % 2 == 0:
                second = pltpu.roll(second, META // 2, 1)
            else:
                first = pltpu.roll(first, META // 2, 1)
            out.append(jnp.where(low, first, second))
    return out


def given_to_gram():
    source, target = iota((TILE, TILE), 0), iota((TILE, TILE), 1)
    return one_hot((target // 16 == source % 16) & (target % 16 == source // 16))


def peers(pos, devices):
    odd = lax.rem(pos, jnp.int32(2))
    return (
        pos + 1 - 2 * odd,
        pos - 1 + 2 * odd,
        lax.rem(pos + devices // 2, jnp.int32(devices)),
    )


def far_first(pos, devices):
    half = devices // 2
    group = (pos % half + 1) // 2 % max(half // 2, 1)
    return group % 2 == 1


def targets(pos, ids, rows, devices):
    cap = rows // 4
    owner = lax.div(ids, jnp.int32(rows))
    goes = []
    for peer in peers(pos, devices):
        here = owner == peer
        for other in goes:
            here = here & ~other
        goes.append(here)
    flags = jnp.concatenate(
        [jnp.where(g, 1.0, 0.0) for g in goes] + [jnp.zeros((5, rows), F32)], axis=0
    )
    before = one_hot(iota((rows, rows), 0) < iota((rows, rows), 1))
    rank = dot(flags.astype(BF16), before).astype(jnp.int32)
    target = jnp.full((1, rows), -1, jnp.int32)
    for side in range(3):
        target = jnp.where(goes[side], rank[side:side + 1] + side * cap, target)
    return target


def fill_block(pick, loads, meta, out_ref):
    width = loads.shape[1]
    cap = pick.shape[0]
    twice = jnp.concatenate([pick, pick], axis=1)
    notes = dot_nt(twice, jnp.concatenate(halves(meta), axis=1))
    body = dot(twice, jnp.concatenate(halves(loads), axis=0))
    parts = width // META
    for part in range(parts):
        out_ref[part * cap:(part + 1) * cap, :] = body[:, part * META:(part + 1) * META]
    out_ref[parts * cap:, :] = notes[:cap // 2] + pltpu.roll(notes[cap // 2:], META // 2, 1)


def read_block(ref, width):
    parts = width // META
    cap = ref.shape[0] * 2 // (2 * parts + 1)
    body = jnp.concatenate([ref[part * cap:(part + 1) * cap, :] for part in range(parts)], axis=1)
    notes = ref[parts * cap:, :]
    notes = jnp.concatenate([notes, pltpu.roll(notes, META // 2, 1)], axis=0)
    return body, jnp.where(iota(notes.shape, 1) < META // 2, notes, 0.0)


def pack_first_kernel(devices, pos_ref, loads_hbm, rows_hbm, dens_hbm, cols_hbm, types_hbm,
                      first_ref, meta_ref, target_ref,
                      loads_ref, rows_ref, dens_ref, cols_ref, types_ref, sems):
    pairs = (
        (rows_hbm, rows_ref), (dens_hbm, dens_ref), (cols_hbm, cols_ref),
        (types_hbm, types_ref), (loads_hbm, loads_ref),
    )
    copies = [
        pltpu.make_async_copy(source, target, sems.at[number])
        for number, (source, target) in enumerate(pairs)
    ]
    for copy in copies:
        copy.start()
    for copy in copies[:4]:
        copy.wait()
    rows = loads_ref.shape[0]
    slots = dens_ref.shape[0]
    cap = rows // 4
    pos = pos_ref[0, 0]
    ids = rows_ref[...]
    owner = lax.div(ids, jnp.int32(rows))
    local = (ids - owner * rows + 1).astype(F32)
    target = targets(pos, ids, rows, devices)
    target_ref[...] = jnp.broadcast_to(target, target_ref.shape)

    density = dens_ref[...]
    kinds = types_ref[...]
    for kind in range(TYPES):
        meta_ref[kind * slots:(kind + 1) * slots, :] = jnp.where(kinds == kind, density, 0.0)
    meta_ref[3 * slots:4 * slots, :] = (cols_ref[...] - ids).astype(F32)
    meta_ref[4 * slots:, :] = jnp.zeros((META - 4 * slots, rows), F32)
    meta_ref[4 * slots:4 * slots + 1, :] = local
    meta_ref[4 * slots + 1:4 * slots + 2, :] = jnp.where(owner == pos, local, 0.0)

    copies[4].wait()
    side = jnp.where(far_first(pos, devices), 2, 1)
    pick = one_hot(iota((cap, rows), 0) + side * cap == target)
    fill_block(pick, loads_ref[...], meta_ref[...], first_ref)


def pack_second_kernel(devices, pos_ref, target_hbm, meta_hbm, loads_hbm, core_ref, second_ref,
                       target_ref, meta_ref, loads_ref, sems):
    pairs = ((target_hbm, target_ref), (meta_hbm, meta_ref), (loads_hbm, loads_ref))
    copies = [
        pltpu.make_async_copy(source, target, sems.at[number])
        for number, (source, target) in enumerate(pairs)
    ]
    for copy in copies:
        copy.start()
    for copy in copies:
        copy.wait()
    rows = loads_ref.shape[0]
    cap = rows // 4
    late = jnp.where(far_first(pos_ref[0, 0], devices), 1, 2)
    for side, out_ref in ((late, second_ref), (0, core_ref)):
        pick = one_hot(iota((cap, rows), 0) + side * cap == target_ref[0:1, :])
        fill_block(pick, loads_ref[...], meta_ref[...], out_ref)


def reorder(parts, tiles):
    count = parts[0].shape[0]
    tall = [p[:, t * TILE:(t + 1) * TILE] for t in range(tiles) for p in parts]
    moved = dot(jnp.concatenate(tall, axis=0), given_to_gram()).astype(BF16)
    return [
        jnp.concatenate(
            [moved[(2 * t + p) * count:(2 * t + p + 1) * count] for t in range(tiles)], axis=1
        )
        for p in range(2)
    ]


def stacked_tiles(value, tiles):
    return jnp.concatenate([value[:, t * TILE:(t + 1) * TILE] for t in range(tiles)], axis=0)


def folded_rows(gram, cases):
    same_dof = iota((TILE, TILE), 0) % 16 == iota((TILE, TILE), 1) % 16
    gram = jnp.where(same_dof, gram, 0.0)
    return jnp.sum(gram.reshape(cases, TILE // cases, TILE), axis=1)


def prepare_kernel(slots, loads_ref, meta_ref, blocks_ref,
                   kept_ref, kept_meta_ref, mixer_ref, first_ref):
    rows, width = loads_ref.shape
    dof = blocks_ref.shape[1]
    tiles = width // TILE
    place = iota((rows, rows), 0) + 1
    own = one_hot(place == meta_ref[4 * slots + 1:4 * slots + 2, :].astype(jnp.int32))
    twice = jnp.concatenate([own, own], axis=1)
    moved = reorder(halves(loads_ref[...]), tiles)
    kept_ref[...] = dot(twice, jnp.concatenate(moved, axis=0))
    high, low = (stacked_tiles(part, tiles) for part in moved)
    gram = dot_tn(high, jnp.concatenate([high, low], axis=1))
    cross = gram[:, TILE:]
    first_ref[...] = folded_rows(gram[:, :TILE] + cross + cross.T, width // dof)
    kept_meta_ref[...] = dot_nt(twice, jnp.concatenate(halves(meta_ref[...]), axis=1))

    def dof_of(lane):
        return lane // 64 * 16 + lane % 16

    fold = one_hot(dof_of(iota((TILE, dof), 0)) == iota((TILE, dof), 1))
    unfold = one_hot(dof_of(iota((dof, TILE), 1)) == iota((dof, TILE), 0))
    same_case = iota((TILE, TILE), 0) // 16 % 4 == iota((TILE, TILE), 1) // 16 % 4
    for kind in range(TYPES):
        for copies, part in zip(((0, 2), (1,)), halves(blocks_ref[kind])):
            wide = dot(dot_nt(fold, part).astype(BF16), unfold)
            wide = jnp.where(same_case, wide, 0.0).astype(BF16)
            for copy in copies:
                start = (copy * TYPES + kind) * TILE
                mixer_ref[start:start + TILE, :] = wide


def arrange_kernel(slots, pos_ref, first_ref, second_ref, core_ref, kept_ref, kept_meta_ref,
                   geo_ref, field_ref, meta_ref, to_core_ref, to_chip_ref):
    rows, width = kept_ref.shape
    tiles = width // TILE
    edge = to_core_ref.shape[0]
    even = lax.rem(pos_ref[0, 0], jnp.int32(2)) == 0
    blocks = [read_block(ref, width) for ref in (first_ref, second_ref, core_ref)]
    arrived = jnp.concatenate([block[0] for block in blocks], axis=0)
    arrived_meta = jnp.concatenate([block[1] for block in blocks], axis=0)
    count = arrived.shape[0]
    unit = one_hot(iota((8, META), 1) == 4 * slots)
    tags = dot_nt(unit, arrived_meta.astype(BF16))[0:1]
    other = one_hot(iota((rows, count), 0) + 1 == tags.astype(jnp.int32))
    twice = jnp.concatenate([other, other], axis=1)
    moved = reorder(halves(arrived), tiles)
    geo = kept_ref[...] + dot(twice, jnp.concatenate(moved, axis=0))
    meta = kept_meta_ref[...] + dot(twice, jnp.concatenate(halves(arrived_meta), axis=0))
    meta_ref[...] = meta

    def send(lanes, value):
        head, tail = value[:edge], value[rows - edge:]
        to_core_ref[:, lanes] = jnp.where(even, tail, head)
        to_chip_ref[:, lanes] = jnp.where(even, head, tail)

    send(slice(width, None), meta)

    def piece(tile, part):
        start = tile * TILE + part * META
        return geo[:, start:start + META]

    for number, value in enumerate(swap_blocks(piece)):
        lanes = slice(number * META, (number + 1) * META)
        send(lanes, value)
        inner = slice(number % 2 * META, (number % 2 + 1) * META)
        for part, half in enumerate(halves(value)):
            field_ref[part, number // 2, :, inner] = half
    for part, half in enumerate(halves(geo)):
        for tile in range(tiles):
            geo_ref[part, tile] = half[:, tile * TILE:(tile + 1) * TILE]


def stencil_rows(meta, slots, first):
    lane = iota((HALO, META), 1)
    spot = iota((HALO, TILE), 1)
    centre = iota((HALO, 1), 0) + first
    sums = [jnp.zeros((HALO, TILE), F32) for _ in range(TYPES)]
    for slot in range(slots):
        column = centre + meta[:, 3 * slots + slot:3 * slots + slot + 1].astype(jnp.int32)
        hit = spot == column
        for kind in range(TYPES):
            weight = meta[:, kind * slots + slot:kind * slots + slot + 1]
            sums[kind] += jnp.where(hit, weight, 0.0)
    out = []
    for kind in range(TYPES):
        inside = (lane >= kind * slots) & (lane < (kind + 1) * slots)
        total = jnp.sum(jnp.where(inside, meta, 0.0), axis=1, keepdims=True)
        high, low = halves(jnp.where(spot == centre, total, 0.0) - sums[kind])
        out.append(jnp.concatenate([high, high, low], axis=1))
    return out


def gathered(weights, near, fine):
    return halves(dot(weights, jnp.concatenate([near, fine, near], axis=0)))


def mixed(buckets, mixer_ref, count):
    highs = [buckets[0, kind, :count, :] for kind in range(TYPES)]
    lows = [buckets[1, kind, :count, :] for kind in range(TYPES)]
    return dot(jnp.concatenate(highs + highs + lows, axis=1), mixer_ref[...])


def interior_kernel(slots, field_ref, meta_ref, mixer_ref, blocks_ref,
                    inner_ref, weights_ref, stencil, buckets):
    tiles, rows = field_ref.shape[1:3]
    edge = ITERS * HALO
    shift = basis_shift(blocks_ref[...], slots)
    inside = rows - 2 * HALO

    def build(chunk, carry):
        first = pl.multiple_of(chunk * HALO, HALO)
        start = pl.multiple_of(chunk * HALO + HALO, HALO)
        for kind, value in enumerate(
            stencil_rows(meta_ref[pl.ds(start, HALO), :], slots, first + HALO)
        ):
            stencil[kind, pl.ds(first, HALO), :] = value
        return carry

    lax.fori_loop(0, inside // HALO, build, 0)

    def build_outer(side, chunk):
        first = chunk * HALO
        start = first + side * (rows - edge)
        spot = first + edge if side == 0 else first + rows - 2 * edge
        for kind, value in enumerate(stencil_rows(meta_ref[start:start + HALO, :], slots, spot)):
            weights_ref[side, kind, first:first + HALO, :] = value

    for step in range(ITERS - 1):
        begin = HALO * (step + 1)
        blank = jnp.zeros((begin, TILE), BF16)
        for part in range(2):
            for tile in range(tiles):
                inner_ref[step, part, tile, :begin, :] = blank
                inner_ref[step, part, tile, rows - begin:, :] = blank
    for step in range(ITERS):
        skip = HALO * step
        count = inside - 2 * skip
        begin = HALO + skip
        weights = jnp.concatenate(
            [stencil[kind, skip:inside - skip, :] for kind in range(TYPES)], axis=0
        )

        def read(part, tile, block):
            if step == 0:
                return field_ref[part, tile, block, :]
            return inner_ref[step - 1, part, tile, block, :]

        for tile in range(tiles):
            every = slice(0, rows)
            for part, half in enumerate(
                gathered(weights, read(0, tile, every), read(1, tile, every))
            ):
                for kind in range(TYPES):
                    buckets[part, kind, tile * count:(tile + 1) * count, :] = (
                        half[kind * count:(kind + 1) * count]
                    )
        for side in range(2):
            build_outer(side, step)
        applied = mixed(buckets, mixer_ref, tiles * count)
        block = slice(begin, begin + count)
        for tile in range(tiles):
            here = read(0, tile, block).astype(F32) + read(1, tile, block).astype(F32)
            value = applied[tile * count:(tile + 1) * count] + (MASS_SHIFT - shift) * here
            for part, half in enumerate(halves(value)):
                inner_ref[step, part, tile, block, :] = half


def sides_kernel(slots, pos_ref, core_ref, chip_ref, field_ref, inner_ref, weights_ref, mixer_ref,
                 blocks_ref, geo_ref, first_ref, basis_ref, moments_ref, v_refs, meta_refs, stencil, buckets):
    tiles, rows = field_ref.shape[1:3]
    width = tiles * TILE
    dof = blocks_ref.shape[1]
    cases = width // dof
    edge = ITERS * HALO
    outer = edge - HALO
    count = edge
    rest = TILE - edge
    shift = basis_shift(blocks_ref[...], slots)
    even = lax.rem(pos_ref[0, 0], jnp.int32(2)) == 0

    for tile in range(tiles + 1):
        lanes = slice(tile * TILE, (tile + 1) * TILE) if tile < tiles else slice(width, None)
        core, chip = core_ref[:, lanes], chip_ref[:, lanes]
        for side, value in enumerate((jnp.where(even, chip, core), jnp.where(even, core, chip))):
            if tile == tiles:
                meta_refs[side] = value
            else:
                for part, half in enumerate(halves(value)):
                    v_refs[0, side, part, tile] = half

    def build(side):
        for first in range(0, outer, HALO):
            start = first + HALO * (1 - side)
            spot = first + HALO if side == 0 else first + rows - edge
            for kind, value in enumerate(
                stencil_rows(meta_refs[side, start:start + HALO, :], slots, spot)
            ):
                stencil[side, kind, first:first + HALO, :] = value

    def window(step, side, part, tile):
        near = v_refs[step, side, part, tile]
        if step == 0:
            if side == 0:
                return jnp.concatenate([near, field_ref[part, tile, :rest, :]], axis=0)
            return jnp.concatenate([field_ref[part, tile, rows - rest:, :], near], axis=0)
        blank = jnp.zeros((HALO * step, TILE), BF16)
        begin = HALO * step
        if side == 0:
            far = inner_ref[step - 1, part, tile, begin:rest, :]
            return jnp.concatenate([blank, near, far], axis=0)
        far = inner_ref[step - 1, part, tile, rows - rest:rows - begin, :]
        return jnp.concatenate([far, near, blank], axis=0)

    def weight_rows(step, side, kind):
        keep = outer - HALO * step
        if side == 0:
            pieces = [weights_ref[0, kind, :count - keep, :]]
            if keep:
                pieces.insert(0, stencil[0, kind, outer - keep:, :])
        else:
            pieces = [weights_ref[1, kind, keep:, :]]
            if keep:
                pieces.append(stencil[1, kind, :keep, :])
        return jnp.concatenate(pieces, axis=0)

    def convert(step):
        begin = HALO * step
        for half in range(2):

            def piece(tile, part):
                lanes = slice(part * META, (part + 1) * META)
                return jnp.concatenate(
                    [
                        v_refs[step, 0, half, tile, count - begin:, lanes],
                        inner_ref[step - 1, half, tile, begin:rows - begin, lanes],
                        v_refs[step, 1, half, tile, :begin, lanes],
                    ],
                    axis=0,
                )

            for number, value in enumerate(swap_blocks(piece)):
                lanes = slice(number % 2 * META, (number % 2 + 1) * META)
                basis_ref[step - 1, half, number // 2, :, lanes] = value

    def tall(step, part):
        if step == 0:
            return jnp.concatenate([geo_ref[part, tile] for tile in range(tiles)], axis=0)
        return jnp.concatenate([basis_ref[step - 1, part, tile] for tile in range(tiles)], axis=0)

    def mixed_gram(high, low):
        return folded_rows(high[:, :TILE] + high[:, TILE:] + low, cases)

    def even_gram(high):
        cross = high[:, TILE:]
        return folded_rows(high[:, :TILE] + cross + cross.T, cases)

    sums = [first_ref[...]]
    for step in range(ITERS):
        centres = []
        for side in range(2):
            if step == 0:
                build(side)
            weights = jnp.concatenate(
                [weight_rows(step, side, kind) for kind in range(TYPES)], axis=0
            )
            for tile in range(tiles):
                row = (side * tiles + tile) * count
                near, fine = (window(step, side, part, tile) for part in range(2))
                first = HALO * (step + 1) if side == 0 else TILE - HALO * (step + 1) - count
                centres.append((near[first:first + count], fine[first:first + count]))
                for part, half in enumerate(gathered(weights, near, fine)):
                    for kind in range(TYPES):
                        buckets[part, kind, row:row + count, :] = (
                            half[kind * count:(kind + 1) * count]
                        )
        applied = mixed(buckets, mixer_ref, 2 * tiles * count)
        for side in range(2):
            for tile in range(tiles):
                number = side * tiles + tile
                near, fine = centres[number]
                here = near.astype(F32) + fine.astype(F32)
                value = applied[number * count:(number + 1) * count] + (MASS_SHIFT - shift) * here
                for part, half in enumerate(halves(value)):
                    v_refs[step + 1, side, part, tile] = half

        convert(step + 1)
        if step == 1:
            others = [tall(k, part) for k in range(3) for part in range(2)]
            high = dot_tn(tall(1, 0), jnp.concatenate(others, axis=1))
            low = dot_tn(tall(1, 1), jnp.concatenate([others[0], others[4]], axis=1))
            sums.append(mixed_gram(high[:, :2 * TILE], low[:, :TILE]))
            sums.append(even_gram(high[:, 2 * TILE:4 * TILE]))
            sums.append(mixed_gram(high[:, 4 * TILE:], low[:, TILE:]))
        elif step == 2:
            others = [tall(k, part) for k in range(2, 4) for part in range(2)]
            high = dot_tn(tall(2, 0), jnp.concatenate(others, axis=1))
            low = dot_tn(tall(2, 1), others[2])
            sums.append(even_gram(high[:, :2 * TILE]))
            sums.append(mixed_gram(high[:, 2 * TILE:], low))

    remainder = jnp.concatenate(sums, axis=0)
    pieces = []
    for _ in range(3):
        pieces.append(remainder.astype(BF16))
        remainder = remainder - pieces[-1].astype(F32)
    collect = one_hot(iota((TILE, META), 0) // 16 == iota((TILE, META), 1) % 16)
    folded = dot(jnp.concatenate(pieces, axis=1), jnp.concatenate([collect] * 3, axis=0))
    group = iota((cases, META), 1) // cases
    moments = jnp.zeros((cases, META), F32)
    for number in range(2 * ITERS):
        part = folded[number * cases:(number + 1) * cases]
        moments = jnp.where(group == number, part, moments)
    for device in range(moments_ref.shape[0]):
        moments_ref[device] = moments


def refined_reciprocal(value):
    guess = pl.reciprocal(value, approx=True)
    for _ in range(2):
        guess = guess * (2.0 - value * guess)
    return guess


def finish_kernel(slots, moments_ref, blocks_ref, geo_ref, basis_ref,
                  solution_hbm, residual_hbm, out_refs, sems):
    rows, width = out_refs.shape[1:]
    dof = blocks_ref.shape[1]
    cases = width // dof
    tiles = width // TILE
    shift = basis_shift(blocks_ref[...], slots)
    moments = moments_ref[0]
    for device in range(1, moments_ref.shape[0]):
        moments = moments + moments_ref[device]
    group = iota((cases, META), 1) // cases
    system = []
    for row in range(ITERS):
        plain = moments if row == 0 else pltpu.roll(moments, META - cases * row, 1)
        ahead = pltpu.roll(moments, META - cases * (row + 1), 1)
        target = pltpu.roll(moments, cases * (ITERS - row), 1)
        system.append(jnp.where(group < ITERS, ahead + shift * plain, target))
    system = jnp.concatenate(system, axis=0)
    size = ITERS * cases
    index = iota((size, 1), 0)
    for pivot in range(0, size, 2):
        column_a = jnp.broadcast_to(system[:, pivot:pivot + 1], (size, META))
        column_b = jnp.broadcast_to(system[:, pivot + 1:pivot + 2], (size, META))
        line_a = system[pivot:pivot + 1, :]
        line_b = system[pivot + 1:pivot + 2, :]
        above = column_b[pivot:pivot + 1, :]
        inverse = refined_reciprocal(column_a[pivot:pivot + 1, :])
        factor = column_a[pivot + 1:pivot + 2, :] * inverse
        corner = column_b[pivot + 1:pivot + 2, :] - factor * above
        line_b = (line_b - factor * line_a) * refined_reciprocal(corner)
        line_a = (line_a - above * line_b) * inverse
        update = system - column_a * line_a - column_b * line_b
        system = jnp.where(index == pivot, line_a, jnp.where(index == pivot + 1, line_b, update))

    unit = jnp.where(iota((cases, META), 1) % cases == iota((cases, META), 0), 1.0, 0.0)
    answers = []
    for row in range(ITERS):
        part = jnp.where(group == ITERS, system[row * cases:(row + 1) * cases], 0.0)
        step = cases
        while step < META:
            part = part + pltpu.roll(part, step, 1)
            step *= 2
        answers.append(part)
    left_over = [unit - shift * answers[0]]
    for row in range(1, ITERS):
        left_over.append(-(answers[row - 1] + shift * answers[row]))
    left_over.append(-answers[ITERS - 1])

    meets = iota((TILE, TILE), 0) % 16 == iota((TILE, TILE), 1) // 16

    def spread(parts):
        highs, lows = [], []
        for part in parts:
            tall = jnp.broadcast_to(part[:, None, :], (cases, TILE // cases, META))
            tall = tall.reshape(TILE, META)
            wide = jnp.concatenate([tall] * (TILE // META), axis=1)
            high, low = halves(jnp.where(meets, wide, 0.0))
            highs.append(high)
            lows.append(low)
        return jnp.concatenate(highs + highs + lows, axis=0)

    def tall(term, part):
        if term == 0:
            return jnp.concatenate([geo_ref[part, tile] for tile in range(tiles)], axis=0)
        return jnp.concatenate([basis_ref[term - 1, part, tile] for tile in range(tiles)], axis=0)

    copies = []
    for number, (out_hbm, parts) in enumerate(
        ((solution_hbm, answers), (residual_hbm, left_over))
    ):
        matrix = spread(parts)
        terms = matrix.shape[0] // (3 * TILE)
        highs = [tall(term, 0) for term in range(terms)]
        lows = [tall(term, 1) for term in range(terms)]
        value = dot(jnp.concatenate(highs + lows + highs, axis=1), matrix)
        for tile in range(tiles):
            lanes = slice(tile * TILE, (tile + 1) * TILE)
            out_refs[number, :, lanes] = value[tile * rows:(tile + 1) * rows]
        copies.append(pltpu.make_async_copy(out_refs.at[number], out_hbm, sems.at[number]))
        copies[number].start()
    for copy in copies:
        copy.wait()


def on_device(loads, row_ids, densities, block_cols, block_types, ref_blocks):
    rows, width = loads.shape
    slots = densities.shape[1]
    cases = width // ref_blocks.shape[1]
    cap = rows // 4
    edge = ITERS * HALO
    tiles = width // TILE
    devices = lax.axis_size("sub")
    position = lax.axis_index("sub").astype(jnp.int32).reshape(1, 1)
    shape = jax.ShapeDtypeStruct
    same_chip = [(i, i ^ 1) for i in range(devices)]
    next_chip = [(i, i + 1) for i in range(1, devices - 1, 2)]
    next_chip += [(i + 1, i) for i in range(1, devices - 1, 2)]
    neighbour = dict(next_chip)
    rounds = [[], []]
    for i in range(devices):
        early = 0 if far_first(i, devices) else 1
        rounds[early].append((i, (i + devices // 2) % devices))
        if i in neighbour:
            rounds[1 - early].append((i, neighbour[i]))

    block = shape((cap * width // META + cap // 2, META), F32)
    to_first, meta, target = pl.pallas_call(
        functools.partial(pack_first_kernel, devices),
        out_shape=(block, shape((META, rows), F32), shape((8, rows), jnp.int32)),
        in_specs=[SMEM] + [HBM] * 5,
        out_specs=(VMEM,) * 3,
        scratch_shapes=[
            pltpu.VMEM((rows, width), F32),
            pltpu.VMEM((1, rows), jnp.int32),
            pltpu.VMEM((slots, rows), F32),
            pltpu.VMEM((slots, rows), jnp.int32),
            pltpu.VMEM((slots, rows), jnp.int32),
            pltpu.SemaphoreType.DMA((5,)),
        ],
        compiler_params=PACK_PARAMS,
        name="pack_first",
    )(position, loads, row_ids.reshape(1, rows), densities.T, block_cols.T, block_types.T)
    from_first = lax.ppermute(to_first, "sub", rounds[0])

    to_core, to_second = pl.pallas_call(
        functools.partial(pack_second_kernel, devices),
        out_shape=(block, block),
        in_specs=[SMEM] + [HBM] * 3,
        out_specs=(VMEM,) * 2,
        scratch_shapes=[
            pltpu.VMEM((8, rows), jnp.int32),
            pltpu.VMEM((META, rows), F32),
            pltpu.VMEM((rows, width), F32),
            pltpu.SemaphoreType.DMA((3,)),
        ],
        compiler_params=PACK_PARAMS,
        name="pack_second",
    )(position, target, meta, loads)
    from_second = lax.ppermute(to_second, "sub", rounds[1])
    from_core = lax.ppermute(to_core, "sub", same_chip)

    mixer_shape = shape((3 * TYPES * TILE, TILE), BF16)
    kept, kept_meta, mixer, first = pl.pallas_call(
        functools.partial(prepare_kernel, slots),
        out_shape=(
            shape((rows, width), F32),
            shape((rows, META), F32),
            mixer_shape,
            shape((cases, TILE), F32),
        ),
        in_specs=[VMEM] * 3,
        out_specs=(VMEM,) * 4,
        compiler_params=PARAMS,
        cost_estimate=pl.CostEstimate(
            flops=4_000_000_000, bytes_accessed=4_000_000, transcendentals=0
        ),
        name="prepare",
    )(loads, meta, ref_blocks)

    border = shape((edge, width + META), F32)
    pair = shape((2, tiles, rows, TILE), BF16)
    geo, field, geo_meta, to_core, to_chip = pl.pallas_call(
        functools.partial(arrange_kernel, slots),
        out_shape=(pair, pair, shape((rows, META), F32), border, border),
        in_specs=[SMEM] + [VMEM] * 5,
        out_specs=(VMEM,) * 5,
        compiler_params=PARAMS,
        name="arrange",
    )(position, from_first, from_second, from_core, kept, kept_meta)

    halo_chip = lax.ppermute(to_chip, "sub", next_chip)
    halo_core = lax.ppermute(to_core, "sub", same_chip)

    basis_shape = shape((ITERS, 2, tiles, rows, TILE), BF16)
    inner, weights = pl.pallas_call(
        functools.partial(interior_kernel, slots),
        out_shape=(basis_shape, shape((2, TYPES, edge, 3 * TILE), BF16)),
        in_specs=[VMEM] * 4,
        out_specs=(VMEM,) * 2,
        scratch_shapes=[
            pltpu.VMEM((TYPES, rows - 2 * HALO, 3 * TILE), BF16),
            pltpu.VMEM((2, TYPES, tiles * (rows - 2 * HALO), TILE), BF16),
        ],
        compiler_params=PARAMS,
        cost_estimate=pl.CostEstimate(
            flops=10_000_000_000, bytes_accessed=8_000_000, transcendentals=0
        ),
        name="interior",
    )(field, geo_meta, mixer, ref_blocks)

    basis, moments = pl.pallas_call(
        functools.partial(sides_kernel, slots),
        out_shape=(basis_shape, shape((devices, cases, META), F32)),
        in_specs=[SMEM] + [VMEM] * 9,
        out_specs=(VMEM,) * 2,
        scratch_shapes=[
            pltpu.VMEM((ITERS + 1, 2, 2, tiles, edge, TILE), BF16),
            pltpu.VMEM((2, edge, META), F32),
            pltpu.VMEM((2, TYPES, edge - HALO, 3 * TILE), BF16),
            pltpu.VMEM((2, TYPES, 2 * tiles * edge, TILE), BF16),
        ],
        compiler_params=PARAMS,
        name="sides",
    )(position, halo_core, halo_chip, field, inner, weights, mixer, ref_blocks, geo, first)

    moments = lax.all_to_all(moments, "sub", split_axis=0, concat_axis=0, tiled=True)

    return pl.pallas_call(
        functools.partial(finish_kernel, slots),
        out_shape=(shape((rows, width), F32), shape((rows, width), F32)),
        in_specs=[VMEM] * 4,
        out_specs=(HBM,) * 2,
        scratch_shapes=[pltpu.VMEM((2, rows, width), F32), pltpu.SemaphoreType.DMA((2,))],
        compiler_params=PARAMS,
        name="finish",
    )(moments, ref_blocks, geo, basis)


def solution(mesh):
    placed = (
        P(("groups", "sub"), None),
        P(("groups", "sub")),
        P(("groups", "sub"), None),
        P(("groups", "sub"), None),
        P(("groups", "sub"), None),
        P(),
    )
    return jax.shard_map(
        on_device,
        mesh=mesh,
        in_specs=placed,
        out_specs=(P(("groups", "sub"), None), P(("groups", "sub"), None)),
        check_vma=False,
    )
```

```python
import functools

import jax
import jax.numpy as jnp
from jax import lax
from jax.experimental import pallas as pl
from jax.experimental.pallas import tpu as pltpu
from jax.sharding import PartitionSpec as P

HALO = 32
TYPES = 3
ITERS = 3
MASS_SHIFT = 0.5
META = 128
TILE = 256

F32 = jnp.float32
BF16 = jnp.bfloat16
VMEM = pl.BlockSpec(memory_space=pltpu.VMEM)
SMEM = pl.BlockSpec(memory_space=pltpu.SMEM)
HBM = pl.BlockSpec(memory_space=pltpu.HBM)
PARAMS = pltpu.CompilerParams(vmem_limit_bytes=40 * 1024 * 1024)


def dot(left, right):
    return jnp.dot(left, right, preferred_element_type=F32)


def dot_nt(left, right):
    return lax.dot_general(left, right, (((1,), (1,)), ((), ())), preferred_element_type=F32)


def dot_tn(left, right):
    return lax.dot_general(left, right, (((0,), (0,)), ((), ())), preferred_element_type=F32)


def halves(value):
    high = value.astype(BF16)
    return high, (value - high.astype(F32)).astype(BF16)


def iota(shape, axis):
    return lax.broadcasted_iota(jnp.int32, shape, axis)


def one_hot(condition):
    return jnp.where(condition, 1.0, 0.0).astype(BF16)


PACK_PARAMS = pltpu.CompilerParams(vmem_limit_bytes=62 * 1024 * 1024)


def basis_shift(blocks, slots):
    dof = blocks.shape[1]
    same = iota((dof, dof), 0) == iota((dof, dof), 1)
    total = sum(jnp.where(same, blocks[t], 0.0) for t in range(TYPES))
    mean = jnp.sum(jnp.sum(total, axis=1, keepdims=True), axis=0, keepdims=True) / (TYPES * dof)
    return MASS_SHIFT + 0.2 * slots * mean


def swap_blocks(piece):
    lane = iota(piece(0, 0).shape, 1)
    low = lane < META // 2
    out = []
    for tile in range(4):
        for part in range(2):
            first, second = piece(2 * part, tile // 2), piece(2 * part + 1, tile // 2)
            if tile % 2 == 0:
                second = pltpu.roll(second, META // 2, 1)
            else:
                first = pltpu.roll(first, META // 2, 1)
            out.append(jnp.where(low, first, second))
    return out


def given_to_gram():
    source, target = iota((TILE, TILE), 0), iota((TILE, TILE), 1)
    return one_hot((target // 16 == source % 16) & (target % 16 == source // 16))


def peers(pos, devices):
    odd = lax.rem(pos, jnp.int32(2))
    return (
        pos + 1 - 2 * odd,
        pos - 1 + 2 * odd,
        lax.rem(pos + devices // 2, jnp.int32(devices)),
    )


def far_first(pos, devices):
    half = devices // 2
    group = (pos % half + 1) // 2 % max(half // 2, 1)
    return group % 2 == 1


def targets(pos, ids, rows, devices):
    cap = rows // 4
    owner = lax.div(ids, jnp.int32(rows))
    goes = []
    for peer in peers(pos, devices):
        here = owner == peer
        for other in goes:
            here = here & ~other
        goes.append(here)
    flags = jnp.concatenate(
        [jnp.where(g, 1.0, 0.0) for g in goes] + [jnp.zeros((5, rows), F32)], axis=0
    )
    before = one_hot(iota((rows, rows), 0) < iota((rows, rows), 1))
    rank = dot(flags.astype(BF16), before).astype(jnp.int32)
    target = jnp.full((1, rows), -1, jnp.int32)
    for side in range(3):
        target = jnp.where(goes[side], rank[side:side + 1] + side * cap, target)
    return target


def fill_block(pick, loads, meta, out_ref):
    width = loads.shape[1]
    cap = pick.shape[0]
    twice = jnp.concatenate([pick, pick], axis=1)
    notes = dot_nt(twice, jnp.concatenate(halves(meta), axis=1))
    body = dot(twice, jnp.concatenate(halves(loads), axis=0))
    parts = width // META
    for part in range(parts):
        out_ref[part * cap:(part + 1) * cap, :] = body[:, part * META:(part + 1) * META]
    out_ref[parts * cap:, :] = notes[:cap // 2] + pltpu.roll(notes[cap // 2:], META // 2, 1)


def read_block(ref, width):
    parts = width // META
    cap = ref.shape[0] * 2 // (2 * parts + 1)
    body = jnp.concatenate([ref[part * cap:(part + 1) * cap, :] for part in range(parts)], axis=1)
    notes = ref[parts * cap:, :]
    notes = jnp.concatenate([notes, pltpu.roll(notes, META // 2, 1)], axis=0)
    return body, jnp.where(iota(notes.shape, 1) < META // 2, notes, 0.0)


def pack_kernel(devices, pos_ref, loads_hbm, rows_hbm, dens_hbm, cols_hbm, types_hbm,
                first_ref, second_ref, core_ref, meta_ref,
                loads_ref, rows_ref, dens_ref, cols_ref, types_ref, sems):
    pairs = (
        (rows_hbm, rows_ref), (dens_hbm, dens_ref), (cols_hbm, cols_ref),
        (types_hbm, types_ref), (loads_hbm, loads_ref),
    )
    copies = [
        pltpu.make_async_copy(source, target, sems.at[number])
        for number, (source, target) in enumerate(pairs)
    ]
    for copy in copies:
        copy.start()
    for copy in copies[:4]:
        copy.wait()
    rows = loads_ref.shape[0]
    slots = dens_ref.shape[0]
    cap = rows // 4
    pos = pos_ref[0, 0]
    ids = rows_ref[...]
    owner = lax.div(ids, jnp.int32(rows))
    local = (ids - owner * rows + 1).astype(F32)
    target = targets(pos, ids, rows, devices)

    density = dens_ref[...]
    kinds = types_ref[...]
    for kind in range(TYPES):
        meta_ref[kind * slots:(kind + 1) * slots, :] = jnp.where(kinds == kind, density, 0.0)
    meta_ref[3 * slots:4 * slots, :] = (cols_ref[...] - ids).astype(F32)
    meta_ref[4 * slots:, :] = jnp.zeros((META - 4 * slots, rows), F32)
    meta_ref[4 * slots:4 * slots + 1, :] = local
    meta_ref[4 * slots + 1:4 * slots + 2, :] = jnp.where(owner == pos, local, 0.0)

    copies[4].wait()
    early = jnp.where(far_first(pos, devices), 2, 1)
    for side, out_ref in ((early, first_ref), (3 - early, second_ref), (0, core_ref)):
        pick = one_hot(iota((cap, rows), 0) + side * cap == target)
        fill_block(pick, loads_ref[...], meta_ref[...], out_ref)


def reorder(parts, tiles):
    count = parts[0].shape[0]
    tall = [p[:, t * TILE:(t + 1) * TILE] for t in range(tiles) for p in parts]
    moved = dot(jnp.concatenate(tall, axis=0), given_to_gram()).astype(BF16)
    return [
        jnp.concatenate(
            [moved[(2 * t + p) * count:(2 * t + p + 1) * count] for t in range(tiles)], axis=1
        )
        for p in range(2)
    ]


def stacked_tiles(value, tiles):
    return jnp.concatenate([value[:, t * TILE:(t + 1) * TILE] for t in range(tiles)], axis=0)


def folded_rows(gram, cases):
    same_dof = iota((TILE, TILE), 0) % 16 == iota((TILE, TILE), 1) % 16
    gram = jnp.where(same_dof, gram, 0.0)
    return jnp.sum(gram.reshape(cases, TILE // cases, TILE), axis=1)


def prepare_kernel(slots, loads_ref, meta_ref, blocks_ref,
                   kept_ref, kept_meta_ref, mixer_ref, first_ref):
    rows, width = loads_ref.shape
    dof = blocks_ref.shape[1]
    tiles = width // TILE
    place = iota((rows, rows), 0) + 1
    own = one_hot(place == meta_ref[4 * slots + 1:4 * slots + 2, :].astype(jnp.int32))
    twice = jnp.concatenate([own, own], axis=1)
    moved = reorder(halves(loads_ref[...]), tiles)
    kept_ref[...] = dot(twice, jnp.concatenate(moved, axis=0))
    high, low = (stacked_tiles(part, tiles) for part in moved)
    gram = dot_tn(high, jnp.concatenate([high, low], axis=1))
    cross = gram[:, TILE:]
    first_ref[...] = folded_rows(gram[:, :TILE] + cross + cross.T, width // dof)
    kept_meta_ref[...] = dot_nt(twice, jnp.concatenate(halves(meta_ref[...]), axis=1))

    def dof_of(lane):
        return lane // 64 * 16 + lane % 16

    fold = one_hot(dof_of(iota((TILE, dof), 0)) == iota((TILE, dof), 1))
    unfold = one_hot(dof_of(iota((dof, TILE), 1)) == iota((dof, TILE), 0))
    same_case = iota((TILE, TILE), 0) // 16 % 4 == iota((TILE, TILE), 1) // 16 % 4
    for kind in range(TYPES):
        for copies, part in zip(((0, 2), (1,)), halves(blocks_ref[kind])):
            wide = dot(dot_nt(fold, part).astype(BF16), unfold)
            wide = jnp.where(same_case, wide, 0.0).astype(BF16)
            for copy in copies:
                start = (copy * TYPES + kind) * TILE
                mixer_ref[start:start + TILE, :] = wide


def arrange_kernel(slots, pos_ref, first_ref, second_ref, core_ref, kept_ref, kept_meta_ref,
                   geo_ref, field_ref, meta_ref, to_core_ref, to_chip_ref):
    rows, width = kept_ref.shape
    tiles = width // TILE
    edge = to_core_ref.shape[0]
    even = lax.rem(pos_ref[0, 0], jnp.int32(2)) == 0
    blocks = [read_block(ref, width) for ref in (first_ref, second_ref, core_ref)]
    arrived = jnp.concatenate([block[0] for block in blocks], axis=0)
    arrived_meta = jnp.concatenate([block[1] for block in blocks], axis=0)
    count = arrived.shape[0]
    unit = one_hot(iota((8, META), 1) == 4 * slots)
    tags = dot_nt(unit, arrived_meta.astype(BF16))[0:1]
    other = one_hot(iota((rows, count), 0) + 1 == tags.astype(jnp.int32))
    twice = jnp.concatenate([other, other], axis=1)
    moved = reorder(halves(arrived), tiles)
    geo = kept_ref[...] + dot(twice, jnp.concatenate(moved, axis=0))
    meta = kept_meta_ref[...] + dot(twice, jnp.concatenate(halves(arrived_meta), axis=0))
    meta_ref[...] = meta

    def send(lanes, value):
        head, tail = value[:edge], value[rows - edge:]
        to_core_ref[:, lanes] = jnp.where(even, tail, head)
        to_chip_ref[:, lanes] = jnp.where(even, head, tail)

    send(slice(width, None), meta)

    def piece(tile, part):
        start = tile * TILE + part * META
        return geo[:, start:start + META]

    for number, value in enumerate(swap_blocks(piece)):
        lanes = slice(number * META, (number + 1) * META)
        send(lanes, value)
        inner = slice(number % 2 * META, (number % 2 + 1) * META)
        for part, half in enumerate(halves(value)):
            field_ref[part, number // 2, :, inner] = half
    for part, half in enumerate(halves(geo)):
        for tile in range(tiles):
            geo_ref[part, tile] = half[:, tile * TILE:(tile + 1) * TILE]


def stencil_rows(meta, slots, first):
    lane = iota((HALO, META), 1)
    spot = iota((HALO, TILE), 1)
    centre = iota((HALO, 1), 0) + first
    sums = [jnp.zeros((HALO, TILE), F32) for _ in range(TYPES)]
    for slot in range(slots):
        column = centre + meta[:, 3 * slots + slot:3 * slots + slot + 1].astype(jnp.int32)
        hit = spot == column
        for kind in range(TYPES):
            weight = meta[:, kind * slots + slot:kind * slots + slot + 1]
            sums[kind] += jnp.where(hit, weight, 0.0)
    out = []
    for kind in range(TYPES):
        inside = (lane >= kind * slots) & (lane < (kind + 1) * slots)
        total = jnp.sum(jnp.where(inside, meta, 0.0), axis=1, keepdims=True)
        high, low = halves(jnp.where(spot == centre, total, 0.0) - sums[kind])
        out.append(jnp.concatenate([high, high, low], axis=1))
    return out


def gathered(weights, near, fine):
    return halves(dot(weights, jnp.concatenate([near, fine, near], axis=0)))


def mixed(buckets, mixer_ref, count):
    highs = [buckets[0, kind, :count, :] for kind in range(TYPES)]
    lows = [buckets[1, kind, :count, :] for kind in range(TYPES)]
    return dot(jnp.concatenate(highs + highs + lows, axis=1), mixer_ref[...])


def interior_kernel(slots, field_ref, meta_ref, mixer_ref, blocks_ref,
                    inner_ref, weights_ref, stencil, buckets):
    tiles, rows = field_ref.shape[1:3]
    edge = ITERS * HALO
    shift = basis_shift(blocks_ref[...], slots)
    inside = rows - 2 * HALO

    def build(chunk, carry):
        first = pl.multiple_of(chunk * HALO, HALO)
        start = pl.multiple_of(chunk * HALO + HALO, HALO)
        for kind, value in enumerate(
            stencil_rows(meta_ref[pl.ds(start, HALO), :], slots, first + HALO)
        ):
            stencil[kind, pl.ds(first, HALO), :] = value
        return carry

    lax.fori_loop(0, inside // HALO, build, 0)

    def build_outer(side, chunk):
        first = chunk * HALO
        start = first + side * (rows - edge)
        spot = first + edge if side == 0 else first + rows - 2 * edge
        for kind, value in enumerate(stencil_rows(meta_ref[start:start + HALO, :], slots, spot)):
            weights_ref[side, kind, first:first + HALO, :] = value

    for step in range(ITERS - 1):
        begin = HALO * (step + 1)
        blank = jnp.zeros((begin, TILE), BF16)
        for part in range(2):
            for tile in range(tiles):
                inner_ref[step, part, tile, :begin, :] = blank
                inner_ref[step, part, tile, rows - begin:, :] = blank
    for step in range(ITERS):
        skip = HALO * step
        count = inside - 2 * skip
        begin = HALO + skip
        weights = jnp.concatenate(
            [stencil[kind, skip:inside - skip, :] for kind in range(TYPES)], axis=0
        )

        def read(part, tile, block):
            if step == 0:
                return field_ref[part, tile, block, :]
            return inner_ref[step - 1, part, tile, block, :]

        for tile in range(tiles):
            every = slice(0, rows)
            for part, half in enumerate(
                gathered(weights, read(0, tile, every), read(1, tile, every))
            ):
                for kind in range(TYPES):
                    buckets[part, kind, tile * count:(tile + 1) * count, :] = (
                        half[kind * count:(kind + 1) * count]
                    )
        for side in range(2):
            build_outer(side, step)
        applied = mixed(buckets, mixer_ref, tiles * count)
        block = slice(begin, begin + count)
        for tile in range(tiles):
            here = read(0, tile, block).astype(F32) + read(1, tile, block).astype(F32)
            value = applied[tile * count:(tile + 1) * count] + (MASS_SHIFT - shift) * here
            for part, half in enumerate(halves(value)):
                inner_ref[step, part, tile, block, :] = half


def sides_kernel(slots, pos_ref, core_ref, chip_ref, field_ref, inner_ref, weights_ref, mixer_ref,
                 blocks_ref, geo_ref, first_ref, basis_ref, moments_ref, v_refs, meta_refs, stencil, buckets):
    tiles, rows = field_ref.shape[1:3]
    width = tiles * TILE
    dof = blocks_ref.shape[1]
    cases = width // dof
    edge = ITERS * HALO
    outer = edge - HALO
    count = edge
    rest = TILE - edge
    shift = basis_shift(blocks_ref[...], slots)
    even = lax.rem(pos_ref[0, 0], jnp.int32(2)) == 0

    for tile in range(tiles + 1):
        lanes = slice(tile * TILE, (tile + 1) * TILE) if tile < tiles else slice(width, None)
        core, chip = core_ref[:, lanes], chip_ref[:, lanes]
        for side, value in enumerate((jnp.where(even, chip, core), jnp.where(even, core, chip))):
            if tile == tiles:
                meta_refs[side] = value
            else:
                for part, half in enumerate(halves(value)):
                    v_refs[0, side, part, tile] = half

    def build(side):
        for first in range(0, outer, HALO):
            start = first + HALO * (1 - side)
            spot = first + HALO if side == 0 else first + rows - edge
            for kind, value in enumerate(
                stencil_rows(meta_refs[side, start:start + HALO, :], slots, spot)
            ):
                stencil[side, kind, first:first + HALO, :] = value

    def window(step, side, part, tile):
        near = v_refs[step, side, part, tile]
        if step == 0:
            if side == 0:
                return jnp.concatenate([near, field_ref[part, tile, :rest, :]], axis=0)
            return jnp.concatenate([field_ref[part, tile, rows - rest:, :], near], axis=0)
        blank = jnp.zeros((HALO * step, TILE), BF16)
        begin = HALO * step
        if side == 0:
            far = inner_ref[step - 1, part, tile, begin:rest, :]
            return jnp.concatenate([blank, near, far], axis=0)
        far = inner_ref[step - 1, part, tile, rows - rest:rows - begin, :]
        return jnp.concatenate([far, near, blank], axis=0)

    def weight_rows(step, side, kind):
        keep = outer - HALO * step
        if side == 0:
            pieces = [weights_ref[0, kind, :count - keep, :]]
            if keep:
                pieces.insert(0, stencil[0, kind, outer - keep:, :])
        else:
            pieces = [weights_ref[1, kind, keep:, :]]
            if keep:
                pieces.append(stencil[1, kind, :keep, :])
        return jnp.concatenate(pieces, axis=0)

    def convert(step):
        begin = HALO * step
        for half in range(2):

            def piece(tile, part):
                lanes = slice(part * META, (part + 1) * META)
                return jnp.concatenate(
                    [
                        v_refs[step, 0, half, tile, count - begin:, lanes],
                        inner_ref[step - 1, half, tile, begin:rows - begin, lanes],
                        v_refs[step, 1, half, tile, :begin, lanes],
                    ],
                    axis=0,
                )

            for number, value in enumerate(swap_blocks(piece)):
                lanes = slice(number % 2 * META, (number % 2 + 1) * META)
                basis_ref[step - 1, half, number // 2, :, lanes] = value

    def tall(step, part):
        if step == 0:
            return jnp.concatenate([geo_ref[part, tile] for tile in range(tiles)], axis=0)
        return jnp.concatenate([basis_ref[step - 1, part, tile] for tile in range(tiles)], axis=0)

    def mixed_gram(high, low):
        return folded_rows(high[:, :TILE] + high[:, TILE:] + low, cases)

    def even_gram(high):
        cross = high[:, TILE:]
        return folded_rows(high[:, :TILE] + cross + cross.T, cases)

    sums = [first_ref[...]]
    for step in range(ITERS):
        centres = []
        for side in range(2):
            if step == 0:
                build(side)
            weights = jnp.concatenate(
                [weight_rows(step, side, kind) for kind in range(TYPES)], axis=0
            )
            for tile in range(tiles):
                row = (side * tiles + tile) * count
                near, fine = (window(step, side, part, tile) for part in range(2))
                first = HALO * (step + 1) if side == 0 else TILE - HALO * (step + 1) - count
                centres.append((near[first:first + count], fine[first:first + count]))
                for part, half in enumerate(gathered(weights, near, fine)):
                    for kind in range(TYPES):
                        buckets[part, kind, row:row + count, :] = (
                            half[kind * count:(kind + 1) * count]
                        )
        applied = mixed(buckets, mixer_ref, 2 * tiles * count)
        for side in range(2):
            for tile in range(tiles):
                number = side * tiles + tile
                near, fine = centres[number]
                here = near.astype(F32) + fine.astype(F32)
                value = applied[number * count:(number + 1) * count] + (MASS_SHIFT - shift) * here
                for part, half in enumerate(halves(value)):
                    v_refs[step + 1, side, part, tile] = half

        convert(step + 1)
        if step == 1:
            others = [tall(k, part) for k in range(3) for part in range(2)]
            high = dot_tn(tall(1, 0), jnp.concatenate(others, axis=1))
            low = dot_tn(tall(1, 1), jnp.concatenate([others[0], others[4]], axis=1))
            sums.append(mixed_gram(high[:, :2 * TILE], low[:, :TILE]))
            sums.append(even_gram(high[:, 2 * TILE:4 * TILE]))
            sums.append(mixed_gram(high[:, 4 * TILE:], low[:, TILE:]))
        elif step == 2:
            others = [tall(k, part) for k in range(2, 4) for part in range(2)]
            high = dot_tn(tall(2, 0), jnp.concatenate(others, axis=1))
            low = dot_tn(tall(2, 1), others[2])
            sums.append(even_gram(high[:, :2 * TILE]))
            sums.append(mixed_gram(high[:, 2 * TILE:], low))

    remainder = jnp.concatenate(sums, axis=0)
    pieces = []
    for _ in range(3):
        pieces.append(remainder.astype(BF16))
        remainder = remainder - pieces[-1].astype(F32)
    collect = one_hot(iota((TILE, META), 0) // 16 == iota((TILE, META), 1) % 16)
    folded = dot(jnp.concatenate(pieces, axis=1), jnp.concatenate([collect] * 3, axis=0))
    group = iota((cases, META), 1) // cases
    moments = jnp.zeros((cases, META), F32)
    for number in range(2 * ITERS):
        part = folded[number * cases:(number + 1) * cases]
        moments = jnp.where(group == number, part, moments)
    for device in range(moments_ref.shape[0]):
        moments_ref[device] = moments


def refined_reciprocal(value):
    guess = pl.reciprocal(value, approx=True)
    for _ in range(2):
        guess = guess * (2.0 - value * guess)
    return guess


def finish_kernel(slots, moments_ref, blocks_ref, geo_ref, basis_ref,
                  solution_hbm, residual_hbm, out_refs, sems):
    rows, width = out_refs.shape[1:]
    dof = blocks_ref.shape[1]
    cases = width // dof
    tiles = width // TILE
    shift = basis_shift(blocks_ref[...], slots)
    moments = moments_ref[0]
    for device in range(1, moments_ref.shape[0]):
        moments = moments + moments_ref[device]
    group = iota((cases, META), 1) // cases
    system = []
    for row in range(ITERS):
        plain = moments if row == 0 else pltpu.roll(moments, META - cases * row, 1)
        ahead = pltpu.roll(moments, META - cases * (row + 1), 1)
        target = pltpu.roll(moments, cases * (ITERS - row), 1)
        system.append(jnp.where(group < ITERS, ahead + shift * plain, target))
    system = jnp.concatenate(system, axis=0)
    size = ITERS * cases
    index = iota((size, 1), 0)
    for pivot in range(0, size, 2):
        column_a = jnp.broadcast_to(system[:, pivot:pivot + 1], (size, META))
        column_b = jnp.broadcast_to(system[:, pivot + 1:pivot + 2], (size, META))
        line_a = system[pivot:pivot + 1, :]
        line_b = system[pivot + 1:pivot + 2, :]
        above = column_b[pivot:pivot + 1, :]
        inverse = refined_reciprocal(column_a[pivot:pivot + 1, :])
        factor = column_a[pivot + 1:pivot + 2, :] * inverse
        corner = column_b[pivot + 1:pivot + 2, :] - factor * above
        line_b = (line_b - factor * line_a) * refined_reciprocal(corner)
        line_a = (line_a - above * line_b) * inverse
        update = system - column_a * line_a - column_b * line_b
        system = jnp.where(index == pivot, line_a, jnp.where(index == pivot + 1, line_b, update))

    unit = jnp.where(iota((cases, META), 1) % cases == iota((cases, META), 0), 1.0, 0.0)
    answers = []
    for row in range(ITERS):
        part = jnp.where(group == ITERS, system[row * cases:(row + 1) * cases], 0.0)
        step = cases
        while step < META:
            part = part + pltpu.roll(part, step, 1)
            step *= 2
        answers.append(part)
    left_over = [unit - shift * answers[0]]
    for row in range(1, ITERS):
        left_over.append(-(answers[row - 1] + shift * answers[row]))
    left_over.append(-answers[ITERS - 1])

    meets = iota((TILE, TILE), 0) % 16 == iota((TILE, TILE), 1) // 16

    def spread(parts):
        highs, lows = [], []
        for part in parts:
            tall = jnp.broadcast_to(part[:, None, :], (cases, TILE // cases, META))
            tall = tall.reshape(TILE, META)
            wide = jnp.concatenate([tall] * (TILE // META), axis=1)
            high, low = halves(jnp.where(meets, wide, 0.0))
            highs.append(high)
            lows.append(low)
        return jnp.concatenate(highs + highs + lows, axis=0)

    def tall(term, part):
        if term == 0:
            return jnp.concatenate([geo_ref[part, tile] for tile in range(tiles)], axis=0)
        return jnp.concatenate([basis_ref[term - 1, part, tile] for tile in range(tiles)], axis=0)

    copies = []
    for number, (out_hbm, parts) in enumerate(
        ((solution_hbm, answers), (residual_hbm, left_over))
    ):
        matrix = spread(parts)
        terms = matrix.shape[0] // (3 * TILE)
        highs = [tall(term, 0) for term in range(terms)]
        lows = [tall(term, 1) for term in range(terms)]
        value = dot(jnp.concatenate(highs + lows + highs, axis=1), matrix)
        for tile in range(tiles):
            lanes = slice(tile * TILE, (tile + 1) * TILE)
            out_refs[number, :, lanes] = value[tile * rows:(tile + 1) * rows]
        copies.append(pltpu.make_async_copy(out_refs.at[number], out_hbm, sems.at[number]))
        copies[number].start()
    for copy in copies:
        copy.wait()


def on_device(loads, row_ids, densities, block_cols, block_types, ref_blocks):
    rows, width = loads.shape
    slots = densities.shape[1]
    cases = width // ref_blocks.shape[1]
    cap = rows // 4
    edge = ITERS * HALO
    tiles = width // TILE
    devices = lax.axis_size("sub")
    position = lax.axis_index("sub").astype(jnp.int32).reshape(1, 1)
    shape = jax.ShapeDtypeStruct
    same_chip = [(i, i ^ 1) for i in range(devices)]
    next_chip = [(i, i + 1) for i in range(1, devices - 1, 2)]
    next_chip += [(i + 1, i) for i in range(1, devices - 1, 2)]
    neighbour = dict(next_chip)
    rounds = [[], []]
    for i in range(devices):
        early = 0 if far_first(i, devices) else 1
        rounds[early].append((i, (i + devices // 2) % devices))
        if i in neighbour:
            rounds[1 - early].append((i, neighbour[i]))

    block = shape((cap * width // META + cap // 2, META), F32)
    *outgoing, meta = pl.pallas_call(
        functools.partial(pack_kernel, devices),
        out_shape=(block, block, block, shape((META, rows), F32)),
        in_specs=[SMEM] + [HBM] * 5,
        out_specs=(VMEM,) * 4,
        scratch_shapes=[
            pltpu.VMEM((rows, width), F32),
            pltpu.VMEM((1, rows), jnp.int32),
            pltpu.VMEM((slots, rows), F32),
            pltpu.VMEM((slots, rows), jnp.int32),
            pltpu.VMEM((slots, rows), jnp.int32),
            pltpu.SemaphoreType.DMA((5,)),
        ],
        compiler_params=PACK_PARAMS,
        name="pack",
    )(position, loads, row_ids.reshape(1, rows), densities.T, block_cols.T, block_types.T)
    routes = (rounds[0], rounds[1], same_chip)
    incoming = [lax.ppermute(part, "sub", route) for part, route in zip(outgoing, routes)]

    mixer_shape = shape((3 * TYPES * TILE, TILE), BF16)
    kept, kept_meta, mixer, first = pl.pallas_call(
        functools.partial(prepare_kernel, slots),
        out_shape=(
            shape((rows, width), F32),
            shape((rows, META), F32),
            mixer_shape,
            shape((cases, TILE), F32),
        ),
        in_specs=[VMEM] * 3,
        out_specs=(VMEM,) * 4,
        compiler_params=PARAMS,
        cost_estimate=pl.CostEstimate(
            flops=4_000_000_000, bytes_accessed=4_000_000, transcendentals=0
        ),
        name="prepare",
    )(loads, meta, ref_blocks)

    border = shape((edge, width + META), F32)
    pair = shape((2, tiles, rows, TILE), BF16)
    geo, field, geo_meta, to_core, to_chip = pl.pallas_call(
        functools.partial(arrange_kernel, slots),
        out_shape=(pair, pair, shape((rows, META), F32), border, border),
        in_specs=[SMEM] + [VMEM] * 5,
        out_specs=(VMEM,) * 5,
        compiler_params=PARAMS,
        name="arrange",
    )(position, *incoming, kept, kept_meta)

    halo_chip = lax.ppermute(to_chip, "sub", next_chip)
    halo_core = lax.ppermute(to_core, "sub", same_chip)

    basis_shape = shape((ITERS, 2, tiles, rows, TILE), BF16)
    inner, weights = pl.pallas_call(
        functools.partial(interior_kernel, slots),
        out_shape=(basis_shape, shape((2, TYPES, edge, 3 * TILE), BF16)),
        in_specs=[VMEM] * 4,
        out_specs=(VMEM,) * 2,
        scratch_shapes=[
            pltpu.VMEM((TYPES, rows - 2 * HALO, 3 * TILE), BF16),
            pltpu.VMEM((2, TYPES, tiles * (rows - 2 * HALO), TILE), BF16),
        ],
        compiler_params=PARAMS,
        cost_estimate=pl.CostEstimate(
            flops=10_000_000_000, bytes_accessed=8_000_000, transcendentals=0
        ),
        name="interior",
    )(field, geo_meta, mixer, ref_blocks)

    basis, moments = pl.pallas_call(
        functools.partial(sides_kernel, slots),
        out_shape=(basis_shape, shape((devices, cases, META), F32)),
        in_specs=[SMEM] + [VMEM] * 9,
        out_specs=(VMEM,) * 2,
        scratch_shapes=[
            pltpu.VMEM((ITERS + 1, 2, 2, tiles, edge, TILE), BF16),
            pltpu.VMEM((2, edge, META), F32),
            pltpu.VMEM((2, TYPES, edge - HALO, 3 * TILE), BF16),
            pltpu.VMEM((2, TYPES, 2 * tiles * edge, TILE), BF16),
        ],
        compiler_params=PARAMS,
        name="sides",
    )(position, halo_core, halo_chip, field, inner, weights, mixer, ref_blocks, geo, first)

    moments = lax.all_to_all(moments, "sub", split_axis=0, concat_axis=0, tiled=True)

    return pl.pallas_call(
        functools.partial(finish_kernel, slots),
        out_shape=(shape((rows, width), F32), shape((rows, width), F32)),
        in_specs=[VMEM] * 4,
        out_specs=(HBM,) * 2,
        scratch_shapes=[pltpu.VMEM((2, rows, width), F32), pltpu.SemaphoreType.DMA((2,))],
        compiler_params=PARAMS,
        name="finish",
    )(moments, ref_blocks, geo, basis)


def solution(mesh):
    placed = (
        P(("groups", "sub"), None),
        P(("groups", "sub")),
        P(("groups", "sub"), None),
        P(("groups", "sub"), None),
        P(("groups", "sub"), None),
        P(),
    )
    return jax.shard_map(
        on_device,
        mesh=mesh,
        in_specs=placed,
        out_specs=(P(("groups", "sub"), None), P(("groups", "sub"), None)),
        check_vma=False,
    )
```

```python
import functools

import jax
import jax.numpy as jnp
from jax import lax
from jax.experimental import pallas as pl
from jax.experimental.pallas import tpu as pltpu
from jax.sharding import PartitionSpec as P

HALO = 32
TYPES = 3
ITERS = 3
MASS_SHIFT = 0.5
META = 128
TILE = 256

F32 = jnp.float32
BF16 = jnp.bfloat16
VMEM = pl.BlockSpec(memory_space=pltpu.VMEM)
SMEM = pl.BlockSpec(memory_space=pltpu.SMEM)
HBM = pl.BlockSpec(memory_space=pltpu.HBM)
PARAMS = pltpu.CompilerParams(vmem_limit_bytes=40 * 1024 * 1024)


def dot(left, right):
    return jnp.dot(left, right, preferred_element_type=F32)


def dot_nt(left, right):
    return lax.dot_general(left, right, (((1,), (1,)), ((), ())), preferred_element_type=F32)


def dot_tn(left, right):
    return lax.dot_general(left, right, (((0,), (0,)), ((), ())), preferred_element_type=F32)


def halves(value):
    high = value.astype(BF16)
    return high, (value - high.astype(F32)).astype(BF16)


def iota(shape, axis):
    return lax.broadcasted_iota(jnp.int32, shape, axis)


def one_hot(condition):
    return jnp.where(condition, 1.0, 0.0).astype(BF16)


PACK_PARAMS = pltpu.CompilerParams(vmem_limit_bytes=62 * 1024 * 1024)


def basis_shift(blocks, slots):
    dof = blocks.shape[1]
    same = iota((dof, dof), 0) == iota((dof, dof), 1)
    total = sum(jnp.where(same, blocks[t], 0.0) for t in range(TYPES))
    mean = jnp.sum(jnp.sum(total, axis=1, keepdims=True), axis=0, keepdims=True) / (TYPES * dof)
    return MASS_SHIFT + 0.2 * slots * mean


def swap_blocks(piece):
    lane = iota(piece(0, 0).shape, 1)
    low = lane < META // 2
    out = []
    for tile in range(4):
        for part in range(2):
            first, second = piece(2 * part, tile // 2), piece(2 * part + 1, tile // 2)
            if tile % 2 == 0:
                second = pltpu.roll(second, META // 2, 1)
            else:
                first = pltpu.roll(first, META // 2, 1)
            out.append(jnp.where(low, first, second))
    return out


def given_to_gram():
    source, target = iota((TILE, TILE), 0), iota((TILE, TILE), 1)
    return one_hot((target // 16 == source % 16) & (target % 16 == source // 16))


def peers(pos, devices):
    odd = lax.rem(pos, jnp.int32(2))
    return (
        pos + 1 - 2 * odd,
        pos - 1 + 2 * odd,
        lax.rem(pos + devices // 2, jnp.int32(devices)),
    )


def targets(pos, ids, rows, devices):
    cap = rows // 4
    owner = lax.div(ids, jnp.int32(rows))
    goes = []
    for peer in peers(pos, devices):
        here = owner == peer
        for other in goes:
            here = here & ~other
        goes.append(here)
    flags = jnp.concatenate(
        [jnp.where(g, 1.0, 0.0) for g in goes] + [jnp.zeros((5, rows), F32)], axis=0
    )
    before = one_hot(iota((rows, rows), 0) < iota((rows, rows), 1))
    rank = dot(flags.astype(BF16), before).astype(jnp.int32)
    target = jnp.full((1, rows), -1, jnp.int32)
    for side in range(3):
        target = jnp.where(goes[side], rank[side:side + 1] + side * cap, target)
    return target


def fill_block(pick, loads, meta, out_ref):
    width = loads.shape[1]
    cap = pick.shape[0]
    twice = jnp.concatenate([pick, pick], axis=1)
    notes = dot_nt(twice, jnp.concatenate(halves(meta), axis=1))
    body = dot(twice, jnp.concatenate(halves(loads), axis=0))
    parts = width // META
    for part in range(parts):
        out_ref[part * cap:(part + 1) * cap, :] = body[:, part * META:(part + 1) * META]
    out_ref[parts * cap:, :] = notes[:cap // 2] + pltpu.roll(notes[cap // 2:], META // 2, 1)


def read_block(ref, width):
    parts = width // META
    cap = ref.shape[0] * 2 // (2 * parts + 1)
    body = jnp.concatenate([ref[part * cap:(part + 1) * cap, :] for part in range(parts)], axis=1)
    notes = ref[parts * cap:, :]
    notes = jnp.concatenate([notes, pltpu.roll(notes, META // 2, 1)], axis=0)
    return body, jnp.where(iota(notes.shape, 1) < META // 2, notes, 0.0)


def pack_first_kernel(devices, pos_ref, loads_hbm, rows_hbm, dens_hbm, cols_hbm, types_hbm,
                      first_ref, meta_ref, target_ref,
                      loads_ref, rows_ref, dens_ref, cols_ref, types_ref, sems):
    pairs = (
        (rows_hbm, rows_ref), (dens_hbm, dens_ref), (cols_hbm, cols_ref),
        (types_hbm, types_ref), (loads_hbm, loads_ref),
    )
    copies = [
        pltpu.make_async_copy(source, target, sems.at[number])
        for number, (source, target) in enumerate(pairs)
    ]
    for copy in copies:
        copy.start()
    for copy in copies[:4]:
        copy.wait()
    rows = loads_ref.shape[0]
    slots = dens_ref.shape[0]
    cap = rows // 4
    pos = pos_ref[0, 0]
    ids = rows_ref[...]
    owner = lax.div(ids, jnp.int32(rows))
    local = (ids - owner * rows + 1).astype(F32)
    target = targets(pos, ids, rows, devices)
    target_ref[...] = jnp.broadcast_to(target, target_ref.shape)

    density = dens_ref[...]
    kinds = types_ref[...]
    for kind in range(TYPES):
        meta_ref[kind * slots:(kind + 1) * slots, :] = jnp.where(kinds == kind, density, 0.0)
    meta_ref[3 * slots:4 * slots, :] = (cols_ref[...] - ids).astype(F32)
    meta_ref[4 * slots:, :] = jnp.zeros((META - 4 * slots, rows), F32)
    meta_ref[4 * slots:4 * slots + 1, :] = local
    meta_ref[4 * slots + 1:4 * slots + 2, :] = jnp.where(owner == pos, local, 0.0)

    copies[4].wait()
    pick = one_hot(iota((cap, rows), 0) + 2 * cap == target)
    fill_block(pick, loads_ref[...], meta_ref[...], first_ref)


def pack_second_kernel(target_hbm, meta_hbm, loads_hbm, core_ref, second_ref,
                       target_ref, meta_ref, loads_ref, sems):
    pairs = ((target_hbm, target_ref), (meta_hbm, meta_ref), (loads_hbm, loads_ref))
    copies = [
        pltpu.make_async_copy(source, target, sems.at[number])
        for number, (source, target) in enumerate(pairs)
    ]
    for copy in copies:
        copy.start()
    for copy in copies:
        copy.wait()
    rows = loads_ref.shape[0]
    cap = rows // 4
    for side, out_ref in enumerate((core_ref, second_ref)):
        pick = one_hot(iota((cap, rows), 0) + side * cap == target_ref[0:1, :])
        fill_block(pick, loads_ref[...], meta_ref[...], out_ref)


def reorder(parts, tiles):
    count = parts[0].shape[0]
    tall = [p[:, t * TILE:(t + 1) * TILE] for t in range(tiles) for p in parts]
    moved = dot(jnp.concatenate(tall, axis=0), given_to_gram()).astype(BF16)
    return [
        jnp.concatenate(
            [moved[(2 * t + p) * count:(2 * t + p + 1) * count] for t in range(tiles)], axis=1
        )
        for p in range(2)
    ]


def stacked_tiles(value, tiles):
    return jnp.concatenate([value[:, t * TILE:(t + 1) * TILE] for t in range(tiles)], axis=0)


def folded_rows(gram, cases):
    same_dof = iota((TILE, TILE), 0) % 16 == iota((TILE, TILE), 1) % 16
    gram = jnp.where(same_dof, gram, 0.0)
    return jnp.sum(gram.reshape(cases, TILE // cases, TILE), axis=1)


def prepare_kernel(slots, loads_ref, meta_ref, blocks_ref,
                   kept_ref, kept_meta_ref, mixer_ref, first_ref):
    rows, width = loads_ref.shape
    dof = blocks_ref.shape[1]
    tiles = width // TILE
    place = iota((rows, rows), 0) + 1
    own = one_hot(place == meta_ref[4 * slots + 1:4 * slots + 2, :].astype(jnp.int32))
    twice = jnp.concatenate([own, own], axis=1)
    moved = reorder(halves(loads_ref[...]), tiles)
    kept_ref[...] = dot(twice, jnp.concatenate(moved, axis=0))
    high, low = (stacked_tiles(part, tiles) for part in moved)
    gram = dot_tn(high, jnp.concatenate([high, low], axis=1))
    cross = gram[:, TILE:]
    first_ref[...] = folded_rows(gram[:, :TILE] + cross + cross.T, width // dof)
    kept_meta_ref[...] = dot_nt(twice, jnp.concatenate(halves(meta_ref[...]), axis=1))

    def dof_of(lane):
        return lane // 64 * 16 + lane % 16

    fold = one_hot(dof_of(iota((TILE, dof), 0)) == iota((TILE, dof), 1))
    unfold = one_hot(dof_of(iota((dof, TILE), 1)) == iota((dof, TILE), 0))
    same_case = iota((TILE, TILE), 0) // 16 % 4 == iota((TILE, TILE), 1) // 16 % 4
    for kind in range(TYPES):
        for copies, part in zip(((0, 2), (1,)), halves(blocks_ref[kind])):
            wide = dot(dot_nt(fold, part).astype(BF16), unfold)
            wide = jnp.where(same_case, wide, 0.0).astype(BF16)
            for copy in copies:
                start = (copy * TYPES + kind) * TILE
                mixer_ref[start:start + TILE, :] = wide


def arrange_kernel(slots, pos_ref, first_ref, core_ref, second_ref, kept_ref, kept_meta_ref,
                   geo_ref, field_ref, meta_ref, to_core_ref, to_chip_ref):
    rows, width = kept_ref.shape
    tiles = width // TILE
    edge = to_core_ref.shape[0]
    even = lax.rem(pos_ref[0, 0], jnp.int32(2)) == 0
    blocks = [read_block(ref, width) for ref in (first_ref, second_ref, core_ref)]
    arrived = jnp.concatenate([block[0] for block in blocks], axis=0)
    arrived_meta = jnp.concatenate([block[1] for block in blocks], axis=0)
    count = arrived.shape[0]
    unit = one_hot(iota((8, META), 1) == 4 * slots)
    tags = dot_nt(unit, arrived_meta.astype(BF16))[0:1]
    other = one_hot(iota((rows, count), 0) + 1 == tags.astype(jnp.int32))
    twice = jnp.concatenate([other, other], axis=1)
    moved = reorder(halves(arrived), tiles)
    geo = kept_ref[...] + dot(twice, jnp.concatenate(moved, axis=0))
    meta = kept_meta_ref[...] + dot(twice, jnp.concatenate(halves(arrived_meta), axis=0))
    meta_ref[...] = meta

    def send(lanes, value):
        head, tail = value[:edge], value[rows - edge:]
        to_core_ref[:, lanes] = jnp.where(even, tail, head)
        to_chip_ref[:, lanes] = jnp.where(even, head, tail)

    send(slice(width, None), meta)

    def piece(tile, part):
        start = tile * TILE + part * META
        return geo[:, start:start + META]

    for number, value in enumerate(swap_blocks(piece)):
        lanes = slice(number * META, (number + 1) * META)
        send(lanes, value)
        inner = slice(number % 2 * META, (number % 2 + 1) * META)
        for part, half in enumerate(halves(value)):
            field_ref[part, number // 2, :, inner] = half
    for part, half in enumerate(halves(geo)):
        for tile in range(tiles):
            geo_ref[part, tile] = half[:, tile * TILE:(tile + 1) * TILE]


def stencil_rows(meta, slots, first):
    lane = iota((HALO, META), 1)
    spot = iota((HALO, TILE), 1)
    centre = iota((HALO, 1), 0) + first
    sums = [jnp.zeros((HALO, TILE), F32) for _ in range(TYPES)]
    for slot in range(slots):
        column = centre + meta[:, 3 * slots + slot:3 * slots + slot + 1].astype(jnp.int32)
        hit = spot == column
        for kind in range(TYPES):
            weight = meta[:, kind * slots + slot:kind * slots + slot + 1]
            sums[kind] += jnp.where(hit, weight, 0.0)
    out = []
    for kind in range(TYPES):
        inside = (lane >= kind * slots) & (lane < (kind + 1) * slots)
        total = jnp.sum(jnp.where(inside, meta, 0.0), axis=1, keepdims=True)
        high, low = halves(jnp.where(spot == centre, total, 0.0) - sums[kind])
        out.append(jnp.concatenate([high, high, low], axis=1))
    return out


def gathered(weights, near, fine):
    return halves(dot(weights, jnp.concatenate([near, fine, near], axis=0)))


def mixed(buckets, mixer_ref, count):
    highs = [buckets[0, kind, :count, :] for kind in range(TYPES)]
    lows = [buckets[1, kind, :count, :] for kind in range(TYPES)]
    return dot(jnp.concatenate(highs + highs + lows, axis=1), mixer_ref[...])


def interior_kernel(slots, field_ref, meta_ref, mixer_ref, blocks_ref,
                    inner_ref, weights_ref, stencil, buckets):
    tiles, rows = field_ref.shape[1:3]
    edge = ITERS * HALO
    shift = basis_shift(blocks_ref[...], slots)
    inside = rows - 2 * HALO

    def build(chunk, carry):
        first = pl.multiple_of(chunk * HALO, HALO)
        start = pl.multiple_of(chunk * HALO + HALO, HALO)
        for kind, value in enumerate(
            stencil_rows(meta_ref[pl.ds(start, HALO), :], slots, first + HALO)
        ):
            stencil[kind, pl.ds(first, HALO), :] = value
        return carry

    lax.fori_loop(0, inside // HALO, build, 0)

    def build_outer(side, chunk):
        first = chunk * HALO
        start = first + side * (rows - edge)
        spot = first + edge if side == 0 else first + rows - 2 * edge
        for kind, value in enumerate(stencil_rows(meta_ref[start:start + HALO, :], slots, spot)):
            weights_ref[side, kind, first:first + HALO, :] = value

    for step in range(ITERS - 1):
        begin = HALO * (step + 1)
        blank = jnp.zeros((begin, TILE), BF16)
        for part in range(2):
            for tile in range(tiles):
                inner_ref[step, part, tile, :begin, :] = blank
                inner_ref[step, part, tile, rows - begin:, :] = blank
    for step in range(ITERS):
        skip = HALO * step
        count = inside - 2 * skip
        begin = HALO + skip
        weights = jnp.concatenate(
            [stencil[kind, skip:inside - skip, :] for kind in range(TYPES)], axis=0
        )

        def read(part, tile, block):
            if step == 0:
                return field_ref[part, tile, block, :]
            return inner_ref[step - 1, part, tile, block, :]

        for tile in range(tiles):
            every = slice(0, rows)
            for part, half in enumerate(
                gathered(weights, read(0, tile, every), read(1, tile, every))
            ):
                for kind in range(TYPES):
                    buckets[part, kind, tile * count:(tile + 1) * count, :] = (
                        half[kind * count:(kind + 1) * count]
                    )
        for side in range(2):
            build_outer(side, step)
        applied = mixed(buckets, mixer_ref, tiles * count)
        block = slice(begin, begin + count)
        for tile in range(tiles):
            here = read(0, tile, block).astype(F32) + read(1, tile, block).astype(F32)
            value = applied[tile * count:(tile + 1) * count] + (MASS_SHIFT - shift) * here
            for part, half in enumerate(halves(value)):
                inner_ref[step, part, tile, block, :] = half


def sides_kernel(slots, pos_ref, core_ref, chip_ref, field_ref, inner_ref, weights_ref, mixer_ref,
                 blocks_ref, geo_ref, first_ref, basis_ref, moments_ref, v_refs, meta_refs, stencil, buckets):
    tiles, rows = field_ref.shape[1:3]
    width = tiles * TILE
    dof = blocks_ref.shape[1]
    cases = width // dof
    edge = ITERS * HALO
    outer = edge - HALO
    count = edge
    rest = TILE - edge
    shift = basis_shift(blocks_ref[...], slots)
    even = lax.rem(pos_ref[0, 0], jnp.int32(2)) == 0

    for tile in range(tiles + 1):
        lanes = slice(tile * TILE, (tile + 1) * TILE) if tile < tiles else slice(width, None)
        core, chip = core_ref[:, lanes], chip_ref[:, lanes]
        for side, value in enumerate((jnp.where(even, chip, core), jnp.where(even, core, chip))):
            if tile == tiles:
                meta_refs[side] = value
            else:
                for part, half in enumerate(halves(value)):
                    v_refs[0, side, part, tile] = half

    def build(side):
        for first in range(0, outer, HALO):
            start = first + HALO * (1 - side)
            spot = first + HALO if side == 0 else first + rows - edge
            for kind, value in enumerate(
                stencil_rows(meta_refs[side, start:start + HALO, :], slots, spot)
            ):
                stencil[side, kind, first:first + HALO, :] = value

    def window(step, side, part, tile):
        near = v_refs[step, side, part, tile]
        if step == 0:
            if side == 0:
                return jnp.concatenate([near, field_ref[part, tile, :rest, :]], axis=0)
            return jnp.concatenate([field_ref[part, tile, rows - rest:, :], near], axis=0)
        blank = jnp.zeros((HALO * step, TILE), BF16)
        begin = HALO * step
        if side == 0:
            far = inner_ref[step - 1, part, tile, begin:rest, :]
            return jnp.concatenate([blank, near, far], axis=0)
        far = inner_ref[step - 1, part, tile, rows - rest:rows - begin, :]
        return jnp.concatenate([far, near, blank], axis=0)

    def weight_rows(step, side, kind):
        keep = outer - HALO * step
        if side == 0:
            pieces = [weights_ref[0, kind, :count - keep, :]]
            if keep:
                pieces.insert(0, stencil[0, kind, outer - keep:, :])
        else:
            pieces = [weights_ref[1, kind, keep:, :]]
            if keep:
                pieces.append(stencil[1, kind, :keep, :])
        return jnp.concatenate(pieces, axis=0)

    def convert(step):
        begin = HALO * step
        for half in range(2):

            def piece(tile, part):
                lanes = slice(part * META, (part + 1) * META)
                return jnp.concatenate(
                    [
                        v_refs[step, 0, half, tile, count - begin:, lanes],
                        inner_ref[step - 1, half, tile, begin:rows - begin, lanes],
                        v_refs[step, 1, half, tile, :begin, lanes],
                    ],
                    axis=0,
                )

            for number, value in enumerate(swap_blocks(piece)):
                lanes = slice(number % 2 * META, (number % 2 + 1) * META)
                basis_ref[step - 1, half, number // 2, :, lanes] = value

    def tall(step, part):
        if step == 0:
            return jnp.concatenate([geo_ref[part, tile] for tile in range(tiles)], axis=0)
        return jnp.concatenate([basis_ref[step - 1, part, tile] for tile in range(tiles)], axis=0)

    def mixed_gram(high, low):
        return folded_rows(high[:, :TILE] + high[:, TILE:] + low, cases)

    def even_gram(high):
        cross = high[:, TILE:]
        return folded_rows(high[:, :TILE] + cross + cross.T, cases)

    sums = [first_ref[...]]
    for step in range(ITERS):
        centres = []
        for side in range(2):
            if step == 0:
                build(side)
            weights = jnp.concatenate(
                [weight_rows(step, side, kind) for kind in range(TYPES)], axis=0
            )
            for tile in range(tiles):
                row = (side * tiles + tile) * count
                near, fine = (window(step, side, part, tile) for part in range(2))
                first = HALO * (step + 1) if side == 0 else TILE - HALO * (step + 1) - count
                centres.append((near[first:first + count], fine[first:first + count]))
                for part, half in enumerate(gathered(weights, near, fine)):
                    for kind in range(TYPES):
                        buckets[part, kind, row:row + count, :] = (
                            half[kind * count:(kind + 1) * count]
                        )
        applied = mixed(buckets, mixer_ref, 2 * tiles * count)
        for side in range(2):
            for tile in range(tiles):
                number = side * tiles + tile
                near, fine = centres[number]
                here = near.astype(F32) + fine.astype(F32)
                value = applied[number * count:(number + 1) * count] + (MASS_SHIFT - shift) * here
                for part, half in enumerate(halves(value)):
                    v_refs[step + 1, side, part, tile] = half

        convert(step + 1)
        if step == 1:
            others = [tall(k, part) for k in range(3) for part in range(2)]
            high = dot_tn(tall(1, 0), jnp.concatenate(others, axis=1))
            low = dot_tn(tall(1, 1), jnp.concatenate([others[0], others[4]], axis=1))
            sums.append(mixed_gram(high[:, :2 * TILE], low[:, :TILE]))
            sums.append(even_gram(high[:, 2 * TILE:4 * TILE]))
            sums.append(mixed_gram(high[:, 4 * TILE:], low[:, TILE:]))
        elif step == 2:
            others = [tall(k, part) for k in range(2, 4) for part in range(2)]
            high = dot_tn(tall(2, 0), jnp.concatenate(others, axis=1))
            low = dot_tn(tall(2, 1), others[2])
            sums.append(even_gram(high[:, :2 * TILE]))
            sums.append(mixed_gram(high[:, 2 * TILE:], low))

    remainder = jnp.concatenate(sums, axis=0)
    pieces = []
    for _ in range(3):
        pieces.append(remainder.astype(BF16))
        remainder = remainder - pieces[-1].astype(F32)
    collect = one_hot(iota((TILE, META), 0) // 16 == iota((TILE, META), 1) % 16)
    folded = dot(jnp.concatenate(pieces, axis=1), jnp.concatenate([collect] * 3, axis=0))
    group = iota((cases, META), 1) // cases
    moments = jnp.zeros((cases, META), F32)
    for number in range(2 * ITERS):
        part = folded[number * cases:(number + 1) * cases]
        moments = jnp.where(group == number, part, moments)
    for device in range(moments_ref.shape[0]):
        moments_ref[device] = moments


def refined_reciprocal(value):
    guess = pl.reciprocal(value, approx=True)
    for _ in range(2):
        guess = guess * (2.0 - value * guess)
    return guess


def finish_kernel(slots, moments_ref, blocks_ref, geo_ref, basis_ref,
                  solution_hbm, residual_hbm, out_refs, sems):
    rows, width = out_refs.shape[1:]
    dof = blocks_ref.shape[1]
    cases = width // dof
    tiles = width // TILE
    shift = basis_shift(blocks_ref[...], slots)
    moments = moments_ref[0]
    for device in range(1, moments_ref.shape[0]):
        moments = moments + moments_ref[device]
    group = iota((cases, META), 1) // cases
    system = []
    for row in range(ITERS):
        plain = moments if row == 0 else pltpu.roll(moments, META - cases * row, 1)
        ahead = pltpu.roll(moments, META - cases * (row + 1), 1)
        target = pltpu.roll(moments, cases * (ITERS - row), 1)
        system.append(jnp.where(group < ITERS, ahead + shift * plain, target))
    system = jnp.concatenate(system, axis=0)
    size = ITERS * cases
    index = iota((size, 1), 0)
    for pivot in range(0, size, 2):
        column_a = jnp.broadcast_to(system[:, pivot:pivot + 1], (size, META))
        column_b = jnp.broadcast_to(system[:, pivot + 1:pivot + 2], (size, META))
        line_a = system[pivot:pivot + 1, :]
        line_b = system[pivot + 1:pivot + 2, :]
        above = column_b[pivot:pivot + 1, :]
        inverse = refined_reciprocal(column_a[pivot:pivot + 1, :])
        factor = column_a[pivot + 1:pivot + 2, :] * inverse
        corner = column_b[pivot + 1:pivot + 2, :] - factor * above
        line_b = (line_b - factor * line_a) * refined_reciprocal(corner)
        line_a = (line_a - above * line_b) * inverse
        update = system - column_a * line_a - column_b * line_b
        system = jnp.where(index == pivot, line_a, jnp.where(index == pivot + 1, line_b, update))

    unit = jnp.where(iota((cases, META), 1) % cases == iota((cases, META), 0), 1.0, 0.0)
    answers = []
    for row in range(ITERS):
        part = jnp.where(group == ITERS, system[row * cases:(row + 1) * cases], 0.0)
        step = cases
        while step < META:
            part = part + pltpu.roll(part, step, 1)
            step *= 2
        answers.append(part)
    left_over = [unit - shift * answers[0]]
    for row in range(1, ITERS):
        left_over.append(-(answers[row - 1] + shift * answers[row]))
    left_over.append(-answers[ITERS - 1])

    meets = iota((TILE, TILE), 0) % 16 == iota((TILE, TILE), 1) // 16

    def spread(parts):
        highs, lows = [], []
        for part in parts:
            tall = jnp.broadcast_to(part[:, None, :], (cases, TILE // cases, META))
            tall = tall.reshape(TILE, META)
            wide = jnp.concatenate([tall] * (TILE // META), axis=1)
            high, low = halves(jnp.where(meets, wide, 0.0))
            highs.append(high)
            lows.append(low)
        return jnp.concatenate(highs + highs + lows, axis=0)

    def tall(term, part):
        if term == 0:
            return jnp.concatenate([geo_ref[part, tile] for tile in range(tiles)], axis=0)
        return jnp.concatenate([basis_ref[term - 1, part, tile] for tile in range(tiles)], axis=0)

    copies = []
    for number, (out_hbm, parts) in enumerate(
        ((solution_hbm, answers), (residual_hbm, left_over))
    ):
        matrix = spread(parts)
        terms = matrix.shape[0] // (3 * TILE)
        highs = [tall(term, 0) for term in range(terms)]
        lows = [tall(term, 1) for term in range(terms)]
        value = dot(jnp.concatenate(highs + lows + highs, axis=1), matrix)
        for tile in range(tiles):
            lanes = slice(tile * TILE, (tile + 1) * TILE)
            out_refs[number, :, lanes] = value[tile * rows:(tile + 1) * rows]
        copies.append(pltpu.make_async_copy(out_refs.at[number], out_hbm, sems.at[number]))
        copies[number].start()
    for copy in copies:
        copy.wait()


def on_device(loads, row_ids, densities, block_cols, block_types, ref_blocks):
    rows, width = loads.shape
    slots = densities.shape[1]
    cases = width // ref_blocks.shape[1]
    cap = rows // 4
    edge = ITERS * HALO
    tiles = width // TILE
    devices = lax.axis_size("sub")
    position = lax.axis_index("sub").astype(jnp.int32).reshape(1, 1)
    shape = jax.ShapeDtypeStruct
    same_chip = [(i, i ^ 1) for i in range(devices)]
    next_chip = [(i, i + 1) for i in range(1, devices - 1, 2)]
    next_chip += [(i + 1, i) for i in range(1, devices - 1, 2)]
    across = [(i, (i + devices // 2) % devices) for i in range(devices)]

    block = shape((cap * width // META + cap // 2, META), F32)
    to_first, meta, target = pl.pallas_call(
        functools.partial(pack_first_kernel, devices),
        out_shape=(block, shape((META, rows), F32), shape((8, rows), jnp.int32)),
        in_specs=[SMEM] + [HBM] * 5,
        out_specs=(VMEM,) * 3,
        scratch_shapes=[
            pltpu.VMEM((rows, width), F32),
            pltpu.VMEM((1, rows), jnp.int32),
            pltpu.VMEM((slots, rows), F32),
            pltpu.VMEM((slots, rows), jnp.int32),
            pltpu.VMEM((slots, rows), jnp.int32),
            pltpu.SemaphoreType.DMA((5,)),
        ],
        compiler_params=PACK_PARAMS,
        name="pack_first",
    )(position, loads, row_ids.reshape(1, rows), densities.T, block_cols.T, block_types.T)
    from_first = lax.ppermute(to_first, "sub", across)

    to_core, to_second = pl.pallas_call(
        pack_second_kernel,
        out_shape=(block, block),
        in_specs=[HBM] * 3,
        out_specs=(VMEM,) * 2,
        scratch_shapes=[
            pltpu.VMEM((8, rows), jnp.int32),
            pltpu.VMEM((META, rows), F32),
            pltpu.VMEM((rows, width), F32),
            pltpu.SemaphoreType.DMA((3,)),
        ],
        compiler_params=PACK_PARAMS,
        name="pack_second",
    )(target, meta, loads)
    from_second = lax.ppermute(to_second, "sub", next_chip)
    from_core = lax.ppermute(to_core, "sub", same_chip)

    mixer_shape = shape((3 * TYPES * TILE, TILE), BF16)
    kept, kept_meta, mixer, first = pl.pallas_call(
        functools.partial(prepare_kernel, slots),
        out_shape=(
            shape((rows, width), F32),
            shape((rows, META), F32),
            mixer_shape,
            shape((cases, TILE), F32),
        ),
        in_specs=[VMEM] * 3,
        out_specs=(VMEM,) * 4,
        compiler_params=PARAMS,
        cost_estimate=pl.CostEstimate(
            flops=4_000_000_000, bytes_accessed=4_000_000, transcendentals=0
        ),
        name="prepare",
    )(loads, meta, ref_blocks)

    border = shape((edge, width + META), F32)
    pair = shape((2, tiles, rows, TILE), BF16)
    geo, field, geo_meta, to_core, to_chip = pl.pallas_call(
        functools.partial(arrange_kernel, slots),
        out_shape=(pair, pair, shape((rows, META), F32), border, border),
        in_specs=[SMEM] + [VMEM] * 5,
        out_specs=(VMEM,) * 5,
        compiler_params=PARAMS,
        name="arrange",
    )(position, from_first, from_core, from_second, kept, kept_meta)

    halo_chip = lax.ppermute(to_chip, "sub", next_chip)
    halo_core = lax.ppermute(to_core, "sub", same_chip)

    basis_shape = shape((ITERS, 2, tiles, rows, TILE), BF16)
    inner, weights = pl.pallas_call(
        functools.partial(interior_kernel, slots),
        out_shape=(basis_shape, shape((2, TYPES, edge, 3 * TILE), BF16)),
        in_specs=[VMEM] * 4,
        out_specs=(VMEM,) * 2,
        scratch_shapes=[
            pltpu.VMEM((TYPES, rows - 2 * HALO, 3 * TILE), BF16),
            pltpu.VMEM((2, TYPES, tiles * (rows - 2 * HALO), TILE), BF16),
        ],
        compiler_params=PARAMS,
        cost_estimate=pl.CostEstimate(
            flops=10_000_000_000, bytes_accessed=8_000_000, transcendentals=0
        ),
        name="interior",
    )(field, geo_meta, mixer, ref_blocks)

    basis, moments = pl.pallas_call(
        functools.partial(sides_kernel, slots),
        out_shape=(basis_shape, shape((devices, cases, META), F32)),
        in_specs=[SMEM] + [VMEM] * 9,
        out_specs=(VMEM,) * 2,
        scratch_shapes=[
            pltpu.VMEM((ITERS + 1, 2, 2, tiles, edge, TILE), BF16),
            pltpu.VMEM((2, edge, META), F32),
            pltpu.VMEM((2, TYPES, edge - HALO, 3 * TILE), BF16),
            pltpu.VMEM((2, TYPES, 2 * tiles * edge, TILE), BF16),
        ],
        compiler_params=PARAMS,
        name="sides",
    )(position, halo_core, halo_chip, field, inner, weights, mixer, ref_blocks, geo, first)

    moments = lax.all_to_all(moments, "sub", split_axis=0, concat_axis=0, tiled=True)

    return pl.pallas_call(
        functools.partial(finish_kernel, slots),
        out_shape=(shape((rows, width), F32), shape((rows, width), F32)),
        in_specs=[VMEM] * 4,
        out_specs=(HBM,) * 2,
        scratch_shapes=[pltpu.VMEM((2, rows, width), F32), pltpu.SemaphoreType.DMA((2,))],
        compiler_params=PARAMS,
        name="finish",
    )(moments, ref_blocks, geo, basis)


def solution(mesh):
    placed = (
        P(("groups", "sub"), None),
        P(("groups", "sub")),
        P(("groups", "sub"), None),
        P(("groups", "sub"), None),
        P(("groups", "sub"), None),
        P(),
    )
    return jax.shard_map(
        on_device,
        mesh=mesh,
        in_specs=placed,
        out_specs=(P(("groups", "sub"), None), P(("groups", "sub"), None)),
        check_vma=False,
    )
```

```python
import functools

import jax
import jax.numpy as jnp
from jax import lax
from jax.experimental import pallas as pl
from jax.experimental.pallas import tpu as pltpu
from jax.sharding import PartitionSpec as P

HALO = 32
TYPES = 3
ITERS = 3
MASS_SHIFT = 0.5
META = 128
TILE = 256

F32 = jnp.float32
BF16 = jnp.bfloat16
VMEM = pl.BlockSpec(memory_space=pltpu.VMEM)
SMEM = pl.BlockSpec(memory_space=pltpu.SMEM)
HBM = pl.BlockSpec(memory_space=pltpu.HBM)
PARAMS = pltpu.CompilerParams(vmem_limit_bytes=40 * 1024 * 1024)


def dot(left, right):
    return jnp.dot(left, right, preferred_element_type=F32)


def dot_nt(left, right):
    return lax.dot_general(left, right, (((1,), (1,)), ((), ())), preferred_element_type=F32)


def dot_tn(left, right):
    return lax.dot_general(left, right, (((0,), (0,)), ((), ())), preferred_element_type=F32)


def halves(value):
    high = value.astype(BF16)
    return high, (value - high.astype(F32)).astype(BF16)


def iota(shape, axis):
    return lax.broadcasted_iota(jnp.int32, shape, axis)


def one_hot(condition):
    return jnp.where(condition, 1.0, 0.0).astype(BF16)


PACK_PARAMS = pltpu.CompilerParams(vmem_limit_bytes=62 * 1024 * 1024)


def basis_shift(blocks, slots):
    dof = blocks.shape[1]
    same = iota((dof, dof), 0) == iota((dof, dof), 1)
    total = sum(jnp.where(same, blocks[t], 0.0) for t in range(TYPES))
    mean = jnp.sum(jnp.sum(total, axis=1, keepdims=True), axis=0, keepdims=True) / (TYPES * dof)
    return MASS_SHIFT + 0.2 * slots * mean


def swap_blocks(piece):
    lane = iota(piece(0, 0).shape, 1)
    low = lane < META // 2
    out = []
    for tile in range(4):
        for part in range(2):
            first, second = piece(2 * part, tile // 2), piece(2 * part + 1, tile // 2)
            if tile % 2 == 0:
                second = pltpu.roll(second, META // 2, 1)
            else:
                first = pltpu.roll(first, META // 2, 1)
            out.append(jnp.where(low, first, second))
    return out


def given_to_gram():
    source, target = iota((TILE, TILE), 0), iota((TILE, TILE), 1)
    return one_hot((target // 16 == source % 16) & (target % 16 == source // 16))


def peers(pos, devices):
    odd = lax.rem(pos, jnp.int32(2))
    return (
        pos + 1 - 2 * odd,
        pos - 1 + 2 * odd,
        lax.rem(pos + devices // 2, jnp.int32(devices)),
    )


def far_first(pos, devices):
    half = devices // 2
    group = (pos % half + 1) // 2 % max(half // 2, 1)
    return group % 2 == 1


def targets(pos, ids, rows, devices):
    cap = rows // 4
    owner = lax.div(ids, jnp.int32(rows))
    goes = []
    for peer in peers(pos, devices):
        here = owner == peer
        for other in goes:
            here = here & ~other
        goes.append(here)
    flags = jnp.concatenate(
        [jnp.where(g, 1.0, 0.0) for g in goes] + [jnp.zeros((5, rows), F32)], axis=0
    )
    before = one_hot(iota((rows, rows), 0) < iota((rows, rows), 1))
    rank = dot(flags.astype(BF16), before).astype(jnp.int32)
    target = jnp.full((1, rows), -1, jnp.int32)
    for side in range(3):
        target = jnp.where(goes[side], rank[side:side + 1] + side * cap, target)
    return target


def fill_block(pick, loads, meta, out_ref):
    width = loads.shape[1]
    cap = pick.shape[0]
    twice = jnp.concatenate([pick, pick], axis=1)
    notes = dot_nt(twice, jnp.concatenate(halves(meta), axis=1))
    body = dot(twice, jnp.concatenate(halves(loads), axis=0))
    parts = width // META
    for part in range(parts):
        out_ref[part * cap:(part + 1) * cap, :] = body[:, part * META:(part + 1) * META]
    out_ref[parts * cap:, :] = notes[:cap // 2] + pltpu.roll(notes[cap // 2:], META // 2, 1)


def read_block(ref, width):
    parts = width // META
    cap = ref.shape[0] * 2 // (2 * parts + 1)
    body = jnp.concatenate([ref[part * cap:(part + 1) * cap, :] for part in range(parts)], axis=1)
    notes = ref[parts * cap:, :]
    notes = jnp.concatenate([notes, pltpu.roll(notes, META // 2, 1)], axis=0)
    return body, jnp.where(iota(notes.shape, 1) < META // 2, notes, 0.0)


def pack_first_kernel(devices, pos_ref, loads_hbm, rows_hbm, dens_hbm, cols_hbm, types_hbm,
                      first_ref, meta_ref, target_ref,
                      loads_ref, rows_ref, dens_ref, cols_ref, types_ref, sems):
    pairs = (
        (rows_hbm, rows_ref), (dens_hbm, dens_ref), (cols_hbm, cols_ref),
        (types_hbm, types_ref), (loads_hbm, loads_ref),
    )
    copies = [
        pltpu.make_async_copy(source, target, sems.at[number])
        for number, (source, target) in enumerate(pairs)
    ]
    for copy in copies:
        copy.start()
    for copy in copies[:4]:
        copy.wait()
    rows = loads_ref.shape[0]
    slots = dens_ref.shape[0]
    cap = rows // 4
    pos = pos_ref[0, 0]
    ids = rows_ref[...]
    owner = lax.div(ids, jnp.int32(rows))
    local = (ids - owner * rows + 1).astype(F32)
    target = targets(pos, ids, rows, devices)
    target_ref[...] = jnp.broadcast_to(target, target_ref.shape)

    density = dens_ref[...]
    kinds = types_ref[...]
    for kind in range(TYPES):
        meta_ref[kind * slots:(kind + 1) * slots, :] = jnp.where(kinds == kind, density, 0.0)
    meta_ref[3 * slots:4 * slots, :] = (cols_ref[...] - ids).astype(F32)
    meta_ref[4 * slots:, :] = jnp.zeros((META - 4 * slots, rows), F32)
    meta_ref[4 * slots:4 * slots + 1, :] = local
    meta_ref[4 * slots + 1:4 * slots + 2, :] = jnp.where(owner == pos, local, 0.0)

    copies[4].wait()
    side = jnp.where(far_first(pos, devices), 2, 1)
    pick = one_hot(iota((cap, rows), 0) + side * cap == target)
    fill_block(pick, loads_ref[...], meta_ref[...], first_ref)


def pack_second_kernel(devices, pos_ref, target_hbm, meta_hbm, loads_hbm, core_ref, second_ref,
                       target_ref, meta_ref, loads_ref, sems):
    pairs = ((target_hbm, target_ref), (meta_hbm, meta_ref), (loads_hbm, loads_ref))
    copies = [
        pltpu.make_async_copy(source, target, sems.at[number])
        for number, (source, target) in enumerate(pairs)
    ]
    for copy in copies:
        copy.start()
    for copy in copies:
        copy.wait()
    rows = loads_ref.shape[0]
    cap = rows // 4
    late = jnp.where(far_first(pos_ref[0, 0], devices), 1, 2)
    for side, out_ref in ((late, second_ref), (0, core_ref)):
        pick = one_hot(iota((cap, rows), 0) + side * cap == target_ref[0:1, :])
        fill_block(pick, loads_ref[...], meta_ref[...], out_ref)


def reorder(parts, tiles):
    count = parts[0].shape[0]
    tall = [p[:, t * TILE:(t + 1) * TILE] for t in range(tiles) for p in parts]
    moved = dot(jnp.concatenate(tall, axis=0), given_to_gram()).astype(BF16)
    return [
        jnp.concatenate(
            [moved[(2 * t + p) * count:(2 * t + p + 1) * count] for t in range(tiles)], axis=1
        )
        for p in range(2)
    ]


def stacked_tiles(value, tiles):
    return jnp.concatenate([value[:, t * TILE:(t + 1) * TILE] for t in range(tiles)], axis=0)


def folded_rows(gram, cases):
    same_dof = iota((TILE, TILE), 0) % 16 == iota((TILE, TILE), 1) % 16
    gram = jnp.where(same_dof, gram, 0.0)
    return jnp.sum(gram.reshape(cases, TILE // cases, TILE), axis=1)


def prepare_kernel(slots, loads_ref, meta_ref, blocks_ref,
                   kept_ref, kept_meta_ref, mixer_ref, first_ref):
    rows, width = loads_ref.shape
    dof = blocks_ref.shape[1]
    tiles = width // TILE
    place = iota((rows, rows), 0) + 1
    own = one_hot(place == meta_ref[4 * slots + 1:4 * slots + 2, :].astype(jnp.int32))
    twice = jnp.concatenate([own, own], axis=1)
    moved = reorder(halves(loads_ref[...]), tiles)
    kept_ref[...] = dot(twice, jnp.concatenate(moved, axis=0))
    high, low = (stacked_tiles(part, tiles) for part in moved)
    gram = dot_tn(high, jnp.concatenate([high, low], axis=1))
    cross = gram[:, TILE:]
    first_ref[...] = folded_rows(gram[:, :TILE] + cross + cross.T, width // dof)
    kept_meta_ref[...] = dot_nt(twice, jnp.concatenate(halves(meta_ref[...]), axis=1))

    def dof_of(lane):
        return lane // 64 * 16 + lane % 16

    fold = one_hot(dof_of(iota((TILE, dof), 0)) == iota((TILE, dof), 1))
    unfold = one_hot(dof_of(iota((dof, TILE), 1)) == iota((dof, TILE), 0))
    same_case = iota((TILE, TILE), 0) // 16 % 4 == iota((TILE, TILE), 1) // 16 % 4
    for kind in range(TYPES):
        for copies, part in zip(((0, 2), (1,)), halves(blocks_ref[kind])):
            wide = dot(dot_nt(fold, part).astype(BF16), unfold)
            wide = jnp.where(same_case, wide, 0.0).astype(BF16)
            for copy in copies:
                start = (copy * TYPES + kind) * TILE
                mixer_ref[start:start + TILE, :] = wide


def arrange_kernel(slots, pos_ref, kept_ref, kept_meta_ref, core_ref, first_ref, second_ref,
                   geo_ref, field_ref, meta_ref, to_core_ref, to_chip_ref):
    rows, width = kept_ref.shape
    tiles = width // TILE
    edge = to_core_ref.shape[0]
    even = lax.rem(pos_ref[0, 0], jnp.int32(2)) == 0
    blocks = [read_block(ref, width) for ref in (core_ref, first_ref, second_ref)]
    arrived = jnp.concatenate([block[0] for block in blocks], axis=0)
    arrived_meta = jnp.concatenate([block[1] for block in blocks], axis=0)
    count = arrived.shape[0]
    unit = one_hot(iota((8, META), 1) == 4 * slots)
    tags = dot_nt(unit, arrived_meta.astype(BF16))[0:1]
    other = one_hot(iota((rows, count), 0) + 1 == tags.astype(jnp.int32))
    twice = jnp.concatenate([other, other], axis=1)
    moved = reorder(halves(arrived), tiles)
    geo = kept_ref[...] + dot(twice, jnp.concatenate(moved, axis=0))
    meta = kept_meta_ref[...] + dot(twice, jnp.concatenate(halves(arrived_meta), axis=0))
    meta_ref[...] = meta

    def send(lanes, value):
        head, tail = value[:edge], value[rows - edge:]
        to_core_ref[:, lanes] = jnp.where(even, tail, head)
        to_chip_ref[:, lanes] = jnp.where(even, head, tail)

    send(slice(width, None), meta)

    def piece(tile, part):
        start = tile * TILE + part * META
        return geo[:, start:start + META]

    for number, value in enumerate(swap_blocks(piece)):
        lanes = slice(number * META, (number + 1) * META)
        send(lanes, value)
        inner = slice(number % 2 * META, (number % 2 + 1) * META)
        for part, half in enumerate(halves(value)):
            field_ref[part, number // 2, :, inner] = half
    for part, half in enumerate(halves(geo)):
        for tile in range(tiles):
            geo_ref[part, tile] = half[:, tile * TILE:(tile + 1) * TILE]


def stencil_rows(meta, slots, first):
    lane = iota((HALO, META), 1)
    spot = iota((HALO, TILE), 1)
    centre = iota((HALO, 1), 0) + first
    sums = [jnp.zeros((HALO, TILE), F32) for _ in range(TYPES)]
    for slot in range(slots):
        column = centre + meta[:, 3 * slots + slot:3 * slots + slot + 1].astype(jnp.int32)
        hit = spot == column
        for kind in range(TYPES):
            weight = meta[:, kind * slots + slot:kind * slots + slot + 1]
            sums[kind] += jnp.where(hit, weight, 0.0)
    out = []
    for kind in range(TYPES):
        inside = (lane >= kind * slots) & (lane < (kind + 1) * slots)
        total = jnp.sum(jnp.where(inside, meta, 0.0), axis=1, keepdims=True)
        high, low = halves(jnp.where(spot == centre, total, 0.0) - sums[kind])
        out.append(jnp.concatenate([high, high, low], axis=1))
    return out


def gathered(weights, near, fine):
    return halves(dot(weights, jnp.concatenate([near, fine, near], axis=0)))


def mixed(buckets, mixer_ref, count):
    highs = [buckets[0, kind, :count, :] for kind in range(TYPES)]
    lows = [buckets[1, kind, :count, :] for kind in range(TYPES)]
    return dot(jnp.concatenate(highs + highs + lows, axis=1), mixer_ref[...])


def interior_kernel(slots, field_ref, meta_ref, mixer_ref, blocks_ref,
                    inner_ref, weights_ref, stencil, buckets):
    tiles, rows = field_ref.shape[1:3]
    edge = ITERS * HALO
    shift = basis_shift(blocks_ref[...], slots)
    inside = rows - 2 * HALO

    def build(chunk, carry):
        first = pl.multiple_of(chunk * HALO, HALO)
        start = pl.multiple_of(chunk * HALO + HALO, HALO)
        for kind, value in enumerate(
            stencil_rows(meta_ref[pl.ds(start, HALO), :], slots, first + HALO)
        ):
            stencil[kind, pl.ds(first, HALO), :] = value
        return carry

    lax.fori_loop(0, inside // HALO, build, 0)

    def build_outer(side, chunk):
        first = chunk * HALO
        start = first + side * (rows - edge)
        spot = first + edge if side == 0 else first + rows - 2 * edge
        for kind, value in enumerate(stencil_rows(meta_ref[start:start + HALO, :], slots, spot)):
            weights_ref[side, kind, first:first + HALO, :] = value

    for step in range(ITERS - 1):
        begin = HALO * (step + 1)
        blank = jnp.zeros((begin, TILE), BF16)
        for part in range(2):
            for tile in range(tiles):
                inner_ref[step, part, tile, :begin, :] = blank
                inner_ref[step, part, tile, rows - begin:, :] = blank
    for step in range(ITERS):
        skip = HALO * step
        count = inside - 2 * skip
        begin = HALO + skip
        weights = jnp.concatenate(
            [stencil[kind, skip:inside - skip, :] for kind in range(TYPES)], axis=0
        )

        def read(part, tile, block):
            if step == 0:
                return field_ref[part, tile, block, :]
            return inner_ref[step - 1, part, tile, block, :]

        for tile in range(tiles):
            every = slice(0, rows)
            for part, half in enumerate(
                gathered(weights, read(0, tile, every), read(1, tile, every))
            ):
                for kind in range(TYPES):
                    buckets[part, kind, tile * count:(tile + 1) * count, :] = (
                        half[kind * count:(kind + 1) * count]
                    )
        for side in range(2):
            build_outer(side, step)
        applied = mixed(buckets, mixer_ref, tiles * count)
        block = slice(begin, begin + count)
        for tile in range(tiles):
            here = read(0, tile, block).astype(F32) + read(1, tile, block).astype(F32)
            value = applied[tile * count:(tile + 1) * count] + (MASS_SHIFT - shift) * here
            for part, half in enumerate(halves(value)):
                inner_ref[step, part, tile, block, :] = half


def sides_kernel(slots, pos_ref, core_ref, chip_ref, field_ref, inner_ref, weights_ref, mixer_ref,
                 blocks_ref, geo_ref, first_ref, basis_ref, moments_ref, v_refs, meta_refs, stencil, buckets):
    tiles, rows = field_ref.shape[1:3]
    width = tiles * TILE
    dof = blocks_ref.shape[1]
    cases = width // dof
    edge = ITERS * HALO
    outer = edge - HALO
    count = edge
    rest = TILE - edge
    shift = basis_shift(blocks_ref[...], slots)
    even = lax.rem(pos_ref[0, 0], jnp.int32(2)) == 0

    for tile in range(tiles + 1):
        lanes = slice(tile * TILE, (tile + 1) * TILE) if tile < tiles else slice(width, None)
        core, chip = core_ref[:, lanes], chip_ref[:, lanes]
        for side, value in enumerate((jnp.where(even, chip, core), jnp.where(even, core, chip))):
            if tile == tiles:
                meta_refs[side] = value
            else:
                for part, half in enumerate(halves(value)):
                    v_refs[0, side, part, tile] = half

    def build(side):
        for first in range(0, outer, HALO):
            start = first + HALO * (1 - side)
            spot = first + HALO if side == 0 else first + rows - edge
            for kind, value in enumerate(
                stencil_rows(meta_refs[side, start:start + HALO, :], slots, spot)
            ):
                stencil[side, kind, first:first + HALO, :] = value

    def window(step, side, part, tile):
        near = v_refs[step, side, part, tile]
        if step == 0:
            if side == 0:
                return jnp.concatenate([near, field_ref[part, tile, :rest, :]], axis=0)
            return jnp.concatenate([field_ref[part, tile, rows - rest:, :], near], axis=0)
        blank = jnp.zeros((HALO * step, TILE), BF16)
        begin = HALO * step
        if side == 0:
            far = inner_ref[step - 1, part, tile, begin:rest, :]
            return jnp.concatenate([blank, near, far], axis=0)
        far = inner_ref[step - 1, part, tile, rows - rest:rows - begin, :]
        return jnp.concatenate([far, near, blank], axis=0)

    def weight_rows(step, side, kind):
        keep = outer - HALO * step
        if side == 0:
            pieces = [weights_ref[0, kind, :count - keep, :]]
            if keep:
                pieces.insert(0, stencil[0, kind, outer - keep:, :])
        else:
            pieces = [weights_ref[1, kind, keep:, :]]
            if keep:
                pieces.append(stencil[1, kind, :keep, :])
        return jnp.concatenate(pieces, axis=0)

    def convert(step):
        begin = HALO * step
        for half in range(2):

            def piece(tile, part):
                lanes = slice(part * META, (part + 1) * META)
                return jnp.concatenate(
                    [
                        v_refs[step, 0, half, tile, count - begin:, lanes],
                        inner_ref[step - 1, half, tile, begin:rows - begin, lanes],
                        v_refs[step, 1, half, tile, :begin, lanes],
                    ],
                    axis=0,
                )

            for number, value in enumerate(swap_blocks(piece)):
                lanes = slice(number % 2 * META, (number % 2 + 1) * META)
                basis_ref[step - 1, half, number // 2, :, lanes] = value

    def tall(step, part):
        if step == 0:
            return jnp.concatenate([geo_ref[part, tile] for tile in range(tiles)], axis=0)
        return jnp.concatenate([basis_ref[step - 1, part, tile] for tile in range(tiles)], axis=0)

    def mixed_gram(high, low):
        return folded_rows(high[:, :TILE] + high[:, TILE:] + low, cases)

    def even_gram(high):
        cross = high[:, TILE:]
        return folded_rows(high[:, :TILE] + cross + cross.T, cases)

    sums = [first_ref[...]]
    for step in range(ITERS):
        centres = []
        for side in range(2):
            if step == 0:
                build(side)
            weights = jnp.concatenate(
                [weight_rows(step, side, kind) for kind in range(TYPES)], axis=0
            )
            for tile in range(tiles):
                row = (side * tiles + tile) * count
                near, fine = (window(step, side, part, tile) for part in range(2))
                first = HALO * (step + 1) if side == 0 else TILE - HALO * (step + 1) - count
                centres.append((near[first:first + count], fine[first:first + count]))
                for part, half in enumerate(gathered(weights, near, fine)):
                    for kind in range(TYPES):
                        buckets[part, kind, row:row + count, :] = (
                            half[kind * count:(kind + 1) * count]
                        )
        applied = mixed(buckets, mixer_ref, 2 * tiles * count)
        for side in range(2):
            for tile in range(tiles):
                number = side * tiles + tile
                near, fine = centres[number]
                here = near.astype(F32) + fine.astype(F32)
                value = applied[number * count:(number + 1) * count] + (MASS_SHIFT - shift) * here
                for part, half in enumerate(halves(value)):
                    v_refs[step + 1, side, part, tile] = half

        convert(step + 1)
        if step == 1:
            others = [tall(k, part) for k in range(3) for part in range(2)]
            high = dot_tn(tall(1, 0), jnp.concatenate(others, axis=1))
            low = dot_tn(tall(1, 1), jnp.concatenate([others[0], others[4]], axis=1))
            sums.append(mixed_gram(high[:, :2 * TILE], low[:, :TILE]))
            sums.append(even_gram(high[:, 2 * TILE:4 * TILE]))
            sums.append(mixed_gram(high[:, 4 * TILE:], low[:, TILE:]))
        elif step == 2:
            others = [tall(k, part) for k in range(2, 4) for part in range(2)]
            high = dot_tn(tall(2, 0), jnp.concatenate(others, axis=1))
            low = dot_tn(tall(2, 1), others[2])
            sums.append(even_gram(high[:, :2 * TILE]))
            sums.append(mixed_gram(high[:, 2 * TILE:], low))

    remainder = jnp.concatenate(sums, axis=0)
    pieces = []
    for _ in range(3):
        pieces.append(remainder.astype(BF16))
        remainder = remainder - pieces[-1].astype(F32)
    collect = one_hot(iota((TILE, META), 0) // 16 == iota((TILE, META), 1) % 16)
    folded = dot(jnp.concatenate(pieces, axis=1), jnp.concatenate([collect] * 3, axis=0))
    group = iota((cases, META), 1) // cases
    moments = jnp.zeros((cases, META), F32)
    for number in range(2 * ITERS):
        part = folded[number * cases:(number + 1) * cases]
        moments = jnp.where(group == number, part, moments)
    moments_ref[...] = moments


def refined_reciprocal(value):
    guess = pl.reciprocal(value, approx=True)
    for _ in range(2):
        guess = guess * (2.0 - value * guess)
    return guess


def finish_kernel(slots, blocks_ref, geo_ref, basis_ref, *refs):
    moment_refs = refs[:-4]
    solution_hbm, residual_hbm, out_refs, sems = refs[-4:]
    rows, width = out_refs.shape[1:]
    dof = blocks_ref.shape[1]
    cases = width // dof
    tiles = width // TILE
    shift = basis_shift(blocks_ref[...], slots)
    moments = moment_refs[0][...]
    for ref in moment_refs[1:]:
        moments = moments + ref[...]
    group = iota((cases, META), 1) // cases
    system = []
    for row in range(ITERS):
        plain = moments if row == 0 else pltpu.roll(moments, META - cases * row, 1)
        ahead = pltpu.roll(moments, META - cases * (row + 1), 1)
        target = pltpu.roll(moments, cases * (ITERS - row), 1)
        system.append(jnp.where(group < ITERS, ahead + shift * plain, target))
    system = jnp.concatenate(system, axis=0)
    size = ITERS * cases
    index = iota((size, 1), 0)
    for pivot in range(0, size, 2):
        column_a = jnp.broadcast_to(system[:, pivot:pivot + 1], (size, META))
        column_b = jnp.broadcast_to(system[:, pivot + 1:pivot + 2], (size, META))
        line_a = system[pivot:pivot + 1, :]
        line_b = system[pivot + 1:pivot + 2, :]
        above = column_b[pivot:pivot + 1, :]
        inverse = refined_reciprocal(column_a[pivot:pivot + 1, :])
        factor = column_a[pivot + 1:pivot + 2, :] * inverse
        corner = column_b[pivot + 1:pivot + 2, :] - factor * above
        line_b = (line_b - factor * line_a) * refined_reciprocal(corner)
        line_a = (line_a - above * line_b) * inverse
        update = system - column_a * line_a - column_b * line_b
        system = jnp.where(index == pivot, line_a, jnp.where(index == pivot + 1, line_b, update))

    unit = jnp.where(iota((cases, META), 1) % cases == iota((cases, META), 0), 1.0, 0.0)
    answers = []
    for row in range(ITERS):
        part = jnp.where(group == ITERS, system[row * cases:(row + 1) * cases], 0.0)
        step = cases
        while step < META:
            part = part + pltpu.roll(part, step, 1)
            step *= 2
        answers.append(part)
    left_over = [unit - shift * answers[0]]
    for row in range(1, ITERS):
        left_over.append(-(answers[row - 1] + shift * answers[row]))
    left_over.append(-answers[ITERS - 1])

    meets = iota((TILE, TILE), 0) % 16 == iota((TILE, TILE), 1) // 16

    def spread(parts):
        highs, lows = [], []
        for part in parts:
            tall = jnp.broadcast_to(part[:, None, :], (cases, TILE // cases, META))
            tall = tall.reshape(TILE, META)
            wide = jnp.concatenate([tall] * (TILE // META), axis=1)
            high, low = halves(jnp.where(meets, wide, 0.0))
            highs.append(high)
            lows.append(low)
        return jnp.concatenate(highs + highs + lows, axis=0)

    def tall(term, part):
        if term == 0:
            return jnp.concatenate([geo_ref[part, tile] for tile in range(tiles)], axis=0)
        return jnp.concatenate([basis_ref[term - 1, part, tile] for tile in range(tiles)], axis=0)

    copies = []
    for number, (out_hbm, parts) in enumerate(
        ((solution_hbm, answers), (residual_hbm, left_over))
    ):
        matrix = spread(parts)
        terms = matrix.shape[0] // (3 * TILE)
        highs = [tall(term, 0) for term in range(terms)]
        lows = [tall(term, 1) for term in range(terms)]
        value = dot(jnp.concatenate(highs + lows + highs, axis=1), matrix)
        for tile in range(tiles):
            lanes = slice(tile * TILE, (tile + 1) * TILE)
            out_refs[number, :, lanes] = value[tile * rows:(tile + 1) * rows]
        copies.append(pltpu.make_async_copy(out_refs.at[number], out_hbm, sems.at[number]))
        copies[number].start()
    for copy in copies:
        copy.wait()


def on_device(loads, row_ids, densities, block_cols, block_types, ref_blocks):
    rows, width = loads.shape
    slots = densities.shape[1]
    cases = width // ref_blocks.shape[1]
    cap = rows // 4
    edge = ITERS * HALO
    tiles = width // TILE
    devices = lax.axis_size("sub")
    position = lax.axis_index("sub").astype(jnp.int32).reshape(1, 1)
    shape = jax.ShapeDtypeStruct
    same_chip = [(i, i ^ 1) for i in range(devices)]
    next_chip = [(i, i + 1) for i in range(1, devices - 1, 2)]
    next_chip += [(i + 1, i) for i in range(1, devices - 1, 2)]
    neighbour = dict(next_chip)
    rounds = [[], []]
    for i in range(devices):
        early = 0 if far_first(i, devices) else 1
        rounds[early].append((i, (i + devices // 2) % devices))
        if i in neighbour:
            rounds[1 - early].append((i, neighbour[i]))

    block = shape((cap * width // META + cap // 2, META), F32)
    to_first, meta, target = pl.pallas_call(
        functools.partial(pack_first_kernel, devices),
        out_shape=(block, shape((META, rows), F32), shape((8, rows), jnp.int32)),
        in_specs=[SMEM] + [HBM] * 5,
        out_specs=(VMEM,) * 3,
        scratch_shapes=[
            pltpu.VMEM((rows, width), F32),
            pltpu.VMEM((1, rows), jnp.int32),
            pltpu.VMEM((slots, rows), F32),
            pltpu.VMEM((slots, rows), jnp.int32),
            pltpu.VMEM((slots, rows), jnp.int32),
            pltpu.SemaphoreType.DMA((5,)),
        ],
        compiler_params=PACK_PARAMS,
        name="pack_first",
    )(position, loads, row_ids.reshape(1, rows), densities.T, block_cols.T, block_types.T)
    from_first = lax.ppermute(to_first, "sub", rounds[0])

    to_core, to_second = pl.pallas_call(
        functools.partial(pack_second_kernel, devices),
        out_shape=(block, block),
        in_specs=[SMEM] + [HBM] * 3,
        out_specs=(VMEM,) * 2,
        scratch_shapes=[
            pltpu.VMEM((8, rows), jnp.int32),
            pltpu.VMEM((META, rows), F32),
            pltpu.VMEM((rows, width), F32),
            pltpu.SemaphoreType.DMA((3,)),
        ],
        compiler_params=PACK_PARAMS,
        name="pack_second",
    )(position, target, meta, loads)
    from_second = lax.ppermute(to_second, "sub", rounds[1])
    from_core = lax.ppermute(to_core, "sub", same_chip)

    mixer_shape = shape((3 * TYPES * TILE, TILE), BF16)
    kept, kept_meta, mixer, first = pl.pallas_call(
        functools.partial(prepare_kernel, slots),
        out_shape=(
            shape((rows, width), F32),
            shape((rows, META), F32),
            mixer_shape,
            shape((cases, TILE), F32),
        ),
        in_specs=[VMEM] * 3,
        out_specs=(VMEM,) * 4,
        compiler_params=PARAMS,
        cost_estimate=pl.CostEstimate(
            flops=4_000_000_000, bytes_accessed=4_000_000, transcendentals=0
        ),
        name="prepare",
    )(loads, meta, ref_blocks)

    border = shape((edge, width + META), F32)
    pair = shape((2, tiles, rows, TILE), BF16)
    geo, field, geo_meta, to_core, to_chip = pl.pallas_call(
        functools.partial(arrange_kernel, slots),
        out_shape=(pair, pair, shape((rows, META), F32), border, border),
        in_specs=[SMEM] + [VMEM] * 5,
        out_specs=(VMEM,) * 5,
        compiler_params=PARAMS,
        name="arrange",
    )(position, kept, kept_meta, from_core, from_first, from_second)

    halo_chip = lax.ppermute(to_chip, "sub", next_chip)
    halo_core = lax.ppermute(to_core, "sub", same_chip)

    basis_shape = shape((ITERS, 2, tiles, rows, TILE), BF16)
    inner, weights = pl.pallas_call(
        functools.partial(interior_kernel, slots),
        out_shape=(basis_shape, shape((2, TYPES, edge, 3 * TILE), BF16)),
        in_specs=[VMEM] * 4,
        out_specs=(VMEM,) * 2,
        scratch_shapes=[
            pltpu.VMEM((TYPES, rows - 2 * HALO, 3 * TILE), BF16),
            pltpu.VMEM((2, TYPES, tiles * (rows - 2 * HALO), TILE), BF16),
        ],
        compiler_params=PARAMS,
        cost_estimate=pl.CostEstimate(
            flops=10_000_000_000, bytes_accessed=8_000_000, transcendentals=0
        ),
        name="interior",
    )(field, geo_meta, mixer, ref_blocks)

    basis, moments = pl.pallas_call(
        functools.partial(sides_kernel, slots),
        out_shape=(basis_shape, shape((cases, META), F32)),
        in_specs=[SMEM] + [VMEM] * 9,
        out_specs=(VMEM,) * 2,
        scratch_shapes=[
            pltpu.VMEM((ITERS + 1, 2, 2, tiles, edge, TILE), BF16),
            pltpu.VMEM((2, edge, META), F32),
            pltpu.VMEM((2, TYPES, edge - HALO, 3 * TILE), BF16),
            pltpu.VMEM((2, TYPES, 2 * tiles * edge, TILE), BF16),
        ],
        compiler_params=PARAMS,
        name="sides",
    )(position, halo_core, halo_chip, field, inner, weights, mixer, ref_blocks, geo, first)

    bits = devices.bit_length() - 1
    gathered_moments = [moments]
    for low, high in ((bits // 2, bits), (0, bits // 2)):
        partial = sum(gathered_moments[1:], gathered_moments[0])
        gathered_moments = [partial]
        for mask in range(1, 1 << (high - low)):
            swap = [(i, i ^ (mask << low)) for i in range(devices)]
            gathered_moments.append(lax.ppermute(partial, "sub", swap))

    return pl.pallas_call(
        functools.partial(finish_kernel, slots),
        out_shape=(shape((rows, width), F32), shape((rows, width), F32)),
        in_specs=[VMEM] * (3 + len(gathered_moments)),
        out_specs=(HBM,) * 2,
        scratch_shapes=[pltpu.VMEM((2, rows, width), F32), pltpu.SemaphoreType.DMA((2,))],
        compiler_params=PARAMS,
        name="finish",
    )(ref_blocks, geo, basis, *gathered_moments)


def solution(mesh):
    placed = (
        P(("groups", "sub"), None),
        P(("groups", "sub")),
        P(("groups", "sub"), None),
        P(("groups", "sub"), None),
        P(("groups", "sub"), None),
        P(),
    )
    return jax.shard_map(
        on_device,
        mesh=mesh,
        in_specs=placed,
        out_specs=(P(("groups", "sub"), None), P(("groups", "sub"), None)),
        check_vma=False,
    )
```
